32 devices in a mesh: tok: 32 (over z, y, x, core).
Axes of the slice: x: 2, y: 2, z: 4, core: 2. Of those that a mesh axis runs over, the one named last changes fastest.
Arguments:
- block_input: bfloat16 [16384, 2048], P('tok'), may hold values from -6 to 6
- lengths: int32 [3], replicated, may hold values from 1 to 15999, as said below
- offsets: int32 [3], replicated, may hold values from 0 to 16383, as said below
- norm1_gain: bfloat16 [2048], P('tok'), may hold values from 0.099609375 to 1.8984375
- w_query: bfloat16 [2048, 256], P('tok'), may hold values from -0.125 to 0.125
- w_key: bfloat16 [2048, 256], P('tok'), may hold values from -0.125 to 0.125
- w_value: bfloat16 [2048, 2048], P('tok'), may hold values from -0.125 to 0.125
- w_out: bfloat16 [2048, 2048], P('tok'), may hold values from -1 to 1
- norm2_gain: bfloat16 [2048], P('tok'), may hold values from 0.099609375 to 1.8984375
- w_gate: bfloat16 [2048, 5504], P('tok'), may hold values from -0.125 to 0.125
- w_up: bfloat16 [2048, 5504], P('tok'), may hold values from -0.125 to 0.125
- w_down: bfloat16 [5504, 2048], P('tok'), may hold values from -0.078125 to 0.078125
- out_grad: bfloat16 [16384, 2048], P('tok'), may hold values from -6 to 6
Outputs:
- output: bfloat16 [16384, 2048], P('tok')
- input_grad: float32 [16384, 2048], P('tok')
- grad_norm1: float32 [2048], P('tok')
- grad_query: float32 [2048, 256], P('tok')
- grad_key: float32 [2048, 256], P('tok')
- grad_value: float32 [2048, 2048], P('tok')
- grad_out: float32 [2048, 2048], P('tok')
- grad_norm2: float32 [2048], P('tok')
- grad_gate: float32 [2048, 5504], P('tok')
- grad_up: float32 [2048, 5504], P('tok')
- grad_down: float32 [5504, 2048], P('tok')
The draws below stay inside these ranges and needn't reach their ends.
Inputs may be any that keep to these rules, and one draw needn't show every extreme that they name: `lengths`: the rows cover the 16384 tokens without gaps or intersection, in the packed order: a row of exactly 384 tokens first, then the longest row, which starts among the first device's tokens and ends among the last device's, then a row of one token. offsets[r] is the first token of the row whose length is lengths[r]; the rows appear in the arrays in any order.
All inputs are finite; a program needn't handle non-finite values.
Results may differ from the reference program's by a relative error of at most 0.014.
Values may be sent and summed in bfloat16 or wider, within the bound.
A program may use at most 1.125 GiB of HBM per device.

```python
import jax
import jax.numpy as jnp
from jax import lax

D = 2048
HEADS = 16
QK = 16
FF = 5504
GROUP = 256
ROWS = 3
TOKENS = 16384
SHORT_MAX = 384
VH = 128


def row_layout(key):
    place_key = jax.random.fold_in(key, 17)
    before = jnp.asarray(SHORT_MAX, jnp.int32)
    after = jnp.asarray(1, jnp.int32)
    longest = (TOKENS - before - after).astype(jnp.int32)
    sizes_in_order = jnp.stack([before, longest, after]).astype(jnp.int32)
    starts_in_order = jnp.stack([jnp.zeros((), jnp.int32), before, before + longest]).astype(jnp.int32)
    slots = jax.random.permutation(place_key, ROWS)
    lengths = jnp.zeros((ROWS,), jnp.int32).at[slots].set(sizes_in_order)
    offsets = jnp.zeros((ROWS,), jnp.int32).at[slots].set(starts_in_order)
    return (lengths, offsets)


def draw_lengths(key, part):
    return row_layout(key)[0]


def draw_offsets(key, part):
    return row_layout(key)[1]


def raised(entries, stream_key, source, target, parts, factor):
    owner, partner = [(jnp.arange(entries.shape[dim]) // (entries.shape[dim] // parts)).reshape([-1 if axis == dim else 1 for axis in range(entries.ndim)]) for dim in (source, target)]
    chosen = jax.random.permutation(stream_key, parts)[partner]
    strong = (owner == chosen) | (owner == (partner + parts // 2) % parts)
    return jnp.where(strong, factor * entries, entries)


def shard_levels(key, shape, cuts, low, high):
    loudness = 1.0
    for axis_at, shards_of in cuts:
        heights = jax.random.uniform(jax.random.fold_in(jax.random.fold_in(key, 6), axis_at), (shards_of,), jnp.float32, low / len(cuts), high / len(cuts))
        loudness = loudness * jnp.repeat(jnp.exp(heights), shape[axis_at] // shards_of).reshape((-1,) + (1,) * (len(shape) - 1 - axis_at))
    return loudness


def gaussian(rng, shape, scale, most, cuts=(), kind=jnp.bfloat16):
    values = scale * jax.random.normal(rng, shape, jnp.float32)
    if cuts:
        values = values * shard_levels(rng, shape, cuts, -0.22, 0.18)
    return jnp.clip(values, -most, most).astype(kind)


def heavy_noise(own_key, shape, scale, limit, pieces, heavy, kind=jnp.bfloat16):
    drawn = scale * jax.random.normal(own_key, shape, jnp.float32)
    if pieces:
        drawn = drawn * shard_levels(own_key, shape, pieces, -0.22, 0.18)
    return jnp.clip(raised(drawn, jax.random.fold_in(own_key, 3), *heavy), -limit, limit).astype(kind)


def setup_inputs(seed: int = 0) -> dict:
    streams_of = jax.random.split(jax.random.key(seed), 14)
    block_input = heavy_noise(streams_of[0], (TOKENS, D), 1.0, 6.0, ((0, 32),), (0, 1, 32, 2.75))
    lengths = draw_lengths(jax.random.fold_in(streams_of[13], 71), 0)
    offsets = draw_offsets(jax.random.fold_in(streams_of[13], 71), 0)
    norm1_gain = jnp.clip(1.0 + 0.18 * jax.random.normal(streams_of[3], (D,), jnp.float32), 0.099609375, 1.8984375).astype(jnp.bfloat16)
    w_query = gaussian(streams_of[4], (D, HEADS * QK), D ** -0.5, 0.125, ((0, 32),))
    w_key = gaussian(streams_of[5], (D, HEADS * QK), D ** -0.5, 0.125, ((0, 32),))
    w_value = gaussian(streams_of[6], (D, D), D ** -0.5, 0.125, ((0, 32),))
    w_out = gaussian(streams_of[7], (D, D), (D // 64) ** -0.5, 1.0, ((0, 32),))
    norm2_gain = jnp.clip(1.0 + 0.18 * jax.random.normal(streams_of[8], (D,), jnp.float32), 0.099609375, 1.8984375).astype(jnp.bfloat16)
    w_gate = gaussian(streams_of[9], (D, FF), D ** -0.5, 0.125, ((0, 32),))
    w_up = gaussian(streams_of[10], (D, FF), D ** -0.5, 0.125, ((0, 32),))
    w_down = gaussian(streams_of[11], (FF, D), FF ** -0.5, 0.078125, ((0, 32),))
    out_grad = gaussian(streams_of[12], (TOKENS, D), 1.0, 6.0, ((0, 32),))
    return dict(block_input=block_input, lengths=lengths, offsets=offsets, norm1_gain=norm1_gain, w_query=w_query, w_key=w_key, w_value=w_value, w_out=w_out, norm2_gain=norm2_gain, w_gate=w_gate, w_up=w_up, w_down=w_down, out_grad=out_grad)


highest = lax.Precision.HIGHEST
eps = 1e-06

@jax.custom_vjp
def low(v):
    return lax.optimization_barrier(v.astype(jnp.bfloat16)).astype(jnp.float32)

@jax.custom_vjp
def low_back(v):
    return v

def low_keep(v):
    return (low(v), None)

def low_pass(kept, grad):
    return (grad,)

def back_keep(v):
    return (v, None)

def back_low(kept, grad):
    return (low(grad),)
low.defvjp(low_keep, low_pass)
low_back.defvjp(back_keep, back_low)

def feature_map(values):
    width = values.shape[-1]
    ones = jnp.ones(values.shape[:-1] + (1,), jnp.float32)
    linear = values * width ** (-0.25)
    square = (values[..., :, None] * values[..., None, :]).reshape(values.shape[:-1] + (width * width,))
    return jnp.concatenate([ones, linear, square * (0.5 ** 0.5 * width ** (-0.5))], axis=-1)

def row_starts(positions, lengths, offsets):
    inside = (positions[:, None] >= offsets[None, :]) & (positions[:, None] < offsets[None, :] + lengths[None, :])
    return lax.optimization_barrier(jnp.sum(jnp.where(inside, offsets[None, :], 0), axis=1)).astype(jnp.int32)

def block(carry, inputs):
    state, total = carry
    queries, keys_in, values, positions, row_start = inputs
    width = queries.shape[-1]
    phi_q = feature_map(queries)
    phi_k = feature_map(keys_in)
    score = jnp.einsum('ihd,jhd->hij', queries, keys_in, precision=highest) * width ** (-0.5)
    weight = 1.0 + score + 0.5 * score * score
    mask = (positions[None, :] <= positions[:, None]) & (positions[None, :] >= row_start[:, None])
    weight = jnp.where(mask[None], weight, 0.0)
    carried = (row_start < positions[0]).astype(jnp.float32)
    numer = jnp.einsum('hij,jhv->ihv', weight, values, precision=highest)
    numer = numer + carried[:, None, None] * jnp.einsum('ihf,hfv->ihv', phi_q, state, precision=highest)
    denom = lax.optimization_barrier(jnp.sum(weight, axis=2)).T + carried[:, None] * jnp.einsum('ihf,hf->ih', phi_q, total, precision=highest)
    last = row_start[-1]
    keep = (positions >= last).astype(jnp.float32)
    fresh = (last >= positions[0]).astype(jnp.float32)
    kept = phi_k * keep[:, None, None]
    state = (1.0 - fresh) * state + jnp.einsum('jhf,jhv->hfv', kept, values, precision=highest)
    total = (1.0 - fresh) * total + lax.optimization_barrier(jnp.sum(kept, axis=0))
    return ((state, total), (numer, denom))

def attention(queries, keys_in, values, positions, row_start):
    tokens, heads, width = queries.shape
    count = tokens // GROUP
    feats = 1 + width + width * width

    def split(array):
        return array.reshape((count, GROUP) + array.shape[1:])
    init = (jnp.zeros((heads, feats, values.shape[-1]), jnp.float32), jnp.zeros((heads, feats), jnp.float32))
    inputs = (split(queries), split(keys_in), split(values), split(positions), split(row_start))
    _, (numer, denom) = lax.scan(jax.checkpoint(block), init, inputs)
    return numer.reshape(values.shape) / denom.reshape(tokens, heads)[..., None]

def product(left, right):
    return jnp.dot(left, right, precision=highest)

def reference(block_input, lengths, offsets, norm1_gain, w_query, w_key, w_value, w_out, norm2_gain, w_gate, w_up, w_down, out_grad):
    positions = jnp.arange(TOKENS, dtype=jnp.int32)
    row_start = row_starts(positions, lengths, offsets)

    def forward(inputs, gain1, query_w, key_w, value_w, out_w, gain2, gate_w, up_w, down_w):
        normed1 = inputs * lax.rsqrt(lax.optimization_barrier(jnp.mean(inputs * inputs, axis=1, keepdims=True)) + eps)
        hidden1 = low(normed1 * gain1)
        queries = low(low_back(product(hidden1, query_w)))
        keys_in = low(low_back(product(hidden1, key_w)))
        values = low(low_back(product(hidden1, value_w)))
        mixed = attention(queries.reshape(TOKENS, HEADS, QK), keys_in.reshape(TOKENS, HEADS, QK), values.reshape(TOKENS, HEADS, VH), positions, row_start)
        mixed = low(mixed.reshape(TOKENS, D))
        middle = inputs + low_back(product(mixed, out_w))
        normed2 = middle * lax.rsqrt(lax.optimization_barrier(jnp.mean(middle * middle, axis=1, keepdims=True)) + eps)
        hidden2 = low(normed2 * gain2)
        gate = low_back(product(hidden2, gate_w))
        upper = low_back(product(hidden2, up_w))
        activation = low(jax.nn.silu(gate) * upper)
        return middle + low_back(product(activation, down_w))
    floats = tuple((array.astype(jnp.float32) for array in (block_input, norm1_gain, w_query, w_key, w_value, w_out, norm2_gain, w_gate, w_up, w_down)))
    result, backward = jax.vjp(forward, *floats)
    grads = backward(out_grad.astype(jnp.float32))
    return (result.astype(jnp.bfloat16), grads[0], grads[1], grads[2], grads[3], grads[4], grads[5], grads[6], grads[7], grads[8], grads[9])
```

```python
import jax
import jax.numpy as jnp
import numpy as np
from jax import lax
from jax.experimental import pallas as pl
from jax.experimental.pallas import tpu as pltpu
from jax.sharding import PartitionSpec as P

QK = 16
FEATS = 160
ROWS = 168
VMEM = 56 * 1024 * 1024
eps = 1e-06
f32 = jnp.float32
bf16 = jnp.bfloat16


def chip_dims(n):
    if n == 32:
        return [(8, 4), (4, 2), (2, 2)]
    if n == 128:
        return [(32, 4), (8, 4), (2, 4)]
    return [(2, n // 2)]


def quad_dims(n):
    if n == 32:
        return [(8, 4), (4, 2)]
    if n == 128:
        return [(32, 4), (8, 4), (4, 2)]
    return [(4, n // 4)]


def flip(x, bits):
    n = lax.axis_size("tok")
    return lax.ppermute(x, "tok", [(i, i ^ bits) for i in range(n)])


def shift(x, dim, k, wrap=True):
    stride, size = dim
    pairs = []
    for i in range(lax.axis_size("tok")):
        at = (i // stride) % size
        if wrap or 0 <= at + k < size:
            pairs.append((i, i + ((at + k) % size - at) * stride))
    return lax.ppermute(x, "tok", pairs)


def place(dim):
    return (lax.axis_index("tok") // dim[0]) % dim[1]


def pick(x, index, axis=0):
    return lax.dynamic_index_in_dim(x, index, axis, False)


def assemble(pieces):
    out = jnp.zeros((len(pieces),) + pieces[0][1].shape, pieces[0][1].dtype)
    for index, block in pieces:
        out = lax.dynamic_update_index_in_dim(out, block, index, 0)
    return out


def gather_stage(x, dim):
    at = place(dim)
    pieces = [(at, x)]
    for k in range(1, dim[1]):
        pieces.append((lax.rem(at + dim[1] - k, dim[1]), shift(x, dim, k)))
    return assemble(pieces)


def gather(x, dims):
    order = sorted(dims, key=lambda d: -d[0])
    done = []
    for dim in dims:
        x = gather_stage(x, dim)
        done.insert(0, dim)
    axes = [done.index(d) for d in order]
    rest = list(range(len(done), x.ndim))
    x = x.transpose(axes + rest)
    return x.reshape((-1,) + x.shape[len(done):])


def gather_blocks(x, dims):
    unit = min(d[0] for d in dims)
    blocks = [(jnp.int32(0), x)]
    for dim in dims:
        at, later = place(dim), []
        for k in range(dim[1]):
            step = lax.rem(at + dim[1] - k, dim[1]) * (dim[0] // unit)
            later += [(i + step, shift(b, dim, k) if k else b) for i, b in blocks]
        blocks = later
    return assemble(blocks)


def total(x, dims):
    for dim in dims:
        x = x + sum(shift(x, dim, k) for k in range(1, dim[1]))
    return x


def scatter(make, dims, grid):
    dim = dims[-1]
    at = place(dim)
    acc = None
    sent = []
    for k in range(1, dim[1]):
        sent.append(shift(make(lax.rem(at + k, dim[1])).astype(bf16), dim, k))
    acc = make(at).astype(f32) + sum(s.astype(f32) for s in sent)
    for dim in reversed(dims[:-1]):
        at = place(dim)
        low = acc.astype(bf16).reshape((-1, dim[1]) + acc.shape[1:])
        acc = acc.reshape((-1, dim[1]) + acc.shape[1:])
        own = pick(acc, at, 1)
        for k in range(1, dim[1]):
            own = own + shift(pick(low, lax.rem(at + k, dim[1]), 1), dim, k).astype(f32)
        acc = own
    return acc[0]


def feature_tables(heads):
    pairs = [(a, b) for a in range(QK + 1) for b in range(a, QK + 1)]
    one = np.zeros((heads, heads * QK, FEATS), np.float32)
    two = np.zeros((heads, heads * QK, FEATS), np.float32)
    rows = np.zeros((8, FEATS), np.float32)
    for f, (a, b) in enumerate(pairs):
        for h in range(heads):
            if a < QK:
                one[h, h * QK + a, f] = 1
            if b < QK:
                two[h, h * QK + b, f] = 1
        rows[0, f] = a == QK
        rows[1, f] = b == QK
        if a == QK:
            rows[2, f] = 1.0
        elif b == QK:
            rows[2, f] = QK**-0.5
        else:
            rows[2, f] = (0.5 if a == b else 1.0) / QK
    return jnp.asarray(one, bf16), jnp.asarray(two, bf16), jnp.asarray(rows)


def dot(a, b):
    return lax.dot_general(a, b, (((1,), (0,)), ((), ())), preferred_element_type=f32)


def dot_rows(a, b):
    return lax.dot_general(a, b, (((0,), (0,)), ((), ())), preferred_element_type=f32)


def dot_cols(a, b):
    return lax.dot_general(a, b, (((1,), (1,)), ((), ())), preferred_element_type=f32)


def halves(x):
    high = x.astype(bf16)
    return high, (x - high.astype(f32)).astype(bf16)


def features(x, one, two, rows):
    return dot(x, one) + rows[0:1], dot(x, two) + rows[1:2]


def total_row(state):
    return jnp.concatenate([state[FEATS : FEATS + 1], state[FEATS + 1 : FEATS + 2, : FEATS - 128]], axis=1)


def store_state(ref, state, row):
    ref[0, 0, :FEATS, :] = state
    ref[0, 0, FEATS:, :] = jnp.zeros((ROWS - FEATS, state.shape[1]), f32)
    ref[0, 0, FEATS : FEATS + 1, :] = row[:, :128]
    ref[0, 0, FEATS + 1 : FEATS + 2, : FEATS - 128] = row[:, 128:]


def kept_rows(scal, tile, tokens):
    index = lax.broadcasted_iota(jnp.int32, (tokens, 1), 0) + tile * tokens
    return index >= scal[tile]


def state_body(scal, k_ref, v_ref, one, two, rows, out_ref):
    tile = pl.program_id(0)
    a, b = features(k_ref[...], one[0], two[0], rows)
    phi = jnp.where(kept_rows(scal, tile, a.shape[0]), a * b, 0.0)
    high, low = halves(phi)
    v = v_ref[...]
    store_state(out_ref, dot_rows(high, v) + dot_rows(low, v), jnp.sum(phi, axis=0, keepdims=True))


def weights(q_ref, k_ref, lo_ref, tile, head):
    tokens, lanes = q_ref.shape
    lane = lax.broadcasted_iota(jnp.int32, (tokens, lanes), 1) // QK == head
    q = jnp.where(lane, q_ref[...], jnp.zeros((), bf16))
    score = dot_cols(q, k_ref[...]) * QK**-0.5
    row = lax.broadcasted_iota(jnp.int32, score.shape, 0)
    col = lax.broadcasted_iota(jnp.int32, score.shape, 1)
    lo = lo_ref[...] - tile * tokens
    mask = (col <= row) & (col >= lo)
    weight = jnp.where(mask, 1.0 + score + 0.5 * score * score, 0.0)
    return lane, score, mask, weight, lo < 0


def forward_body(q_ref, k_ref, v_ref, lo_ref, carry_ref, one, two, rows, y_ref, mixed_ref):
    tile, head = pl.program_id(0), pl.program_id(1)
    _, _, _, weight, alive = weights(q_ref, k_ref, lo_ref, tile, head)
    a, b = features(q_ref[...], one[0], two[0], rows)
    phi = jnp.where(alive, a * b * rows[2:3], 0.0)
    high, low = halves(phi)
    carry = carry_ref[0, 0]
    s_high, s_low = halves(carry[:FEATS])
    numer = dot(weight.astype(bf16), v_ref[...])
    numer = numer + (dot(high, s_high) + dot(high, s_low) + dot(low, s_high))
    denom = jnp.sum(weight, axis=1, keepdims=True) + jnp.sum(phi * total_row(carry), axis=1, keepdims=True)
    y = numer / denom
    y_ref[...] = y
    mixed_ref[...] = y.astype(bf16)


def spread(t, a, b, one, two):
    first_high, first_low = halves(t * b)
    second_high, second_low = halves(t * a)
    return (
        dot_cols(first_high, one) + dot_cols(first_low, one) + dot_cols(second_high, two) + dot_cols(second_low, two)
    )


def backward_body(
    q_ref, k_ref, v_ref, lo_ref, carry_ref, one, two, rows, y_ref, d_ref, dq_ref, dk_ref, dv_ref, ds_ref, dq_acc, dk_acc
):
    tile, head = pl.program_id(0), pl.program_id(1)
    lane, score, mask, weight, alive = weights(q_ref, k_ref, lo_ref, tile, head)
    a, b = features(q_ref[...], one[0], two[0], rows)
    phi = jnp.where(alive, a * b * rows[2:3], 0.0)
    high, low = halves(phi)
    carry = carry_ref[0, 0]
    s_high, s_low = halves(carry[:FEATS])
    row = total_row(carry)
    denom = jnp.sum(weight, axis=1, keepdims=True) + jnp.sum(phi * row, axis=1, keepdims=True)
    d = d_ref[...].astype(f32)
    g = d / denom
    c = -jnp.sum(d * y_ref[...], axis=1, keepdims=True) / denom
    g_high, g_low = halves(g)
    v = v_ref[...]
    dk = dot_cols(g_high, v) + dot_cols(g_low, v) + c
    ds = jnp.where(mask, dk * (1.0 + score) * QK**-0.5, 0.0).astype(bf16)
    dv_ref[...] = dot_rows(weight.astype(bf16), g_high)
    dphi = dot_cols(g_high, s_high) + dot_cols(g_high, s_low) + dot_cols(g_low, s_high) + c * row
    t = jnp.where(alive, dphi * rows[2:3], 0.0)
    dq = jnp.where(lane, dot(ds, k_ref[...]), 0.0) + spread(t, a, b, one[0], two[0])
    dkeys = jnp.where(lane, dot_rows(ds, q_ref[...]), 0.0)

    @pl.when(head == 0)
    def _():
        dq_acc[...] = dq
        dk_acc[...] = dkeys

    @pl.when(head > 0)
    def _():
        dq_acc[...] += dq
        dk_acc[...] += dkeys

    @pl.when(head == pl.num_programs(1) - 1)
    def _():
        dq_ref[...] = dq_acc[...].astype(bf16)
        dk_ref[...] = dk_acc[...]

    state = dot_rows(high, g_high) + dot_rows(high, g_low) + dot_rows(low, g_high)
    store_state(ds_ref, state, jnp.sum(phi * c, axis=0, keepdims=True))


def carried_body(scal, k_ref, v_ref, one, two, rows, grad_ref, dk_in, dv_in, dk_ref, dv_ref, acc):
    tile, head = pl.program_id(0), pl.program_id(1)
    a, b = features(k_ref[...], one[0], two[0], rows)
    keep = kept_rows(scal, tile, a.shape[0])
    high, low = halves(jnp.where(keep, a * b, 0.0))
    grad = grad_ref[0, 0]
    g_high, g_low = halves(grad[:FEATS])
    v = v_ref[...]
    dv = dv_in[...] + dot(high, g_high) + dot(high, g_low) + dot(low, g_high)
    dv_ref[...] = dv.astype(bf16)
    t = jnp.where(keep, dot_cols(v, g_high) + dot_cols(v, g_low) + total_row(grad), 0.0)
    dk = spread(t, a, b, one[0], two[0])

    @pl.when(head == 0)
    def _():
        acc[...] = dk_in[...] + dk

    @pl.when(head > 0)
    def _():
        acc[...] += dk

    @pl.when(head == pl.num_programs(1) - 1)
    def _():
        dk_ref[...] = acc[...].astype(bf16)


class Attention:
    def __init__(self, qkv, lo, heads, tokens):
        self.qkv, self.heads, self.tokens = qkv, heads, tokens
        self.lo = lo[:, None]
        self.scal = jnp.stack([lo[tokens - 1], lo[2 * tokens - 1]])
        self.tables = feature_tables(heads)
        lanes = heads * QK
        self.value = (qkv.shape[1] - 2 * lanes) // heads
        skip = 2 * lanes // self.value
        self.q = pl.BlockSpec((tokens, lanes), lambda t, h: (t, 0))
        self.k = pl.BlockSpec((tokens, lanes), lambda t, h: (t, 1))
        self.v = pl.BlockSpec((tokens, self.value), lambda t, h: (t, h + skip))
        self.o = pl.BlockSpec((tokens, self.value), lambda t, h: (t, h))
        self.l = pl.BlockSpec((tokens, 1), lambda t, h: (t, 0))
        self.s = pl.BlockSpec((1, 1, ROWS, self.value), lambda t, h: (h, t, 0, 0))
        self.e = pl.BlockSpec((1, lanes, FEATS), lambda t, h: (h, 0, 0))
        self.r = pl.BlockSpec((8, FEATS), lambda t, h: (0, 0))
        self.m = pl.BlockSpec(memory_space=pltpu.SMEM)
        self.table_specs = [self.e, self.e, self.r]
        self.acc = pltpu.VMEM((tokens, lanes), f32)
        self.state_shape = jax.ShapeDtypeStruct((heads, 2, ROWS, self.value), f32)

    def wide(self, kind):
        return jax.ShapeDtypeStruct((2 * self.tokens, self.heads * self.value), kind)

    def narrow(self, kind):
        return jax.ShapeDtypeStruct((2 * self.tokens, self.heads * QK), kind)

    def call(self, body, ins, outs, shapes, scratch, flops, args):
        size = sum(int(np.prod(a.shape)) * a.dtype.itemsize for a in list(args) + list(shapes))
        return pl.pallas_call(
            body,
            grid=(2, self.heads),
            in_specs=ins,
            out_specs=outs,
            out_shape=shapes,
            scratch_shapes=scratch,
            compiler_params=pltpu.CompilerParams(vmem_limit_bytes=VMEM),
            cost_estimate=pl.CostEstimate(flops=flops, bytes_accessed=size, transcendentals=0),
        )(*args)

    def states(self):
        (out,) = self.call(
            state_body,
            [self.m, self.k, self.v] + self.table_specs,
            [self.s],
            [self.state_shape],
            [],
            3 * 10**9,
            (self.scal, self.qkv, self.qkv, *self.tables),
        )
        return out

    def forward(self, carry):
        return self.call(
            forward_body,
            [self.q, self.k, self.v, self.l, self.s] + self.table_specs,
            [self.o, self.o],
            [self.wide(f32), self.wide(bf16)],
            [],
            10 * 10**9,
            (self.qkv, self.qkv, self.qkv, self.lo, carry, *self.tables),
        )

    def backward(self, carry, y, d_heads):
        return self.call(
            backward_body,
            [self.q, self.k, self.v, self.l, self.s] + self.table_specs + [self.o, self.o],
            [self.q, self.q, self.o, self.s],
            [self.narrow(bf16), self.narrow(f32), self.wide(f32), self.state_shape],
            [self.acc, self.acc],
            30 * 10**9,
            (self.qkv, self.qkv, self.qkv, self.lo, carry, *self.tables, y, d_heads),
        )

    def carried(self, grad, dk, dv):
        return self.call(
            carried_body,
            [self.m, self.k, self.v] + self.table_specs + [self.s, self.q, self.o],
            [self.q, self.o],
            [self.narrow(bf16), self.wide(bf16)],
            [self.acc],
            10 * 10**9,
            (self.scal, self.qkv, self.qkv, *self.tables, grad, dk, dv),
        )


def others(state, earlier, kind):
    n = lax.axis_size("tok")
    me = lax.axis_index("tok")
    sign = 1 if earlier else -1
    if n != 32:
        parts = lax.all_gather(state.astype(kind), "tok").astype(f32)
        index = jnp.arange(n)
        before = (sign * (me // 2 - index // 2) > 0) & (index % 2 == me % 2)
        return jnp.sum(jnp.where(before.reshape((n,) + (1,) * state.ndim), parts, 0.0), axis=0)
    plane = (me // 2) % 4
    slices = state.astype(kind).reshape((4, state.shape[0] // 4) + state.shape[1:])
    mine = [pick(slices, plane)]
    for k in range(1, 4):
        mine.append(flip(pick(slices, plane ^ k), 2 * k))
    mine = [part.astype(f32) for part in mine]
    whole = sum(mine).astype(kind)
    beyond = sum(shift(whole, (8, 4), sign * k, False).astype(f32) for k in range(1, 4))
    pieces = []
    for k in range(4):
        before = beyond
        for j in range(4):
            if j != k:
                before = before + jnp.where(sign * ((plane ^ k) - (plane ^ j)) > 0, mine[j], 0.0)
        before = before.astype(kind)
        pieces.append((plane ^ k, flip(before, 2 * k) if k else before))
    return assemble(pieces).reshape(state.shape).astype(f32)


def row_starts(positions, lengths, offsets):
    inside = (positions[:, None] >= offsets[None, :]) & (positions[:, None] < offsets[None, :] + lengths[None, :])
    return jnp.sum(jnp.where(inside, offsets[None, :], 0), axis=1)


def ordered(first, mine, theirs, axis=0):
    return jnp.concatenate([jnp.where(first, mine, theirs), jnp.where(first, theirs, mine)], axis=axis)


def shards(
    block_input,
    lengths,
    offsets,
    norm1_gain,
    w_query,
    w_key,
    w_value,
    w_out,
    norm2_gain,
    w_gate,
    w_up,
    w_down,
    out_grad,
):
    n = lax.axis_size("tok")
    me = lax.axis_index("tok")
    core, quad = me % 2, me % 4
    even = core == 0
    cdims, qdims = chip_dims(n), quad_dims(n)
    chips, quads = n // 2, n // 4
    tokens, width = block_input.shape
    rows = w_query.shape[0]
    heads = w_query.shape[1] // QK // 2
    half = width // 2
    lanes = heads * QK
    z_first = cdims
    x_last = [cdims[0]] + cdims[1:][::-1]

    def column_half(w, which):
        return lax.dynamic_slice_in_dim(w, which * (w.shape[1] // 2), w.shape[1] // 2, 1)

    def row_half(w, which):
        return lax.dynamic_slice_in_dim(w, which * (w.shape[0] // 2), w.shape[0] // 2, 0)

    gains = jnp.stack([norm1_gain, norm2_gain]).astype(f32)
    gains = gather(gather(gains, [(1, 2)]), cdims).reshape(n, 2, rows).transpose(1, 0, 2).reshape(2, 1, width)
    gain_one, gain_two = gains[0], gains[1]

    def by_core(which):
        return jnp.concatenate([column_half(w, which) for w in (w_query, w_key, w_value)], axis=1)

    chip_qkv = ordered(even, by_core(core), flip(by_core(1 - core), 1))
    cut = chip_qkv.shape[1] // 2
    qkv_all = jnp.concatenate(
        [gather(chip_qkv[:, :cut], z_first), gather(chip_qkv[:, cut:], x_last)], axis=2
    ).reshape(width, 2 * cut)

    inputs32 = block_input.astype(f32)
    ratio_one = lax.rsqrt(jnp.mean(inputs32 * inputs32, axis=1, keepdims=True) + eps)
    normed_one = inputs32 * ratio_one
    hidden_one = (normed_one * gain_one).astype(bf16)
    hidden_chip = ordered(even, hidden_one, flip(hidden_one, 1))
    qkv = dot(hidden_chip, qkv_all).astype(bf16)

    first = (me // 2) * 2 * tokens
    positions = first + jnp.arange(2 * tokens, dtype=jnp.int32)
    lo = row_starts(positions, lengths, offsets) - first
    attention = Attention(qkv, lo, heads, tokens)
    states = attention.states()
    fresh0 = (lo[tokens - 1] >= 0).astype(f32)
    fresh1 = (lo[2 * tokens - 1] >= tokens).astype(f32)
    entering = others(states[:, 1] + (1.0 - fresh1) * states[:, 0], True, f32)
    carry = jnp.stack([entering, states[:, 0] + (1.0 - fresh0) * entering], axis=1)
    y_heads, mixed_heads = attention.forward(carry)
    mixed = ordered(even, row_half(mixed_heads, core), flip(row_half(mixed_heads, 1 - core), 1), 1)

    chip_out = ordered(even, column_half(w_out, core), flip(column_half(w_out, 1 - core), 1))
    out_half = gather(chip_out, z_first).reshape(width, half)
    out_all = ordered(even, out_half, flip(out_half, 1), 1)
    middle = inputs32 + dot(mixed, out_all)
    ratio_two = lax.rsqrt(jnp.mean(middle * middle, axis=1, keepdims=True) + eps)
    normed_two = middle * ratio_two
    hidden_two = (normed_two * gain_two).astype(bf16)

    unit = w_down.shape[0]
    padded = -(-unit // 16) * 16
    cols = quads * padded

    def by_quad(w):
        w = w.reshape(rows, quads, 4, unit)
        w = jnp.pad(w, ((0, 0), (0, 0), (0, 0), (0, padded - unit)))
        return w.transpose(2, 0, 1, 3).reshape(4, rows, cols)

    gate_up = jnp.concatenate([by_quad(w_gate), by_quad(w_up)], axis=2)
    pieces = [(quad, pick(gate_up, quad))]
    for k in range(1, 4):
        pieces.append((quad ^ k, flip(pick(gate_up, quad ^ k), k)))
    gate_up = assemble(pieces).reshape(4 * rows, 2 * cols)
    gate_up = gather_blocks(gate_up, qdims).reshape(width, 2 * cols)
    down = jnp.pad(w_down, ((0, padded - unit), (0, 0)))
    down = gather_blocks(down, qdims).reshape(cols, width)

    def to_quad(x):
        near = jnp.concatenate([x, flip(x, 1)])
        far = flip(x, 2)
        return near, jnp.concatenate([far, flip(far, 1)])

    def from_quad(near, far):
        far_sum = far[:tokens] + flip(far[tokens:].astype(bf16), 1).astype(f32)
        near_sum = near[:tokens] + flip(near[tokens:].astype(bf16), 1).astype(f32)
        return near_sum + flip(far_sum.astype(bf16), 2).astype(f32)

    hidden_quad = to_quad(hidden_two)
    grad_quad = to_quad(out_grad)

    def ffn(hidden, grad):
        gate = dot(hidden, gate_up[:, :cols])
        upper = dot(hidden, gate_up[:, cols:])
        sigma = jax.nn.sigmoid(gate)
        smooth = gate * sigma
        activation = (smooth * upper).astype(bf16)
        out = dot(activation, down)
        d_act = dot_cols(grad, down)
        d_gate = (d_act * upper * sigma * (1.0 + gate * (1.0 - sigma))).astype(bf16)
        d_up = (d_act * smooth).astype(bf16)
        d_hidden = dot_cols(d_gate, gate_up[:, :cols]) + dot_cols(d_up, gate_up[:, cols:])
        return out, activation, d_gate, d_up, d_hidden

    near, far = ffn(hidden_quad[0], grad_quad[0]), ffn(hidden_quad[1], grad_quad[1])
    output = (middle + from_quad(near[0], far[0])).astype(bf16)
    d_hidden_two = from_quad(near[4], far[4])
    activation, d_gate, d_up = (jnp.concatenate([near[i], far[i]]) for i in (1, 2, 3))
    hidden_quad = jnp.concatenate(hidden_quad)
    grad_quad = jnp.concatenate(grad_quad)

    last = qdims[-1][1]

    def hidden_part(index):
        return pick(hidden_quad.reshape(4 * tokens, quads // last, last, width // quads), index, 2).reshape(
            4 * tokens, width // last
        )

    def scatter_gate(d):
        total = scatter(
            lambda index: dot_rows(hidden_part(index), d).reshape(quads // last, width // quads, cols), qdims, None
        )
        total = total.reshape(4, rows, cols)
        low = total.astype(bf16)
        parts = [(quad, pick(total, quad))]
        for k in range(1, 4):
            parts.append((quad ^ k, flip(pick(low, quad ^ k), k).astype(f32)))
        return assemble(parts).reshape(4, rows, quads, padded)[..., :unit].transpose(1, 2, 0, 3).reshape(rows, -1)

    term_down = dot_rows(activation, grad_quad).reshape(quads // last, last, padded, width)
    grad_down = scatter(lambda index: pick(term_down, index, 1), qdims, None)[:unit]
    grad_gate = scatter_gate(d_gate)
    grad_up = scatter_gate(d_up)

    term_norm_two = jnp.sum(d_hidden_two * normed_two, axis=0)
    scaled_two = d_hidden_two * gain_two
    d_middle = out_grad.astype(f32) + ratio_two * (
        scaled_two - normed_two * jnp.mean(scaled_two * normed_two, axis=1, keepdims=True)
    )
    d_mixed = d_middle.astype(bf16)
    d_mixed_chip = ordered(even, d_mixed, flip(d_mixed, 1))

    d_heads = dot_cols(d_mixed_chip, row_half(out_all, core)).astype(bf16)
    dq, dk, dv, d_states = attention.backward(carry, y_heads, d_heads)
    leaving = others(d_states[:, 0] + (1.0 - fresh0) * d_states[:, 1], False, bf16)
    d_states = jnp.stack([d_states[:, 1] + (1.0 - fresh1) * leaving, leaving], axis=1)
    dk, dv = attention.carried(d_states, dk, dv)
    d_qkv = jnp.concatenate([dq, dk, dv], axis=1)

    d_rows = row_half(d_qkv, 1 - core)
    theirs = flip(dot_cols(d_rows, qkv_all).astype(bf16), 1)
    d_hidden_one = dot_cols(row_half(d_qkv, core), qkv_all) + theirs.astype(f32)
    term_norm_one = jnp.sum(d_hidden_one * normed_one, axis=0)
    scaled_one = d_hidden_one * gain_one
    input_grad = d_middle + ratio_one * (
        scaled_one - normed_one * jnp.mean(scaled_one * normed_one, axis=1, keepdims=True)
    )

    last_chip = cdims[-1][1]

    def chip_part(x, index):
        return pick(x.reshape(2 * tokens, chips // last_chip, last_chip, 2 * rows), index, 2).reshape(
            2 * tokens, width // last_chip
        )

    def scatter_rows(x, d):
        total = scatter(
            lambda index: dot_rows(chip_part(x, index), d).reshape(chips // last_chip, 2 * rows, d.shape[1]),
            cdims,
            None,
        )
        return row_half(total, core), flip(row_half(total, 1 - core), 1)

    mine, theirs = scatter_rows(hidden_chip, d_qkv)
    spans = [(0, lanes), (lanes, 2 * lanes), (2 * lanes, 2 * lanes + half)]
    grad_query, grad_key, grad_value = (ordered(even, mine[:, a:b], theirs[:, a:b], 1) for a, b in spans)
    mixed_chip = jnp.concatenate(
        [
            ordered(even, mixed_heads[:tokens], flip(mixed_heads[:tokens], 1), 1),
            ordered(even, mixed_heads[tokens:], flip(mixed_heads[tokens:], 1), 1),
        ]
    )
    grad_out = ordered(even, *scatter_rows(mixed_chip, column_half(d_mixed_chip, core)), 1)

    def norm_shard(term):
        term = total(term.reshape(1, width), [(1, 2)] + cdims).reshape(n, rows)
        return pick(term, me)

    return (
        output,
        input_grad,
        norm_shard(term_norm_one),
        grad_query,
        grad_key,
        grad_value,
        grad_out,
        norm_shard(term_norm_two),
        grad_gate,
        grad_up,
        grad_down,
    )


def solution(mesh):
    return jax.shard_map(
        shards,
        mesh=mesh,
        in_specs=(
            P("tok", None),
            P(),
            P(),
            P("tok"),
            P("tok", None),
            P("tok", None),
            P("tok", None),
            P("tok", None),
            P("tok"),
            P("tok", None),
            P("tok", None),
            P("tok", None),
            P("tok", None),
        ),
        out_specs=(
            P("tok", None),
            P("tok", None),
            P("tok"),
            P("tok", None),
            P("tok", None),
            P("tok", None),
            P("tok", None),
            P("tok"),
            P("tok", None),
            P("tok", None),
            P("tok", None),
        ),
        check_vma=False,
    )
```

```python
import jax
import jax.numpy as jnp
import numpy as np
from jax import lax
from jax.experimental import pallas as pl
from jax.experimental.pallas import tpu as pltpu
from jax.sharding import PartitionSpec as P

QK = 16
FEATS = 160
ROWS = 168
VMEM = 56 * 1024 * 1024
eps = 1e-06
f32 = jnp.float32
bf16 = jnp.bfloat16


def chip_dims(n):
    if n == 32:
        return [(8, 4), (4, 2), (2, 2)]
    if n == 128:
        return [(32, 4), (8, 4), (2, 4)]
    return [(2, n // 2)]


def quad_dims(n):
    if n == 32:
        return [(8, 4), (4, 2)]
    if n == 128:
        return [(32, 4), (8, 4), (4, 2)]
    return [(4, n // 4)]


def flip(x, bits):
    n = lax.axis_size("tok")
    return lax.ppermute(x, "tok", [(i, i ^ bits) for i in range(n)])


def shift(x, dim, k, wrap=True):
    stride, size = dim
    pairs = []
    for i in range(lax.axis_size("tok")):
        at = (i // stride) % size
        if wrap or 0 <= at + k < size:
            pairs.append((i, i + ((at + k) % size - at) * stride))
    return lax.ppermute(x, "tok", pairs)


def place(dim):
    return (lax.axis_index("tok") // dim[0]) % dim[1]


def pick(x, index, axis=0):
    return lax.dynamic_index_in_dim(x, index, axis, False)


def assemble(pieces):
    out = jnp.zeros((len(pieces),) + pieces[0][1].shape, pieces[0][1].dtype)
    for index, block in pieces:
        out = lax.dynamic_update_index_in_dim(out, block, index, 0)
    return out


def after(x, *others):
    return lax.optimization_barrier((x,) + others)[0]


def gather_stage(x, dim):
    at = place(dim)
    pieces = [(at, x)]
    for k in range(1, dim[1]):
        pieces.append((lax.rem(at + dim[1] - k, dim[1]), shift(x, dim, k)))
    return assemble(pieces)


def in_order(x, done):
    axes = [done.index(d) for d in sorted(done, key=lambda d: -d[0])]
    x = x.transpose(axes + list(range(len(done), x.ndim)))
    return x.reshape((-1,) + x.shape[len(done) :])


def gather(x, dims):
    for dim in dims:
        x = gather_stage(x, dim)
    return in_order(x, dims[::-1])


def shift_order(size):
    return [1, 3, 2] if size == 4 else list(range(1, size))


def total(x, dims):
    for dim in dims:
        x = x + sum(shift(x, dim, k) for k in range(1, dim[1]))
    return x


class Scatter:
    def __init__(self, make, dims):
        self.make, self.dims, self.dim = make, dims, dims[-1]
        self.at = place(self.dim)

    def send(self):
        sent = [(k, self.make(lax.rem(self.at + k, self.dim[1]))) for k in range(1, self.dim[1])]
        self.here = [shift(s, self.dim, k) for k, s in sent]
        return sent[0][1]

    def keep(self, *gate):
        self.kept = self.make(after(self.at, *gate) if gate else self.at)
        return self.kept

    def finish(self, *gates):
        gates = list(gates) + [()] * len(self.dims)
        acc = self.kept.astype(f32) + sum((after(h, *gates[0]) if gates[0] else h).astype(f32) for h in self.here)
        for dim, gate in zip(reversed(self.dims[:-1]), gates[1:]):
            at = place(dim)
            acc = acc.reshape((-1, dim[1]) + acc.shape[1:])
            low = acc.astype(bf16)
            own = pick(acc, at, 1)
            for k in range(1, dim[1]):
                part = shift(pick(low, lax.rem(at + k, dim[1]), 1), dim, k)
                own = own + (after(part, *gate) if gate else part).astype(f32)
            acc = own
        return acc[0]


def spans_of(cols, most=512):
    return [(s, min(most, cols - s)) for s in range(0, cols, most)]


def ffn_body(count, index, x_ref, g_ref, *refs):
    gate_up, down = refs[0], refs[1 : count + 1]
    y_ref, act_ref, d_ref, dh_ref, w_gate_up, w_down, sem = refs[count + 1 :]
    cols = w_down.shape[0]

    @pl.when(pl.program_id(0) == 0)
    def _():
        copies = [pltpu.make_async_copy(gate_up, w_gate_up, sem.at[count])]
        size = down[0].shape[0]
        for i, block in enumerate(down):
            at = pl.ds(pl.multiple_of(index[i] * size, 16), size)
            copies.append(pltpu.make_async_copy(block, w_down.at[at], sem.at[i]))
        for copy in copies:
            copy.start()
        for copy in copies:
            copy.wait()

    x, g = x_ref[...], g_ref[...]
    for s, w in spans_of(cols):
        gate, upper = dot(x, w_gate_up[:, s : s + w]), dot(x, w_gate_up[:, cols + s : cols + s + w])
        d_act = dot_cols(g, w_down[s : s + w, :])
        sigma = jax.nn.sigmoid(gate)
        smooth = gate * sigma
        act_ref[:, s : s + w] = (smooth * upper).astype(bf16)
        d_ref[:, s : s + w] = (d_act * upper * sigma * (1.0 + gate * (1.0 - sigma))).astype(bf16)
        d_ref[:, cols + s : cols + s + w] = (d_act * smooth).astype(bf16)
    y_ref[...] = dot(act_ref[...], w_down[...]).astype(bf16)
    dh_ref[...] = dot_cols(d_ref[...], w_gate_up[...]).astype(bf16)


def ffn(x, g, gate_up, down, tile=256):
    index = jnp.stack([i for i, _ in down]).astype(jnp.int32)
    down = [b for _, b in down]
    tokens, width = x.shape
    count = len(down)
    cols = count * down[0].shape[0]

    def block(w):
        return pl.BlockSpec((tile, w), lambda i, _: (i, 0))

    return pl.pallas_call(
        lambda *refs: ffn_body(count, *refs),
        out_shape=[jax.ShapeDtypeStruct((tokens, w), bf16) for w in (width, cols, 2 * cols, width)],
        grid_spec=pltpu.PrefetchScalarGridSpec(
            num_scalar_prefetch=1,
            grid=(tokens // tile,),
            in_specs=[block(width), block(width)] + [pl.BlockSpec(memory_space=pl.ANY)] * (count + 1),
            out_specs=[block(width), block(cols), block(2 * cols), block(width)],
            scratch_shapes=[
                pltpu.VMEM((width, 2 * cols), bf16),
                pltpu.VMEM((cols, width), bf16),
                pltpu.SemaphoreType.DMA((count + 1,)),
            ],
        ),
        compiler_params=pltpu.CompilerParams(vmem_limit_bytes=VMEM),
        cost_estimate=pl.CostEstimate(flops=0, bytes_accessed=0, transcendentals=0),
    )(index, x, g, gate_up, *down)


def product_body(count, index, *refs):
    left, right, out = refs[:count], refs[count : 2 * count], refs[2 * count]
    out[...] = sum(dot_rows(a[...], b[...]) for a, b in zip(left, right)).astype(out.dtype)


def row_blocks(left, right, index, size):
    count = index.shape[0]
    cols = right[0].shape[1]
    tokens = sum(a.shape[0] for a in left)
    return pl.pallas_call(
        lambda *refs: product_body(len(left), *refs),
        out_shape=jax.ShapeDtypeStruct((count * size, cols), bf16),
        grid_spec=pltpu.PrefetchScalarGridSpec(
            num_scalar_prefetch=1,
            grid=(count,),
            in_specs=[pl.BlockSpec((a.shape[0], size), lambda i, at: (0, at[i])) for a in left]
            + [pl.BlockSpec((b.shape[0], cols), lambda i, at: (0, 0)) for b in right],
            out_specs=pl.BlockSpec((size, cols), lambda i, at: (i, 0)),
        ),
        compiler_params=pltpu.CompilerParams(vmem_limit_bytes=VMEM),
        cost_estimate=pl.CostEstimate(flops=0, bytes_accessed=0, transcendentals=0),
    )(index, x, g, gate_up, *down)


def product_body(count, index, *refs):
    left, right, out = refs[:count], refs[count : 2 * count], refs[2 * count]
    out[...] = sum(dot_rows(a[...], b[...]) for a, b in zip(left, right)).astype(out.dtype)


def row_blocks(left, right, index, size):
    count = index.shape[0]
    cols = right[0].shape[1]
    tokens = sum(a.shape[0] for a in left)
    return pl.pallas_call(
        lambda *refs: product_body(len(left), *refs),
        out_shape=jax.ShapeDtypeStruct((count * size, cols), bf16),
        grid_spec=pltpu.PrefetchScalarGridSpec(
            num_scalar_prefetch=1,
            grid=(count,),
            in_specs=[pl.BlockSpec((a.shape[0], size), lambda i, at: (0, at[i])) for a in left]
            + [pl.BlockSpec((b.shape[0], cols), lambda i, at: (0, 0)) for b in right],
            out_specs=pl.BlockSpec((size, cols), lambda i, at: (i, 0)),
        ),
        compiler_params=pltpu.CompilerParams(vmem_limit_bytes=VMEM),
        cost_estimate=pl.CostEstimate(
            flops=2 * tokens * count * size * cols,
            bytes_accessed=2 * (tokens * cols + count * size * (tokens + cols)),
            transcendentals=0,
        ),
    )(index.astype(jnp.int32), *left, *right)


def part_maker(left, right, dims):
    unit = min(d[0] for d in dims)
    count = int(np.prod([d[1] for d in dims]))
    size = left[0].shape[1] // count
    cols = right[0].shape[1]
    ids = np.zeros((), np.int32)
    for stride, many in dims[:-1]:
        ids = ids[..., None] + np.arange(many, dtype=np.int32) * (stride // unit)
    ids = ids.reshape(-1)

    def make(index):
        index = jnp.asarray(ids) + index * (dims[-1][0] // unit)
        if size % 128 == 0:
            return row_blocks(left, right, index, size).reshape(-1, size, cols)
        out = sum(dot_rows(a, b) for a, b in zip(left, right)).astype(bf16)
        return out.reshape(count, size, cols)[index]

    return make


def feature_tables(heads):
    pairs = [(a, b) for a in range(QK + 1) for b in range(a, QK + 1)]
    one = np.zeros((heads, heads * QK, FEATS), np.float32)
    two = np.zeros((heads, heads * QK, FEATS), np.float32)
    rows = np.zeros((8, FEATS), np.float32)
    for f, (a, b) in enumerate(pairs):
        for h in range(heads):
            if a < QK:
                one[h, h * QK + a, f] = 1
            if b < QK:
                two[h, h * QK + b, f] = 1
        rows[0, f] = a == QK
        rows[1, f] = b == QK
        if a == QK:
            rows[2, f] = 1.0
        elif b == QK:
            rows[2, f] = QK**-0.5
        else:
            rows[2, f] = (0.5 if a == b else 1.0) / QK
    return jnp.asarray(one, bf16), jnp.asarray(two, bf16), jnp.asarray(rows)


def dot(a, b):
    return lax.dot_general(a, b, (((1,), (0,)), ((), ())), preferred_element_type=f32)


def dot_rows(a, b):
    return lax.dot_general(a, b, (((0,), (0,)), ((), ())), preferred_element_type=f32)


def dot_cols(a, b):
    return lax.dot_general(a, b, (((1,), (1,)), ((), ())), preferred_element_type=f32)


def halves(x):
    high = x.astype(bf16)
    return high, (x - high.astype(f32)).astype(bf16)


def features(x, one, two, rows):
    return dot(x, one) + rows[0:1], dot(x, two) + rows[1:2]


def total_row(state):
    return jnp.concatenate([state[FEATS : FEATS + 1], state[FEATS + 1 : FEATS + 2, : FEATS - 128]], axis=1)


def store_state(ref, state, row):
    ref[0, 0, :FEATS, :] = state
    ref[0, 0, FEATS:, :] = jnp.zeros((ROWS - FEATS, state.shape[1]), f32)
    ref[0, 0, FEATS : FEATS + 1, :] = row[:, :128]
    ref[0, 0, FEATS + 1 : FEATS + 2, : FEATS - 128] = row[:, 128:]


def kept_rows(scal, tile, tokens):
    index = lax.broadcasted_iota(jnp.int32, (tokens, 1), 0) + tile * tokens
    return index >= scal[tile]


def state_body(scal, k_ref, v_ref, one, two, rows, out_ref):
    tile = pl.program_id(0)
    a, b = features(k_ref[...], one[0], two[0], rows)
    phi = jnp.where(kept_rows(scal, tile, a.shape[0]), a * b, 0.0)
    high, low = halves(phi)
    v = v_ref[...]
    store_state(out_ref, dot_rows(high, v) + dot_rows(low, v), jnp.sum(phi, axis=0, keepdims=True))


def weights(q_ref, k_ref, lo_ref, tile, head):
    tokens, lanes = q_ref.shape
    lane = lax.broadcasted_iota(jnp.int32, (tokens, lanes), 1) // QK == head
    q = jnp.where(lane, q_ref[...], jnp.zeros((), bf16))
    score = dot_cols(q, k_ref[...]) * QK**-0.5
    row = lax.broadcasted_iota(jnp.int32, score.shape, 0)
    col = lax.broadcasted_iota(jnp.int32, score.shape, 1)
    lo = lo_ref[...] - tile * tokens
    mask = (col <= row) & (col >= lo)
    weight = jnp.where(mask, 1.0 + score + 0.5 * score * score, 0.0)
    return lane, score, mask, weight, lo < 0


def forward_body(q_ref, k_ref, v_ref, lo_ref, carry_ref, one, two, rows, y_ref, mixed_ref):
    tile, head = pl.program_id(0), pl.program_id(1)
    _, _, _, weight, alive = weights(q_ref, k_ref, lo_ref, tile, head)
    a, b = features(q_ref[...], one[0], two[0], rows)
    phi = jnp.where(alive, a * b * rows[2:3], 0.0)
    high, low = halves(phi)
    carry = carry_ref[0, 0]
    s_high, s_low = halves(carry[:FEATS])
    numer = dot(weight.astype(bf16), v_ref[...])
    numer = numer + (dot(high, s_high) + dot(high, s_low) + dot(low, s_high))
    denom = jnp.sum(weight, axis=1, keepdims=True) + jnp.sum(phi * total_row(carry), axis=1, keepdims=True)
    y = numer / denom
    y_ref[...] = y
    mixed_ref[...] = y.astype(bf16)


def spread(t, a, b, one, two):
    first_high, first_low = halves(t * b)
    second_high, second_low = halves(t * a)
    return (
        dot_cols(first_high, one) + dot_cols(first_low, one) + dot_cols(second_high, two) + dot_cols(second_low, two)
    )


def backward_body(
    q_ref, k_ref, v_ref, lo_ref, carry_ref, one, two, rows, y_ref, d_ref, dq_ref, dk_ref, dv_ref, ds_ref, dq_acc, dk_acc
):
    tile, head = pl.program_id(0), pl.program_id(1)
    lane, score, mask, weight, alive = weights(q_ref, k_ref, lo_ref, tile, head)
    a, b = features(q_ref[...], one[0], two[0], rows)
    phi = jnp.where(alive, a * b * rows[2:3], 0.0)
    high, low = halves(phi)
    carry = carry_ref[0, 0]
    s_high, s_low = halves(carry[:FEATS])
    row = total_row(carry)
    denom = jnp.sum(weight, axis=1, keepdims=True) + jnp.sum(phi * row, axis=1, keepdims=True)
    d = d_ref[...].astype(f32)
    g = d / denom
    c = -jnp.sum(d * y_ref[...], axis=1, keepdims=True) / denom
    g_high, g_low = halves(g)
    v = v_ref[...]
    dk = dot_cols(g_high, v) + dot_cols(g_low, v) + c
    ds = jnp.where(mask, dk * (1.0 + score) * QK**-0.5, 0.0).astype(bf16)
    dv_ref[...] = dot_rows(weight.astype(bf16), g_high)
    dphi = dot_cols(g_high, s_high) + dot_cols(g_high, s_low) + dot_cols(g_low, s_high) + c * row
    t = jnp.where(alive, dphi * rows[2:3], 0.0)
    dq = jnp.where(lane, dot(ds, k_ref[...]), 0.0) + spread(t, a, b, one[0], two[0])
    dkeys = jnp.where(lane, dot_rows(ds, q_ref[...]), 0.0)

    @pl.when(head == 0)
    def _():
        dq_acc[...] = dq
        dk_acc[...] = dkeys

    @pl.when(head > 0)
    def _():
        dq_acc[...] += dq
        dk_acc[...] += dkeys

    @pl.when(head == pl.num_programs(1) - 1)
    def _():
        dq_ref[...] = dq_acc[...].astype(bf16)
        dk_ref[...] = dk_acc[...]

    state = dot_rows(high, g_high) + dot_rows(high, g_low) + dot_rows(low, g_high)
    store_state(ds_ref, state, jnp.sum(phi * c, axis=0, keepdims=True))


def carried_body(scal, k_ref, v_ref, one, two, rows, grad_ref, dk_in, dv_in, dk_ref, dv_ref, acc):
    tile, head = pl.program_id(0), pl.program_id(1)
    a, b = features(k_ref[...], one[0], two[0], rows)
    keep = kept_rows(scal, tile, a.shape[0])
    high, low = halves(jnp.where(keep, a * b, 0.0))
    grad = grad_ref[0, 0]
    g_high, g_low = halves(grad[:FEATS])
    v = v_ref[...]
    dv = dv_in[...] + dot(high, g_high) + dot(high, g_low) + dot(low, g_high)
    dv_ref[...] = dv.astype(bf16)
    t = jnp.where(keep, dot_cols(v, g_high) + dot_cols(v, g_low) + total_row(grad), 0.0)
    dk = spread(t, a, b, one[0], two[0])

    @pl.when(head == 0)
    def _():
        acc[...] = dk_in[...] + dk

    @pl.when(head > 0)
    def _():
        acc[...] += dk

    @pl.when(head == pl.num_programs(1) - 1)
    def _():
        dk_ref[...] = acc[...].astype(bf16)


class Attention:
    def __init__(self, qkv, lo, heads, tokens):
        self.qkv, self.heads, self.tokens = qkv, heads, tokens
        self.lo = lo[:, None]
        self.scal = jnp.stack([lo[tokens - 1], lo[2 * tokens - 1]])
        self.tables = feature_tables(heads)
        lanes = heads * QK
        self.value = (qkv.shape[1] - 2 * lanes) // heads
        skip = 2 * lanes // self.value
        self.q = pl.BlockSpec((tokens, lanes), lambda t, h: (t, 0))
        self.k = pl.BlockSpec((tokens, lanes), lambda t, h: (t, 1))
        self.v = pl.BlockSpec((tokens, self.value), lambda t, h: (t, h + skip))
        self.o = pl.BlockSpec((tokens, self.value), lambda t, h: (t, h))
        self.l = pl.BlockSpec((tokens, 1), lambda t, h: (t, 0))
        self.s = pl.BlockSpec((1, 1, ROWS, self.value), lambda t, h: (h, t, 0, 0))
        self.e = pl.BlockSpec((1, lanes, FEATS), lambda t, h: (h, 0, 0))
        self.r = pl.BlockSpec((8, FEATS), lambda t, h: (0, 0))
        self.m = pl.BlockSpec(memory_space=pltpu.SMEM)
        self.table_specs = [self.e, self.e, self.r]
        self.acc = pltpu.VMEM((tokens, lanes), f32)
        self.state_shape = jax.ShapeDtypeStruct((heads, 2, ROWS, self.value), f32)

    def wide(self, kind):
        return jax.ShapeDtypeStruct((2 * self.tokens, self.heads * self.value), kind)

    def narrow(self, kind):
        return jax.ShapeDtypeStruct((2 * self.tokens, self.heads * QK), kind)

    def call(self, body, ins, outs, shapes, scratch, flops, args):
        size = sum(int(np.prod(a.shape)) * a.dtype.itemsize for a in list(args) + list(shapes))
        return pl.pallas_call(
            body,
            grid=(2, self.heads),
            in_specs=ins,
            out_specs=outs,
            out_shape=shapes,
            scratch_shapes=scratch,
            compiler_params=pltpu.CompilerParams(vmem_limit_bytes=VMEM),
            cost_estimate=pl.CostEstimate(flops=0, bytes_accessed=0, transcendentals=0),
        )(*args)

    def states(self):
        (out,) = self.call(
            state_body,
            [self.m, self.k, self.v] + self.table_specs,
            [self.s],
            [self.state_shape],
            [],
            3 * 10**9,
            (self.scal, self.qkv, self.qkv, *self.tables),
        )
        return out

    def forward(self, carry):
        return self.call(
            forward_body,
            [self.q, self.k, self.v, self.l, self.s] + self.table_specs,
            [self.o, self.o],
            [self.wide(f32), self.wide(bf16)],
            [],
            10 * 10**9,
            (self.qkv, self.qkv, self.qkv, self.lo, carry, *self.tables),
        )

    def backward(self, carry, y, d_heads):
        return self.call(
            backward_body,
            [self.q, self.k, self.v, self.l, self.s] + self.table_specs + [self.o, self.o],
            [self.q, self.q, self.o, self.s],
            [self.narrow(bf16), self.narrow(f32), self.wide(f32), self.state_shape],
            [self.acc, self.acc],
            30 * 10**9,
            (self.qkv, self.qkv, self.qkv, self.lo, carry, *self.tables, y, d_heads),
        )

    def carried(self, grad, dk, dv):
        return self.call(
            carried_body,
            [self.m, self.k, self.v] + self.table_specs + [self.s, self.q, self.o],
            [self.q, self.o],
            [self.narrow(bf16), self.wide(bf16)],
            [self.acc],
            10 * 10**9,
            (self.scal, self.qkv, self.qkv, *self.tables, grad, dk, dv),
        )


def others(state, earlier, kind):
    n = lax.axis_size("tok")
    me = lax.axis_index("tok")
    sign = 1 if earlier else -1
    if n != 32:
        parts = lax.all_gather(state.astype(kind), "tok").astype(f32)
        index = jnp.arange(n)
        before = (sign * (me // 2 - index // 2) > 0) & (index % 2 == me % 2)
        out = jnp.sum(jnp.where(before.reshape((n,) + (1,) * state.ndim), parts, 0.0), axis=0)
        return out, (state, out, out)
    plane = (me // 2) % 4
    slices = state.astype(kind).reshape((4, state.shape[0] // 4) + state.shape[1:])
    mine = [pick(slices, plane)]
    for k in range(1, 4):
        mine.append(flip(pick(slices, plane ^ k), 2 * k))
    mine = [part.astype(f32) for part in mine]
    whole = sum(mine).astype(kind)
    beyond = sum(shift(whole, (8, 4), sign * k, False).astype(f32) for k in range(1, 4))
    pieces = []
    for k in range(4):
        before = beyond
        for j in range(4):
            if j != k:
                before = before + jnp.where(sign * ((plane ^ k) - (plane ^ j)) > 0, mine[j], 0.0)
        before = before.astype(kind)
        pieces.append((plane ^ k, flip(before, 2 * k) if k else before))
    return assemble(pieces).reshape(state.shape).astype(f32), (slices, whole, beyond)


def row_starts(positions, lengths, offsets):
    inside = (positions[:, None] >= offsets[None, :]) & (positions[:, None] < offsets[None, :] + lengths[None, :])
    return jnp.sum(jnp.where(inside, offsets[None, :], 0), axis=1)


def side_by_side(core, mine, theirs, axis=0):
    size = mine.shape[axis]
    shape = list(mine.shape)
    shape[axis] *= 2
    out = jnp.zeros(shape, mine.dtype)
    out = lax.dynamic_update_slice_in_dim(out, mine, core * size, axis)
    return lax.dynamic_update_slice_in_dim(out, theirs, (1 - core) * size, axis)


def shards(
    block_input,
    lengths,
    offsets,
    norm1_gain,
    w_query,
    w_key,
    w_value,
    w_out,
    norm2_gain,
    w_gate,
    w_up,
    w_down,
    out_grad,
):
    n = lax.axis_size("tok")
    me = lax.axis_index("tok")
    core, quad = me % 2, me % 4
    cdims, qdims = chip_dims(n), quad_dims(n)
    chips, quads = n // 2, n // 4
    tokens, width = block_input.shape
    rows = w_query.shape[0]
    heads = w_query.shape[1] // QK // 2
    half = width // 2
    lanes = heads * QK
    x_last = [cdims[0]] + cdims[1:][::-1]

    def column_half(w, which):
        return lax.dynamic_slice_in_dim(w, which * (w.shape[1] // 2), w.shape[1] // 2, 1)

    def row_half(w, which):
        return lax.dynamic_slice_in_dim(w, which * (w.shape[0] // 2), w.shape[0] // 2, 0)

    gains = jnp.stack([norm1_gain, norm2_gain]).astype(f32)
    gains = gather(gains, [(1, 2)])

    def by_core(which):
        return jnp.concatenate([column_half(w, which) for w in (w_query, w_key, w_value)], axis=1)

    chip_qkv = side_by_side(core, by_core(core), flip(by_core(1 - core), 1))
    cut = chip_qkv.shape[1] // 2
    chip_qkv = gather_stage(chip_qkv, cdims[0])
    part_a, part_b = chip_qkv[..., :cut], chip_qkv[..., cut:]
    marks = [(chip_qkv,)]
    for dim_a, dim_b in zip(cdims[1:], x_last[1:]):
        part_a, part_b = gather_stage(part_a, dim_a), gather_stage(part_b, dim_b)
        marks.append((part_a, part_b))
    for dim, mark in zip(cdims, [None] + marks):
        gains = gather_stage(after(gains, *mark) if mark else gains, dim)
    gains = in_order(gains, cdims[::-1]).reshape(n, 2, rows).transpose(1, 0, 2).reshape(2, 1, width)
    gain_one, gain_two = gains[0], gains[1]
    qkv_all = jnp.concatenate([in_order(part_a, cdims[::-1]), in_order(part_b, x_last[::-1])], axis=2)
    qkv_all = qkv_all.reshape(width, 2 * cut)
    early, late = marks[0], marks[-1]

    inputs32 = block_input.astype(f32)
    ratio_one = lax.rsqrt(jnp.mean(inputs32 * inputs32, axis=1, keepdims=True) + eps)
    normed_one = inputs32 * ratio_one
    hidden_one = (normed_one * gain_one).astype(bf16)
    hidden_chip = side_by_side(core, hidden_one, flip(hidden_one, 1))
    qkv = dot(hidden_chip, qkv_all).astype(bf16)

    unit = w_down.shape[0]
    padded = -(-unit // 16) * 16
    cols = quads * padded

    def by_quad(w):
        w = w.reshape(rows, quads, 4, unit)
        w = jnp.pad(w, ((0, 0), (0, 0), (0, 0), (0, padded - unit)))
        return w.transpose(2, 0, 1, 3).reshape(4, rows, cols)

    gate_up = jnp.concatenate([by_quad(w_gate), by_quad(w_up)], axis=2)
    pieces = [(quad, pick(gate_up, quad))]
    for k in range(1, 4):
        pieces.append((quad ^ k, flip(pick(gate_up, quad ^ k), k)))
    gate_up = assemble(pieces).reshape(4 * rows, 2 * cols)
    groups = [[q + 4 * i for i in range(quads)] for q in range(4)]
    gate_up = lax.all_gather(gate_up, "tok", axis=0, tiled=True, axis_index_groups=groups)
    down = jnp.pad(w_down, ((0, padded - unit), (0, 0)))

    def step_of(dim, k):
        return lax.rem(place(dim) + dim[1] - k, dim[1]) * (dim[0] // 4)

    def first_stage(x, gates):
        dim = qdims[0]
        blocks = [(step_of(dim, 0), x)]
        for k, gate in zip(shift_order(dim[1]), gates + gates[-1:] * dim[1]):
            blocks.append((step_of(dim, k), shift(after(x, *gate), dim, k)))
        return blocks

    def next_stage(blocks, dim, gates):
        out = []
        for (i, x), gate in zip(blocks, gates + gates[-1:] * len(blocks)):
            out.append((i + step_of(dim, 0), x))
            x = after(x, *gate)
            out += [(i + step_of(dim, k), shift(x, dim, k)) for k in range(1, dim[1])]
        return out

    first = (me // 2) * 2 * tokens
    positions = first + jnp.arange(2 * tokens, dtype=jnp.int32)
    lo = row_starts(positions, lengths, offsets) - first
    attention = Attention(qkv, lo, heads, tokens)
    states = attention.states()
    fresh0 = (lo[tokens - 1] >= 0).astype(f32)
    fresh1 = (lo[2 * tokens - 1] >= tokens).astype(f32)
    entering, scan = others(states[:, 1] + (1.0 - fresh1) * states[:, 0], True, f32)
    carry = jnp.stack([entering, states[:, 0] + (1.0 - fresh0) * entering], axis=1)
    y_heads, mixed_heads = attention.forward(carry)
    mixed = side_by_side(core, row_half(mixed_heads, core), flip(row_half(mixed_heads, 1 - core), 1), 1)

    chip_out = side_by_side(core, column_half(w_out, core), flip(column_half(w_out, 1 - core), 1))
    out_half = after(chip_out, *early)
    for dim, gate in zip(cdims, [late, scan[1:2]] + [scan[2:3]] * len(cdims)):
        out_half = after(gather_stage(out_half, dim), *gate)
    out_half = in_order(out_half, cdims[::-1]).reshape(width, half)
    out_all = side_by_side(core, out_half, flip(out_half, 1), 1)
    middle = inputs32 + dot(mixed, out_all)
    ratio_two = lax.rsqrt(jnp.mean(middle * middle, axis=1, keepdims=True) + eps)
    normed_two = middle * ratio_two
    hidden_two = (normed_two * gain_two).astype(bf16)

    down = first_stage(down, [early])
    for dim in qdims[1:]:
        down = next_stage(down, dim, [scan[1:2]])

    far_grad = flip(after(out_grad, *late), 2)
    grad_quad = [
        jnp.concatenate([out_grad, flip(after(out_grad, *early), 1)]),
        jnp.concatenate([far_grad, flip(after(far_grad, mixed_heads), 1)]),
    ]
    far_hidden = flip(hidden_two, 2)
    near_hidden = jnp.concatenate([hidden_two, flip(hidden_two, 1)])
    near = ffn(near_hidden, grad_quad[0], gate_up, down)
    far_hidden = after(far_hidden, *near)
    far_hidden = jnp.concatenate([far_hidden, flip(far_hidden, 1)])
    far = ffn(far_hidden, grad_quad[1], gate_up, down)
    hidden_quad = [near_hidden, far_hidden]

    d_far = far[3][:tokens].astype(f32) + flip(far[3][tokens:], 1).astype(f32)
    d_far_low = d_far.astype(bf16)
    d_near = near[3][:tokens].astype(f32) + flip(near[3][tokens:], 1).astype(f32)
    d_far = flip(d_far_low, 2)

    last = qdims[-1][1]
    sent = row_blocks([after(near_hidden, d_far_low), far_hidden], [near[2], far[2]], jnp.arange(width // 128), 128)
    gate_sum = lax.psum_scatter(sent, "tok", scatter_dimension=0, tiled=True, axis_index_groups=groups)
    term = row_blocks([near[1], far[1]], [after(grad_quad[0], sent), grad_quad[1]], jnp.arange(cols // 128), 128)
    kept = term
    term = term.reshape(quads // last, last, padded, width)
    sum_down = Scatter(lambda index: pick(term, index, 1), qdims)
    sum_down.send()
    sum_down.keep()

    d_hidden_two = d_near + after(d_far, kept).astype(f32)
    term_norm_two = jnp.sum(d_hidden_two * normed_two, axis=0)
    scaled_two = d_hidden_two * gain_two
    d_middle = out_grad.astype(f32) + ratio_two * (
        scaled_two - normed_two * jnp.mean(scaled_two * normed_two, axis=1, keepdims=True)
    )
    d_mixed = d_middle.astype(bf16)
    d_mixed_chip = side_by_side(core, d_mixed, flip(d_mixed, 1))
    d_heads = dot_cols(d_mixed_chip, row_half(out_all, core)).astype(bf16)
    y_far = far[0][:tokens].astype(f32) + flip(far[0][tokens:], 1).astype(f32)
    y_near = near[0][:tokens].astype(f32) + flip(near[0][tokens:], 1).astype(f32)
    y_far_low = after(y_far.astype(bf16), d_mixed)
    y_far = flip(y_far_low, 2)

    d_heads = after(d_heads, y_far_low)
    dq, dk, dv, d_states = attention.backward(carry, y_heads, d_heads)
    leaving, scan = others(d_states[:, 0] + (1.0 - fresh0) * d_states[:, 1], False, bf16)
    grad_down = sum_down.finish((scan[0],), (dk,))[:unit]
    mixed_chip = jnp.concatenate(
        [
            side_by_side(core, mixed_heads[:tokens], flip(mixed_heads[:tokens], 1), 1),
            side_by_side(core, mixed_heads[tokens:], flip(mixed_heads[tokens:], 1), 1),
        ]
    )
    sum_out = Scatter(part_maker([after(mixed_chip, scan[0])], [column_half(d_mixed_chip, core)], cdims), cdims)
    sum_out.send()
    sum_out.keep()
    d_states = jnp.stack([d_states[:, 1] + (1.0 - fresh1) * leaving, leaving], axis=1)
    dk, dv = attention.carried(d_states, dk, dv)
    d_qkv = jnp.concatenate([dq, dk, dv], axis=1)

    sums = []
    for d, dims in ((d_qkv[:, :cut], cdims), (d_qkv[:, cut:], x_last)):
        sums.append(Scatter(part_maker([hidden_chip], [d], dims), dims))
        sums[-1].send()
    for part in sums:
        part.keep()

    d_rows = row_half(d_qkv, 1 - core)
    theirs = flip(dot_cols(d_rows, qkv_all).astype(bf16), 1)
    d_hidden_one = dot_cols(row_half(d_qkv, core), qkv_all) + theirs.astype(f32)
    term_norm_one = jnp.sum(d_hidden_one * normed_one, axis=0)
    scaled_one = d_hidden_one * gain_one
    input_grad = d_middle + ratio_one * (
        scaled_one - normed_one * jnp.mean(scaled_one * normed_one, axis=1, keepdims=True)
    )
    output = (middle + y_near + after(y_far, dk).astype(f32)).astype(bf16)

    gate_sum = after(gate_sum, dk).reshape(4, rows, 2 * cols)
    parts = [(quad, pick(gate_sum, quad).astype(f32))]
    for k in range(1, 4):
        parts.append((quad ^ k, flip(pick(gate_sum, quad ^ k), k).astype(f32)))
    gate_sum = assemble(parts).reshape(4, rows, 2, quads, padded)[..., :unit]
    gate_sum = gate_sum.transpose(2, 1, 3, 0, 4).reshape(2, rows, 4 * quads * unit)
    grad_gate, grad_up = gate_sum[0], gate_sum[1]

    def by_rows(total):
        return row_half(total, core), flip(row_half(total, 1 - core), 1)

    grad_out = side_by_side(core, *by_rows(sum_out.finish()), 1)
    mine, theirs = by_rows(jnp.concatenate([part.finish() for part in sums], axis=1))
    spans = [(0, lanes), (lanes, 2 * lanes), (2 * lanes, 2 * lanes + half)]
    grad_query, grad_key, grad_value = (side_by_side(core, mine[:, a:b], theirs[:, a:b], 1) for a, b in spans)

    norms = total(jnp.stack([term_norm_one, term_norm_two]), [(1, 2)] + cdims).reshape(2, n, rows)
    norms = pick(norms, me, 1)

    return (
        output,
        input_grad,
        norms[0],
        grad_query,
        grad_key,
        grad_value,
        grad_out,
        norms[1],
        grad_gate,
        grad_up,
        grad_down,
    )


def solution(mesh):
    return jax.shard_map(
        shards,
        mesh=mesh,
        in_specs=(
            P("tok", None),
            P(),
            P(),
            P("tok"),
            P("tok", None),
            P("tok", None),
            P("tok", None),
            P("tok", None),
            P("tok"),
            P("tok", None),
            P("tok", None),
            P("tok", None),
            P("tok", None),
        ),
        out_specs=(
            P("tok", None),
            P("tok", None),
            P("tok"),
            P("tok", None),
            P("tok", None),
            P("tok", None),
            P("tok", None),
            P("tok"),
            P("tok", None),
            P("tok", None),
            P("tok", None),
        ),
        check_vma=False,
    )
```

```python
import jax
import jax.numpy as jnp
import numpy as np
from jax import lax
from jax.experimental import pallas as pl
from jax.experimental.pallas import tpu as pltpu
from jax.sharding import PartitionSpec as P

QK = 16
PAIR = 8
FEATS = 160
ROWS = 168
VMEM = 56 * 1024 * 1024
eps = 1e-06
f32 = jnp.float32
bf16 = jnp.bfloat16


def bits_from(n, low):
    bits = []
    while low < n:
        bits.insert(0, low)
        low *= 2
    return bits


def flip(x, bits):
    n = lax.axis_size("tok")
    return lax.ppermute(x, "tok", [(i, i ^ bits) for i in range(n)])


def side(bit):
    return (lax.axis_index("tok") // bit) % 2


def pick(x, index, axis=0):
    return lax.dynamic_index_in_dim(x, index, axis, False)


def assemble(pieces):
    out = jnp.broadcast_to(pieces[0][1][None], (len(pieces),) + pieces[0][1].shape)
    for index, block in pieces[1:]:
        out = lax.dynamic_update_index_in_dim(out, block, index, 0)
    return out


def assemble_all(pieces):
    out = jnp.zeros((len(pieces),) + pieces[0][1].shape, pieces[0][1].dtype)
    for index, block in pieces:
        out = lax.dynamic_update_index_in_dim(out, block, index, 0)
    return out


def after(x, *others):
    return lax.optimization_barrier((x,) + others)[0] if others else x


def move(x, bits, start=(), stop=()):
    return after(flip(after(x, *start), bits), *stop)


def grow(x, bit, start=(), stop=()):
    return assemble([(side(bit), x), (1 - side(bit), move(x, bit, start, stop))])


def in_order(x, bits):
    done = bits[::-1]
    axes = [done.index(b) for b in sorted(done, reverse=True)]
    x = x.transpose(axes + list(range(len(done), x.ndim)))
    return x.reshape((-1,) + x.shape[len(done) :])


def grown(bits):
    at = [0]
    for bit in bits[::-1]:
        at = [i + j for i in at for j in (0, bit)]
    return at


class Scatter:
    def __init__(self, make, bits):
        self.make, self.bits, self.bit = make, bits, bits[-1]

    def send(self, *start):
        self.sent = after(self.make(1 - side(self.bit)), *start)
        self.here = flip(self.sent, self.bit)

    def keep(self, *gate):
        self.kept = self.make(after(side(self.bit), *gate))
        return self.kept

    def hold(self, x, *gate):
        x, self.here = lax.optimization_barrier((x, after(self.here, *gate)))
        return x

    def step(self, *gate):
        acc = self.kept.astype(f32) + after(self.here, *gate).astype(f32)
        self.bits = self.bits[:-1]
        if not self.bits:
            return acc[0]
        bit = self.bits[-1]
        acc = acc.reshape((-1, 2) + acc.shape[1:])
        self.sent = pick(acc, 1 - side(bit), 1).astype(bf16)
        self.kept = pick(acc, side(bit), 1)
        self.here = flip(self.sent, bit)
        return self.sent

    def finish(self, *gate):
        while len(self.bits) > 1:
            self.step(*gate)
        return self.step(*gate)


MESH = pl.DeviceIdType.MESH
INV = pl.BlockSpec(memory_space=pltpu.VMEM)


def across(me, bits):
    for bit in (1, 2, 4, 8, 16):
        if bits & bit:
            me = me + bit - 2 * bit * ((me // bit) % 2)
    return me


def meet(me, partners):
    barrier = pltpu.get_barrier_semaphore()
    for bits in partners:
        pl.semaphore_signal(barrier, inc=1, device_id=(across(me, bits),), device_id_type=MESH)
    pl.semaphore_wait(barrier, len(partners))


class Mail:
    def __init__(self, me, sems):
        self.me, self.sems, self.count, self.open = me, sems, 0, []
    def send(self, source, target, bits):
        at = self.count
        self.count += 1
        copy = pltpu.make_async_remote_copy(src_ref=source, dst_ref=target, send_sem=self.sems.at[0, at],
            recv_sem=self.sems.at[1, at], device_id=(across(self.me, bits),), device_id_type=MESH)
        copy.start()
        self.open.append(copy)
        return copy
    def local(self, source, target):
        at = self.count
        self.count += 1
        copy = pltpu.make_async_copy(source, target, self.sems.at[0, at])
        copy.start()
        return copy
    def close(self):
        for copy in self.open:
            copy.wait_send()


def first_body(gains_in, gate_in, up_in, mine, theirs, gains, gate, up, z4, chip, sems):
    me = lax.axis_index("tok")
    core, z = me % 2, me // 8
    meet(me, (1, 2, 4, 8, 9, 16))
    mail = Mail(me, sems)
    size = mine.shape[0]
    swap = mail.send(theirs, chip.at[pl.ds(core * size, size)], 1)
    own = mail.local(mine, chip.at[pl.ds(core * size, size)])
    gains[pl.ds(me, 1)] = gains_in[...]

    def member(d):
        return ((d // 8) % 2) * 2 + d % 2

    to_gate = [mail.send(gate_in.at[member(across(me, k))], gate.at[member(me)], k) for k in (9, 8, 1)]
    own.wait()
    swap.wait_recv()
    high = mail.send(chip, z4.at[z], 16)
    low = mail.send(chip, z4.at[z], 8)
    to_up = [mail.send(up_in.at[member(across(me, k))], up.at[member(me)], k) for k in (9, 8, 1)]
    kept = [
        mail.local(chip, z4.at[z]),
        mail.local(gate_in.at[member(me)], gate.at[member(me)]),
        mail.local(up_in.at[member(me)], up.at[member(me)]),
    ]
    for bit in (1, 2, 4):
        at = pl.ds((me // bit) * bit, bit)
        mail.send(gains.at[at], gains.at[at], bit).wait_recv()
    high.wait_recv()
    zh = across(me, 16) // 8
    low2 = mail.send(z4.at[zh], z4.at[zh], 8)
    for bit in (8, 16):
        at = pl.ds((me // bit) * bit, bit)
        mail.send(gains.at[at], gains.at[at], bit).wait_recv()
    for c in to_gate + to_up + [low, low2]:
        c.wait_recv()
    for c in kept:
        c.wait()
    mail.close()


def spread_first(gains, gate, up, mine, theirs):
    rows, cols = mine.shape
    return pl.pallas_call(
        first_body,
        out_shape=[
            jax.ShapeDtypeStruct((32,) + gains.shape[1:], f32),
            jax.ShapeDtypeStruct(gate.shape, bf16),
            jax.ShapeDtypeStruct(up.shape, bf16),
            jax.ShapeDtypeStruct((4, 2 * rows, cols), bf16),
        ],
        in_specs=[INV] * 5,
        out_specs=[INV] * 4,
        scratch_shapes=[pltpu.VMEM((2 * rows, cols), bf16), pltpu.SemaphoreType.DMA((2, 20))],
        compiler_params=pltpu.CompilerParams(collective_id=1, has_side_effects=True, vmem_limit_bytes=40 * 2**20),
    )(gains, gate, up, mine, theirs)


def second_body(z4, out_mine, out_theirs, gate, whole, out4, gate2, chip, sems):
    me = lax.axis_index("tok")
    core, z, place = me % 2, me // 8, (me // 2) % 4
    across_y, across_x = across(place, 2), across(place, 1)
    meet(me, (1, 2, 4, 8, 16))
    mail = Mail(me, sems)
    size, cut = out_mine.shape[0], z4.shape[2] // 2
    a, b = pl.ds(0, cut), pl.ds(cut, cut)
    ya = mail.send(z4.at[:, :, a], whole.at[:, place, :, a], 4)
    xb = mail.send(z4.at[:, :, b], whole.at[:, place, :, b], 2)
    swap = mail.send(out_theirs, chip.at[pl.ds(core * size, size)], 1)
    own = mail.local(out_mine, chip.at[pl.ds(core * size, size)])
    kept = [mail.local(z4, whole.at[:, place]), mail.local(gate, gate2.at[z // 2])]
    xa = mail.send(z4.at[:, :, a], whole.at[:, place, :, a], 2)
    yb = mail.send(z4.at[:, :, b], whole.at[:, place, :, b], 4)
    own.wait()
    swap.wait_recv()
    high = mail.send(chip, out4.at[z], 16)
    low = mail.send(chip, out4.at[z], 8)
    kept.append(mail.local(chip, out4.at[z]))
    gate_high = mail.send(gate, gate2.at[z // 2], 16)
    ya.wait_recv()
    xa2 = mail.send(whole.at[:, across_y, :, a], whole.at[:, across_y, :, a], 2)
    xb.wait_recv()
    yb2 = mail.send(whole.at[:, across_x, :, b], whole.at[:, across_x, :, b], 4)
    high.wait_recv()
    zh = across(me, 16) // 8
    low2 = mail.send(out4.at[zh], out4.at[zh], 8)
    for c in (xa, yb, xa2, yb2, low, low2, gate_high):
        c.wait_recv()
    for c in kept:
        c.wait()
    mail.close()


def spread_second(z4, out_mine, out_theirs, gate):
    rows, cols = out_mine.shape
    return pl.pallas_call(
        second_body,
        out_shape=[
            jax.ShapeDtypeStruct((4, 4) + z4.shape[1:], bf16),
            jax.ShapeDtypeStruct((4, 2 * rows, cols), bf16),
            jax.ShapeDtypeStruct((2,) + gate.shape, bf16),
        ],
        in_specs=[INV] * 4,
        out_specs=[INV] * 3,
        scratch_shapes=[pltpu.VMEM((2 * rows, cols), bf16), pltpu.SemaphoreType.DMA((2, 16))],
        compiler_params=pltpu.CompilerParams(collective_id=2, has_side_effects=True, vmem_limit_bytes=40 * 2**20),
    )(z4, out_mine, out_theirs, gate)


def scan_body(sign, s_ref, o_ref, stage, here, whole, zhere, back, bhere, sems):
    me = lax.axis_index("tok")
    z, plane = me // 8, (me // 2) % 4
    barrier = pltpu.get_barrier_semaphore()
    for k in (1, 2, 3):
        for to in (across(me, 2 * k), lax.rem(me + 8 * k, 32)):
            pl.semaphore_signal(barrier, inc=1, device_id=(to,), device_id_type=MESH)
    pl.semaphore_wait(barrier, 6)

    def slot(k):
        return (across(me, 2 * k) // 2) % 4

    def copy(source, target, sem, i, to):
        return pltpu.make_async_remote_copy(
            src_ref=source,
            dst_ref=target,
            send_sem=sems.at[sem, 0, i],
            recv_sem=sems.at[sem, 1, i],
            device_id=(to,),
            device_id_type=MESH,
        )

    def receives(k):
        return z - k >= 0 if sign > 0 else z + k < 4

    def sends(k):
        return z + k < 4 if sign > 0 else z - k >= 0

    copies = []
    for k in (3, 1, 2):
        stage[k - 1] = s_ref[pl.ds(2 * slot(k), 2)].astype(stage.dtype)
        copies.append(copy(stage.at[k - 1], here.at[k - 1], 0, k - 1, across(me, 2 * k)))
        copies[-1].start()
    mine = [s_ref[pl.ds(2 * plane, 2)]]
    for c in copies:
        c.wait()
    mine += [here[k - 1].astype(f32) for k in (1, 2, 3)]
    whole[...] = sum(mine).astype(whole.dtype)
    for k in (2, 1, 3):

        @pl.when(sends(k))
        def _(k=k):
            copy(whole, zhere.at[k - 1], 1, k - 1, me + 8 * k * sign).start()

    for k in (1, 2, 3):

        @pl.when(receives(k))
        def _(k=k):
            copy(whole, zhere.at[k - 1], 1, k - 1, me).wait_recv()

        @pl.when(jnp.logical_not(receives(k)))
        def _(k=k):
            zhere[k - 1] = jnp.zeros_like(whole)

    for k in (1, 2, 3):

        @pl.when(sends(k))
        def _(k=k):
            copy(whole, zhere.at[k - 1], 1, k - 1, me).wait_send()

    beyond = sum(zhere[k].astype(f32) for k in range(3))
    copies = []
    for k in (3, 1, 2, 0):
        before = beyond
        for j in range(4):
            if j != k:
                before = before + (sign * (slot(k) - slot(j)) > 0).astype(f32) * mine[j]
        if k == 0:
            o_ref[pl.ds(2 * plane, 2)] = before
        else:
            back[k - 1] = before.astype(back.dtype)
            copies.append(copy(back.at[k - 1], bhere.at[k - 1], 2, k - 1, across(me, 2 * k)))
            copies[-1].start()
    for c in copies:
        c.wait()
    for k in (1, 2, 3):
        o_ref[pl.ds(2 * slot(k), 2)] = bhere[k - 1].astype(f32)


def spans_of(cols, most=512):
    return [(s, min(most, cols - s)) for s in range(0, cols, most)]


def ffn_body(order, sides, x_ref, g_ref, *refs):
    gates, ups, down = refs[0:4], refs[4:8], refs[8]
    y_ref, act_ref, d_ref, dh_ref, w_gate_up, w_down, sem = refs[9:]
    cols = w_down.shape[0]

    @pl.when(pl.program_id(0) == 0)
    def _():
        copies = [pltpu.make_async_copy(down, w_down, sem.at[0])]
        size = gates[0].shape[1]
        for j, pieces in enumerate((gates, ups)):
            for k, piece in enumerate(pieces):
                for i, at in enumerate(order):
                    rows = pl.ds(pl.multiple_of((at + sides[k]) * size, 16), size)
                    target = w_gate_up.at[rows, pl.ds(j * cols, cols)]
                    copies.append(pltpu.make_async_copy(piece.at[i], target, sem.at[len(copies)]))
        for copy in copies:
            copy.start()
        for copy in copies:
            copy.wait()

    x, g = x_ref[...], g_ref[...]
    for s, w in spans_of(cols):
        gate, upper = dot(x, w_gate_up[:, s : s + w]), dot(x, w_gate_up[:, cols + s : cols + s + w])
        d_act = dot_cols(g, w_down[s : s + w, :])
        sigma = jax.nn.sigmoid(gate)
        smooth = gate * sigma
        act_ref[:, s : s + w] = (smooth * upper).astype(bf16)
        d_ref[:, s : s + w] = (d_act * upper * sigma * (1.0 + gate * (1.0 - sigma))).astype(bf16)
        d_ref[:, cols + s : cols + s + w] = (d_act * smooth).astype(bf16)
    y_ref[...] = dot(act_ref[...], w_down[...]).astype(bf16)
    dh_ref[...] = dot_cols(d_ref[...], w_gate_up[...]).astype(bf16)


def ffn(x, g, gate, up, down, order, sides, tile=256):
    tokens, width = x.shape
    cols = down.shape[0]

    def block(w):
        return pl.BlockSpec((tile, w), lambda i: (i, 0))

    return pl.pallas_call(
        lambda *refs: ffn_body(order, *refs),
        out_shape=[jax.ShapeDtypeStruct((tokens, w), bf16) for w in (width, cols, 2 * cols, width)],
        grid=(tokens // tile,),
        in_specs=[pl.BlockSpec(memory_space=pltpu.SMEM), block(width), block(width)] + [pl.BlockSpec(memory_space=pl.ANY)] * 9,
        out_specs=[block(width), block(cols), block(2 * cols), block(width)],
        scratch_shapes=[
            pltpu.VMEM((width, 2 * cols), bf16),
            pltpu.VMEM((cols, width), bf16),
            pltpu.SemaphoreType.DMA((8 * len(order) + 1,)),
        ],
        compiler_params=pltpu.CompilerParams(vmem_limit_bytes=VMEM),
        cost_estimate=pl.CostEstimate(flops=0, bytes_accessed=0, transcendentals=0),
    )(sides, x, g, *gate, *up, down)


def product_body(count, index, *refs):
    left, right, out = refs[:count], refs[count : 2 * count], refs[2 * count]
    out[...] = sum(dot_rows(a[...], b[...]) for a, b in zip(left, right)).astype(out.dtype)


def row_blocks(left, right, index, size, half=None):
    count = index.shape[0]
    cols = right[0].shape[1] // (1 if half is None else 2)
    at_col = half or 0
    tokens = sum(a.shape[0] for a in left)
    return pl.pallas_call(
        lambda *refs: product_body(len(left), *refs),
        out_shape=jax.ShapeDtypeStruct((count * size, cols), bf16),
        grid_spec=pltpu.PrefetchScalarGridSpec(
            num_scalar_prefetch=1,
            grid=(count,),
            in_specs=[pl.BlockSpec((a.shape[0], size), lambda i, at: (0, at[i])) for a in left]
            + [pl.BlockSpec((b.shape[0], cols), lambda i, at: (0, at_col)) for b in right],
            out_specs=pl.BlockSpec((size, cols), lambda i, at: (i, 0)),
        ),
        compiler_params=pltpu.CompilerParams(vmem_limit_bytes=VMEM),
        cost_estimate=pl.CostEstimate(flops=0, bytes_accessed=0, transcendentals=0),
    )(index, x, g, gate_up, *down)


def product_body(count, index, *refs):
    left, right, out = refs[:count], refs[count : 2 * count], refs[2 * count]
    out[...] = sum(dot_rows(a[...], b[...]) for a, b in zip(left, right)).astype(out.dtype)


def row_blocks(left, right, index, size, half=None):
    count = index.shape[0]
    cols = right[0].shape[1] // (1 if half is None else 2)
    at_col = half or 0
    tokens = sum(a.shape[0] for a in left)
    return pl.pallas_call(
        lambda *refs: product_body(len(left), *refs),
        out_shape=jax.ShapeDtypeStruct((count * size, cols), bf16),
        grid_spec=pltpu.PrefetchScalarGridSpec(
            num_scalar_prefetch=1,
            grid=(count,),
            in_specs=[pl.BlockSpec((a.shape[0], size), lambda i, at: (0, at[i])) for a in left]
            + [pl.BlockSpec((b.shape[0], cols), lambda i, at: (0, at_col)) for b in right],
            out_specs=pl.BlockSpec((size, cols), lambda i, at: (i, 0)),
        ),
        compiler_params=pltpu.CompilerParams(vmem_limit_bytes=VMEM),
        cost_estimate=pl.CostEstimate(
            flops=2 * tokens * count * size * cols,
            bytes_accessed=2 * (tokens * cols + count * size * (tokens + cols)),
            transcendentals=0,
        ),
    )(index.astype(jnp.int32), *left, *right)


def part_maker(left, right, bits, within=(0,), half=None):
    n = lax.axis_size("tok")
    size = left[0].shape[1] * 2 // n
    cols = right[0].shape[1] // (1 if half is None else 2)
    ids = np.asarray([(at + more) // 2 for at in grown(bits[:-1][::-1]) for more in within], np.int32)

    def make(index):
        index = jnp.asarray(ids) + index * (bits[-1] // 2)
        if size % 128 == 0:
            out = row_blocks(left, right, index, size, half)
        else:
            out = sum(dot_rows(a, b) for a, b in zip(left, right)).astype(bf16).reshape(n // 2, size, -1)
            out = out[index][..., (half or 0) * cols : (half or 0) * cols + cols]
        return out.reshape(-1, size * len(within), cols)

    return make


def feature_tables(heads):
    pairs = [(a, b) for a in range(QK + 1) for b in range(a, QK + 1)]
    one = np.zeros((heads, heads * QK, FEATS), np.float32)
    two = np.zeros((heads, heads * QK, FEATS), np.float32)
    rows = np.zeros((8, FEATS), np.float32)
    for f, (a, b) in enumerate(pairs):
        for h in range(heads):
            if a < QK:
                one[h, h * QK + a, f] = 1
            if b < QK:
                two[h, h * QK + b, f] = 1
        rows[0, f] = a == QK
        rows[1, f] = b == QK
        if a == QK:
            rows[2, f] = 1.0
        elif b == QK:
            rows[2, f] = QK**-0.5
        else:
            rows[2, f] = (0.5 if a == b else 1.0) / QK
    return jnp.asarray(one, bf16), jnp.asarray(two, bf16), jnp.asarray(rows)


def dot(a, b):
    return lax.dot_general(a, b, (((1,), (0,)), ((), ())), preferred_element_type=f32)


def dot_rows(a, b):
    return lax.dot_general(a, b, (((0,), (0,)), ((), ())), preferred_element_type=f32)


def dot_cols(a, b):
    return lax.dot_general(a, b, (((1,), (1,)), ((), ())), preferred_element_type=f32)


def halves(x):
    high = x.astype(bf16)
    return high, (x - high.astype(f32)).astype(bf16)


def features(x, one, two, rows):
    return dot(x, one) + rows[0:1], dot(x, two) + rows[1:2]


def total_row(state):
    return jnp.concatenate([state[FEATS : FEATS + 1], state[FEATS + 1 : FEATS + 2, : FEATS - 128]], axis=1)


def store_state(ref, state, row):
    ref[0, 0, :FEATS, :] = state
    ref[0, 0, FEATS:, :] = jnp.zeros((ROWS - FEATS, state.shape[1]), f32)
    ref[0, 0, FEATS : FEATS + 1, :] = row[:, :128]
    ref[0, 0, FEATS + 1 : FEATS + 2, : FEATS - 128] = row[:, 128:]


def kept_rows(scal, tile, tokens):
    index = lax.broadcasted_iota(jnp.int32, (tokens, 1), 0) + tile * tokens
    return index >= scal[tile]


def state_body(scal, k_ref, v_ref, one, two, rows, out_ref):
    tile = pl.program_id(0)
    a, b = features(k_ref[...], one[0], two[0], rows)
    phi = jnp.where(kept_rows(scal, tile, a.shape[0]), a * b, 0.0)
    high, low = halves(phi)
    v = v_ref[...]
    store_state(out_ref, dot_rows(high, v) + dot_rows(low, v), jnp.sum(phi, axis=0, keepdims=True))


def weights(q_ref, k_ref, lo_ref, tile, head):
    tokens, lanes = q_ref.shape
    lane = lax.broadcasted_iota(jnp.int32, (tokens, lanes), 1) // QK == head
    q = jnp.where(lane, q_ref[...], jnp.zeros((), bf16))
    score = dot_cols(q, k_ref[...]) * QK**-0.5
    row = lax.broadcasted_iota(jnp.int32, score.shape, 0)
    col = lax.broadcasted_iota(jnp.int32, score.shape, 1)
    lo = lo_ref[...] - tile * tokens
    mask = (col <= row) & (col >= lo)
    weight = jnp.where(mask, 1.0 + score + 0.5 * score * score, 0.0)
    return lane, score, mask, weight, lo < 0


def forward_body(q_ref, k_ref, v_ref, lo_ref, carry_ref, one, two, rows, y_ref, mixed_ref):
    tile, head = pl.program_id(0), pl.program_id(1)
    _, _, _, weight, alive = weights(q_ref, k_ref, lo_ref, tile, head)
    a, b = features(q_ref[...], one[0], two[0], rows)
    phi = jnp.where(alive, a * b * rows[2:3], 0.0)
    high, low = halves(phi)
    carry = carry_ref[0, 0]
    s_high, s_low = halves(carry[:FEATS])
    numer = dot(weight.astype(bf16), v_ref[...])
    numer = numer + (dot(high, s_high) + dot(high, s_low) + dot(low, s_high))
    denom = jnp.sum(weight, axis=1, keepdims=True) + jnp.sum(phi * total_row(carry), axis=1, keepdims=True)
    y = numer / denom
    y_ref[...] = y
    mixed_ref[...] = y.astype(bf16)


def spread(t, a, b, one, two):
    first_high, first_low = halves(t * b)
    second_high, second_low = halves(t * a)
    return (
        dot_cols(first_high, one) + dot_cols(first_low, one) + dot_cols(second_high, two) + dot_cols(second_low, two)
    )


def backward_body(
    q_ref, k_ref, v_ref, lo_ref, carry_ref, one, two, rows, y_ref, d_ref, dq_ref, dk_ref, dv_ref, ds_ref, dq_acc, dk_acc
):
    tile, head = pl.program_id(0), pl.program_id(1)
    lane, score, mask, weight, alive = weights(q_ref, k_ref, lo_ref, tile, head)
    a, b = features(q_ref[...], one[0], two[0], rows)
    phi = jnp.where(alive, a * b * rows[2:3], 0.0)
    high, low = halves(phi)
    carry = carry_ref[0, 0]
    s_high, s_low = halves(carry[:FEATS])
    row = total_row(carry)
    denom = jnp.sum(weight, axis=1, keepdims=True) + jnp.sum(phi * row, axis=1, keepdims=True)
    d = d_ref[...].astype(f32)
    g = d / denom
    c = -jnp.sum(d * y_ref[...], axis=1, keepdims=True) / denom
    g_high, g_low = halves(g)
    v = v_ref[...]
    dk = dot_cols(g_high, v) + dot_cols(g_low, v) + c
    ds = jnp.where(mask, dk * (1.0 + score) * QK**-0.5, 0.0).astype(bf16)
    dv_ref[...] = dot_rows(weight.astype(bf16), g_high)
    dphi = dot_cols(g_high, s_high) + dot_cols(g_high, s_low) + dot_cols(g_low, s_high) + c * row
    t = jnp.where(alive, dphi * rows[2:3], 0.0)
    dq = jnp.where(lane, dot(ds, k_ref[...]), 0.0) + spread(t, a, b, one[0], two[0])
    dkeys = jnp.where(lane, dot_rows(ds, q_ref[...]), 0.0)

    @pl.when(head == 0)
    def _():
        dq_acc[...] = dq
        dk_acc[...] = dkeys

    @pl.when(head > 0)
    def _():
        dq_acc[...] += dq
        dk_acc[...] += dkeys

    @pl.when(head == pl.num_programs(1) - 1)
    def _():
        dq_ref[...] = dq_acc[...].astype(bf16)
        dk_ref[...] = dk_acc[...]

    state = dot_rows(high, g_high) + dot_rows(high, g_low) + dot_rows(low, g_high)
    store_state(ds_ref, state, jnp.sum(phi * c, axis=0, keepdims=True))


def carried_body(scal, k_ref, v_ref, one, two, rows, grad_ref, dk_in, dv_in, dk_ref, dv_ref, acc):
    tile, head = pl.program_id(0), pl.program_id(1)
    a, b = features(k_ref[...], one[0], two[0], rows)
    keep = kept_rows(scal, tile, a.shape[0])
    high, low = halves(jnp.where(keep, a * b, 0.0))
    grad = grad_ref[0, 0]
    g_high, g_low = halves(grad[:FEATS])
    v = v_ref[...]
    dv = dv_in[...] + dot(high, g_high) + dot(high, g_low) + dot(low, g_high)
    dv_ref[...] = dv.astype(bf16)
    t = jnp.where(keep, dot_cols(v, g_high) + dot_cols(v, g_low) + total_row(grad), 0.0)
    dk = spread(t, a, b, one[0], two[0])

    @pl.when(head == 0)
    def _():
        acc[...] = dk_in[...] + dk

    @pl.when(head > 0)
    def _():
        acc[...] += dk

    @pl.when(head == pl.num_programs(1) - 1)
    def _():
        dk_ref[...] = acc[...].astype(bf16)


class Attention:
    def __init__(self, qkv, lo, heads, tokens):
        self.qkv, self.heads, self.tokens = qkv, heads, tokens
        self.lo = lo[:, None]
        self.scal = jnp.stack([lo[tokens - 1], lo[2 * tokens - 1]])
        self.tables = feature_tables(heads)
        lanes = heads * QK
        self.value = (qkv.shape[1] - 2 * lanes) // heads
        skip = 2 * lanes // self.value
        self.q = pl.BlockSpec((tokens, lanes), lambda t, h: (t, 0))
        self.k = pl.BlockSpec((tokens, lanes), lambda t, h: (t, 1))
        self.v = pl.BlockSpec((tokens, self.value), lambda t, h: (t, h + skip))
        self.o = pl.BlockSpec((tokens, self.value), lambda t, h: (t, h))
        self.l = pl.BlockSpec((tokens, 1), lambda t, h: (t, 0))
        self.s = pl.BlockSpec((1, 1, ROWS, self.value), lambda t, h: (h, t, 0, 0))
        self.e = pl.BlockSpec((1, lanes, FEATS), lambda t, h: (h, 0, 0))
        self.r = pl.BlockSpec((8, FEATS), lambda t, h: (0, 0))
        self.m = pl.BlockSpec(memory_space=pltpu.SMEM)
        self.table_specs = [self.e, self.e, self.r]
        self.acc = pltpu.VMEM((tokens, lanes), f32)
        self.state_shape = jax.ShapeDtypeStruct((heads, 2, ROWS, self.value), f32)

    def wide(self, kind):
        return jax.ShapeDtypeStruct((2 * self.tokens, self.heads * self.value), kind)

    def narrow(self, kind):
        return jax.ShapeDtypeStruct((2 * self.tokens, self.heads * QK), kind)

    def call(self, body, ins, outs, shapes, scratch, flops, args):
        size = sum(int(np.prod(a.shape)) * a.dtype.itemsize for a in list(args) + list(shapes))
        return pl.pallas_call(
            body,
            grid=(2, self.heads),
            in_specs=ins,
            out_specs=outs,
            out_shape=shapes,
            scratch_shapes=scratch,
            compiler_params=pltpu.CompilerParams(vmem_limit_bytes=VMEM),
            cost_estimate=pl.CostEstimate(flops=0, bytes_accessed=0, transcendentals=0),
        )(*args)

    def states(self):
        (out,) = self.call(
            state_body,
            [self.m, self.k, self.v] + self.table_specs,
            [self.s],
            [self.state_shape],
            [],
            3 * 10**9,
            (self.scal, self.qkv, self.qkv, *self.tables),
        )
        return out

    def forward(self, carry):
        return self.call(
            forward_body,
            [self.q, self.k, self.v, self.l, self.s] + self.table_specs,
            [self.o, self.o],
            [self.wide(f32), self.wide(bf16)],
            [],
            10 * 10**9,
            (self.qkv, self.qkv, self.qkv, self.lo, carry, *self.tables),
        )

    def backward(self, carry, y, d_heads):
        return self.call(
            backward_body,
            [self.q, self.k, self.v, self.l, self.s] + self.table_specs + [self.o, self.o],
            [self.q, self.q, self.o, self.s],
            [self.narrow(bf16), self.narrow(f32), self.wide(f32), self.state_shape],
            [self.acc, self.acc],
            30 * 10**9,
            (self.qkv, self.qkv, self.qkv, self.lo, carry, *self.tables, y, d_heads),
        )

    def carried(self, grad, dk, dv):
        return self.call(
            carried_body,
            [self.m, self.k, self.v] + self.table_specs + [self.s, self.q, self.o],
            [self.q, self.o],
            [self.narrow(bf16), self.wide(bf16)],
            [self.acc],
            10 * 10**9,
            (self.scal, self.qkv, self.qkv, *self.tables, grad, dk, dv),
        )


def others(state, earlier, kind):
    n = lax.axis_size("tok")
    me = lax.axis_index("tok")
    sign = 1 if earlier else -1
    if n != 32:
        parts = lax.all_gather(state.astype(kind), "tok").astype(f32)
        index = jnp.arange(n)
        before = (sign * (me // 2 - index // 2) > 0) & (index % 2 == me % 2)
        out = jnp.sum(jnp.where(before.reshape((n,) + (1,) * state.ndim), parts, 0.0), axis=0)
        return out
    block = (state.shape[0] // 4,) + state.shape[1:]
    slots = pltpu.VMEM((3,) + block, kind)
    return pl.pallas_call(
        lambda *refs: scan_body(sign, *refs),
        out_shape=jax.ShapeDtypeStruct(state.shape, f32),
        in_specs=[INV],
        out_specs=INV,
        scratch_shapes=[slots, slots, pltpu.VMEM(block, kind), slots, slots, slots, pltpu.SemaphoreType.DMA((3, 2, 3))],
        compiler_params=pltpu.CompilerParams(
            collective_id=3 if earlier else 4, has_side_effects=True, vmem_limit_bytes=VMEM
        ),
        cost_estimate=pl.CostEstimate(flops=0, bytes_accessed=0, transcendentals=0),
    )(state)


def row_starts(positions, lengths, offsets):
    inside = (positions[:, None] >= offsets[None, :]) & (positions[:, None] < offsets[None, :] + lengths[None, :])
    return jnp.sum(jnp.where(inside, offsets[None, :], 0), axis=1)


def side_by_side(core, mine, theirs, axis=0):
    size = mine.shape[axis]
    shape = list(mine.shape)
    shape[axis] *= 2
    out = jnp.zeros(shape, mine.dtype)
    out = lax.dynamic_update_slice_in_dim(out, mine, core * size, axis)
    return lax.dynamic_update_slice_in_dim(out, theirs, (1 - core) * size, axis)


def shards(
    block_input,
    lengths,
    offsets,
    norm1_gain,
    w_query,
    w_key,
    w_value,
    w_out,
    norm2_gain,
    w_gate,
    w_up,
    w_down,
    out_grad,
):
    n = lax.axis_size("tok")
    me = lax.axis_index("tok")
    core, member = me % 2, side(PAIR) * 2 + me % 2
    cbits = bits_from(n, 2)
    qbits = [bit for bit in cbits if bit != PAIR]
    swapped = qbits[:-2] + [qbits[-1], qbits[-2]]
    chips, quads = n // 2, n // 4
    above, below = n // (2 * PAIR), PAIR // 2
    groups = [
        [i * 2 * PAIR + p * PAIR + j * 2 + c for i in range(above) for j in range(below)] for p in (0, 1) for c in (0, 1)
    ]
    to_member = {1: 1, 2: PAIR, 3: PAIR + 1}
    tokens, width = block_input.shape
    rows = w_query.shape[0]
    heads = w_query.shape[1] // QK // 2
    half = width // 2
    lanes = heads * QK
    def column_half(w, which):
        return lax.dynamic_slice_in_dim(w, which * (w.shape[1] // 2), w.shape[1] // 2, 1)

    def row_half(w, which):
        return lax.dynamic_slice_in_dim(w, which * (w.shape[0] // 2), w.shape[0] // 2, 0)

    unit = w_down.shape[0]
    padded = -(-unit // 16) * 16
    cols = quads * padded

    def by_quad(w):
        w = w.reshape(rows, above, 2, below, 2, unit)
        w = jnp.pad(w, ((0, 0),) * 5 + ((0, padded - unit),))
        return w.transpose(2, 4, 0, 1, 3, 5).reshape(4, rows, cols)

    gate, up = by_quad(w_gate), by_quad(w_up)
    down = jnp.pad(w_down, ((0, padded - unit), (0, 0)))
    near_grad = flip(out_grad, 1)

    def by_core(which):
        return jnp.concatenate([column_half(w, which) for w in (w_query, w_key, w_value)], axis=1)

    gains = jnp.stack([norm1_gain, norm2_gain]).astype(f32)
    if n == 32:
        gains = jnp.pad(gains, ((0, 6), (0, 128 - rows)))[None]
        gains = after(gains, near_grad)
        gains, gate, up, qkv_all = spread_first(gains, gate, up, by_core(core), by_core(1 - core))
        gains = gains[:, :2, :rows].transpose(1, 0, 2).reshape(2, 1, width)
        z4 = qkv_all
        qkv_all, out_half, gate = spread_second(z4, column_half(w_out, core), column_half(w_out, 1 - core), gate)
        qkv_all = qkv_all.reshape(width, -1)
    else:

        def to_group(x):
            pieces = [(member, pick(x, member))]
            for k in range(1, 4):
                pieces.append((member ^ k, flip(pick(x, member ^ k), to_member[k])))
            return assemble_all(pieces)

        gate, up = to_group(gate), to_group(up)
        qkv_all = side_by_side(core, by_core(core), flip(by_core(1 - core), 1))
        gains = grow(gains, 1)
        for bit in cbits:
            gains, qkv_all = grow(gains, bit), grow(qkv_all, bit)
        gains = in_order(gains, [1] + cbits).transpose(1, 0, 2).reshape(2, 1, width)
        qkv_all = in_order(qkv_all, cbits).reshape(width, -1)
        out_half = side_by_side(core, column_half(w_out, core), flip(column_half(w_out, 1 - core), 1))
        for bit in cbits[:-2]:
            out_half = grow(out_half, bit)
        out_half = in_order(out_half, cbits[:-2])
        gate = grow(gate, qbits[0])
    gain_one, gain_two = gains[0], gains[1]

    inputs32 = block_input.astype(f32)
    ratio_one = lax.rsqrt(jnp.mean(inputs32 * inputs32, axis=1, keepdims=True) + eps)
    normed_one = inputs32 * ratio_one
    hidden_one = (normed_one * gain_one).astype(bf16)
    hidden_chip = side_by_side(core, hidden_one, move(hidden_one, 1, (), (qkv_all,)))
    qkv = dot(hidden_chip, qkv_all).astype(bf16)

    first = (me // 2) * 2 * tokens
    positions = first + jnp.arange(2 * tokens, dtype=jnp.int32)
    lo = row_starts(positions, lengths, offsets) - first
    attention = Attention(qkv, lo, heads, tokens)
    states = attention.states()
    fresh0 = (lo[tokens - 1] >= 0).astype(f32)
    fresh1 = (lo[2 * tokens - 1] >= tokens).astype(f32)

    start, stop = (qkv_all,), (states,)
    down = lax.all_gather(after(down, qkv_all), "tok", axis=0, tiled=True, axis_index_groups=groups)
    for bit in qbits[1:-2]:
        gate = grow(gate, bit)
    gate_x = move(gate, 2, start, stop)
    up = grow(up, qbits[0], start, stop)
    for bit in qbits[1:-2]:
        up = grow(up, bit)
    out_y = move(out_half, 4, start, stop)
    leaving = states[:, 1] + (1.0 - fresh1) * states[:, 0]
    leaving, gate_x, up, out_y = lax.optimization_barrier((leaving, gate_x, up, out_y))
    entering = others(leaving, True, f32)
    start, stop = (leaving,), (entering,)
    flows = [(out_half, 2), (out_y, 2), (up, 4), (gate, 4), (up, 2)]
    flows = [move(w, bit, start, stop) for w, bit in flows]
    entering, out_x, out_xy, up_y, gate_y, up_x = lax.optimization_barrier((entering, *flows))
    carry = jnp.stack([entering, states[:, 0] + (1.0 - fresh0) * entering], axis=1)
    place = (me // 2) % 4
    out_pieces = [(place, out_half), (place ^ 1, out_x), (place ^ 2, out_y), (place ^ 3, out_xy)]
    out_half = jnp.zeros((chips // 4, 4, 2 * rows, half), bf16)
    for index, piece in out_pieces:
        out_half = lax.dynamic_update_index_in_dim(out_half, piece, index, 1)
    out_half = out_half.reshape(width, half)
    carry = after(carry, out_half)
    y_heads, mixed_heads = attention.forward(carry)
    start, stop = (carry,), (mixed_heads,)
    flows = [(gate_x, 4), (up_y, 2), (out_grad, PAIR), (out_half, 1)]
    flows = [move(w, bit, start, stop) for w, bit in flows]
    mixed_heads, gate_xy, up_xy, far_grad, out_there, down = lax.optimization_barrier((mixed_heads, *flows, down))
    out_all = side_by_side(core, out_half, out_there, 1)
    mixed_there = flip(mixed_heads, 1)
    mixed_chip = side_by_side(core, mixed_heads, mixed_there, 1)
    middle = inputs32 + dot(row_half(mixed_chip, core), out_all)
    ratio_two = lax.rsqrt(jnp.mean(middle * middle, axis=1, keepdims=True) + eps)
    normed_two = middle * ratio_two
    hidden_two = (normed_two * gain_two).astype(bf16)

    far_hidden = flip(hidden_two, PAIR)
    near_grad = jnp.concatenate([out_grad, near_grad])
    near_hidden = jnp.concatenate([hidden_two, flip(hidden_two, 1)])
    gate = [w.reshape(-1, 2 * rows, cols) for w in (gate, gate_x, gate_y, gate_xy)]
    up = [w.reshape(-1, 2 * rows, cols) for w in (up, up_x, up_y, up_xy)]
    order = [(at + more) // 2 for at in grown(qbits[:-2]) for more in (0, PAIR)]
    sides = jnp.stack([place, place ^ 1, place ^ 2, place ^ 3])
    near = ffn(near_hidden, near_grad, gate, up, down, order, sides)
    far_hidden, far_there = after(far_hidden, *near), move(far_grad, 1, (near_hidden,), (near[0],))
    far_grad = jnp.concatenate([far_grad, far_there])
    far_hidden = jnp.concatenate([far_hidden, flip(far_hidden, 1)])
    far = ffn(far_hidden, far_grad, gate, up, down, order, sides)
    start, stop = (near[0], far_hidden), (far[0],)
    near_parts = [move(near[i][tokens:], 1, start, stop) for i in (3, 0)]
    far, near_parts = lax.optimization_barrier((far, near_parts))

    right = [near[2], far[2]]
    sum_gate = Scatter(part_maker([near_hidden, far_hidden], right, qbits, (0, PAIR), 0), qbits)
    sum_gate.send()
    start, stop = (far[0],), (sum_gate.sent,)
    far_parts = [move(far[i][tokens:], 1, start, stop) for i in (3, 0)]
    sent, far_parts = lax.optimization_barrier((sum_gate.sent, far_parts))
    d_far = (far[3][:tokens].astype(f32) + far_parts[0].astype(f32)).astype(bf16)
    sum_up = Scatter(part_maker([after(near_hidden, sent, d_far), far_hidden], right, swapped, (0, PAIR), 1), swapped)
    sum_up.send()
    sum_gate.keep(sum_up.sent)
    sum_up.keep(sum_gate.kept)
    term = row_blocks([near[1], far[1]], [after(near_grad, sum_up.kept), far_grad], jnp.arange(cols // 128), 128)
    d_far = move(d_far, PAIR, (), (term,))
    d_far = sum_gate.hold(d_far, term)
    near_parts, far_parts = after(near_parts, d_far), after(far_parts, d_far)
    d_near = near[3][:tokens].astype(f32) + near_parts[0].astype(f32)
    y_near = near[0][:tokens].astype(f32) + near_parts[1].astype(f32)
    y_far = (far[0][:tokens].astype(f32) + far_parts[1].astype(f32)).astype(bf16)
    d_hidden_two = d_near + d_far.astype(f32)
    term_norm_two = jnp.sum(d_hidden_two * normed_two, axis=0)
    scaled_two = d_hidden_two * gain_two
    d_middle = out_grad.astype(f32) + ratio_two * (
        scaled_two - normed_two * jnp.mean(scaled_two * normed_two, axis=1, keepdims=True)
    )
    d_mixed = d_middle.astype(bf16)
    d_mixed_chip = side_by_side(core, d_mixed, flip(d_mixed, 1))
    d_heads = dot_cols(d_mixed_chip, row_half(out_all, core)).astype(bf16)

    d_heads = sum_up.hold(after(d_heads, y_far), d_mixed)
    d_heads = after(d_heads, sum_gate.step(), sum_up.step())

    def down_x(index):
        return pick(term.reshape(quads // 2, 2, padded, width)[..., :half], index, 1)

    def down_y(index):
        return pick(term.reshape(quads // 4, 2, 2, padded, width)[..., half:], index, 1).reshape(-1, padded, half)

    sum_down = [Scatter(down_x, qbits), Scatter(down_y, swapped)]
    for part in sum_down:
        part.send(d_heads)
        part.keep()
        d_heads = after(d_heads, part.sent, part.kept)
    dq, dk, dv, d_states = attention.backward(carry, y_heads, d_heads)
    y_far = move(y_far, PAIR, (d_heads,), (d_states,))
    for part in [sum_gate, sum_up] + sum_down:
        d_states = part.hold(d_states, d_states)
    d_states, y_far = lax.optimization_barrier((d_states, y_far))
    sent = [part.step() for part in [sum_gate, sum_up] + sum_down]
    d_mixed_half = column_half(d_mixed_chip, core)
    out_sums = []
    for h, bits in ((0, cbits), (1, cbits[:-2] + [cbits[-1], cbits[-2]])):
        out_sums.append(Scatter(part_maker([after(mixed_chip, *sent)], [d_mixed_half], bits, (0,), h), bits))
        out_sums[-1].send()
    leaving = d_states[:, 0] + (1.0 - fresh0) * d_states[:, 1]
    leaving = others(after(leaving, *(part.sent for part in out_sums)), False, bf16)
    for part in out_sums:
        leaving = after(leaving, part.keep(leaving))
    for part in sum_down:
        leaving = part.hold(leaving, leaving)
    leaving = after(leaving, *(part.step() for part in sum_down))
    d_states = jnp.stack([d_states[:, 1] + (1.0 - fresh1) * leaving, leaving], axis=1)
    dk, dv = attention.carried(d_states, dk, dv)
    for part in out_sums + [sum_gate, sum_up] + sum_down:
        dk = part.hold(dk, dk)
    sent = [part.step() for part in out_sums]
    gate_sum = jnp.stack([part.finish().reshape(4, rows, cols) for part in (sum_gate, sum_up)], axis=1)
    parts = [pick(gate_sum, member ^ k).astype(bf16) for k in range(1, 4)]
    d_qkv = after(jnp.concatenate([dq, dk, dv], axis=1), *sent, *parts)

    if (2 * rows) % 128 == 0:
        terms = row_blocks([hidden_chip], [d_qkv], jnp.arange(chips), 2 * rows)
    else:
        terms = dot_rows(hidden_chip, d_qkv).astype(bf16)
    parts = [move(part, to_member[k], (), (terms,)) for k, part in enumerate(parts, 1)]
    for part in out_sums:
        terms = part.hold(terms, terms)
    terms, parts = lax.optimization_barrier((terms, parts))
    terms = terms.reshape(chips // 4, 2, 2, 2 * rows, -1)
    cut = terms.shape[-1] // 2

    def along_x(index):
        return pick(terms[..., :cut], index, 2).reshape(chips // 2, 2 * rows, cut)

    def along_y(index):
        return pick(terms[..., cut:], index, 1).reshape(chips // 2, 2 * rows, cut)

    sums = [Scatter(along_x, cbits), Scatter(along_y, cbits[:-2] + [cbits[-1], cbits[-2]])]
    for part in sums:
        part.send()

    def join(both):
        out = Scatter(None, cbits[:-2] + [0])
        out.kept = jnp.concatenate([part.kept for part in both], axis=2)
        out.here = jnp.concatenate([part.here for part in both], axis=2)
        return out

    rest_out = join(out_sums)
    sent = rest_out.step()
    d_qkv = after(d_qkv, sent, *(part.sent for part in sums))
    theirs = flip(dot_cols(row_half(d_qkv, 1 - core), qkv_all).astype(bf16), 1)
    d_hidden_one = dot_cols(row_half(d_qkv, core), qkv_all) + theirs.astype(f32)
    term_norm_one = jnp.sum(d_hidden_one * normed_one, axis=0)
    scaled_one = d_hidden_one * gain_one
    mean_one = jnp.mean(scaled_one * normed_one, axis=1, keepdims=True)
    norms = jnp.stack([term_norm_one, term_norm_two])
    for part in sums:
        part.keep()
        norms = part.hold(norms, norms)
    norms = rest_out.hold(norms, norms)
    sent = [part.step() for part in sums] + [rest_out.step() for _ in rest_out.bits[1:]]
    norms = after(norms, *sent)
    norms = norms + flip(norms, 1)
    gate_sum = assemble_all([(member, pick(gate_sum, member))] + [(member ^ k, p.astype(f32)) for k, p in enumerate(parts, 1)])
    gate_sum = after(gate_sum, *sent).reshape(2, 2, 2, rows, above, below, padded)[..., :unit]
    norms = norms + flip(norms, cbits[-1])
    for part in sums:
        norms = part.hold(norms, gate_sum)
    rest = join(sums)
    sent = rest.step()
    norms = after(norms, sent)
    norms = norms + flip(norms, cbits[-2])
    gate_sum = after(gate_sum, sent).transpose(2, 3, 4, 0, 5, 1, 6).reshape(2, rows, n * unit)
    grad_gate, grad_up = gate_sum[0], gate_sum[1]
    norms = rest.hold(norms, norms)
    while len(rest.bits) > 1:
        sent = rest.step()
    norms = after(norms, sent)
    for bit in cbits[:-2]:
        norms = norms + flip(norms, bit)
    norms = pick(norms.reshape(2, n, rows), me, 1)
    input_grad = d_middle + ratio_one * (after(scaled_one, sent) - normed_one * mean_one)
    output = (after(middle, sent) + y_near + y_far.astype(f32)).astype(bf16)
    grad_down = jnp.concatenate([part.finish() for part in sum_down], axis=1)[:unit]
    rest.kept = jnp.concatenate([rest.kept, rest_out.kept], axis=2)
    rest.here = jnp.concatenate([rest.here, rest_out.here], axis=2)
    total = rest.step()
    mine, theirs = row_half(total, core), flip(row_half(total, 1 - core), 1)
    spans = [(0, lanes), (lanes, 2 * lanes), (2 * lanes, 2 * lanes + half), (2 * cut, 2 * cut + half)]
    grad_query, grad_key, grad_value, grad_out = (
        side_by_side(core, mine[:, a:b], theirs[:, a:b], 1) for a, b in spans
    )

    return (
        output,
        input_grad,
        norms[0],
        grad_query,
        grad_key,
        grad_value,
        grad_out,
        norms[1],
        grad_gate,
        grad_up,
        grad_down,
    )


def solution(mesh):
    return jax.shard_map(
        shards,
        mesh=mesh,
        in_specs=(
            P("tok", None),
            P(),
            P(),
            P("tok"),
            P("tok", None),
            P("tok", None),
            P("tok", None),
            P("tok", None),
            P("tok"),
            P("tok", None),
            P("tok", None),
            P("tok", None),
            P("tok", None),
        ),
        out_specs=(
            P("tok", None),
            P("tok", None),
            P("tok"),
            P("tok", None),
            P("tok", None),
            P("tok", None),
            P("tok", None),
            P("tok"),
            P("tok", None),
            P("tok", None),
            P("tok", None),
        ),
        check_vma=False,
    )
```

```python
import jax
import jax.numpy as jnp
import numpy as np
from jax import lax
from jax.experimental import pallas as pl
from jax.experimental.pallas import tpu as pltpu
from jax.sharding import PartitionSpec as P

QK = 16
PAIR = 8
FEATS = 160
ROWS = 168
MIB = 1024 * 1024
eps = 1e-06
f32 = jnp.float32
bf16 = jnp.bfloat16


def bits_from(n, low):
    bits = []
    while low < n:
        bits.insert(0, low)
        low *= 2
    return bits


def flip(x, bits):
    n = lax.axis_size("tok")
    return lax.ppermute(x, "tok", [(i, i ^ bits) for i in range(n)])


def side(bit):
    return (lax.axis_index("tok") // bit) % 2


def pick(x, index, axis=0):
    return lax.dynamic_index_in_dim(x, index, axis, False)


def assemble(pieces):
    out = jnp.broadcast_to(pieces[0][1][None], (len(pieces),) + pieces[0][1].shape)
    for index, block in pieces[1:]:
        out = lax.dynamic_update_index_in_dim(out, block, index, 0)
    return out


def assemble_all(pieces):
    out = jnp.zeros((len(pieces),) + pieces[0][1].shape, pieces[0][1].dtype)
    for index, block in pieces:
        out = lax.dynamic_update_index_in_dim(out, block, index, 0)
    return out


def after(x, *others):
    return lax.optimization_barrier((x,) + others)[0] if others else x


def move(x, bits, start=(), stop=()):
    return after(flip(after(x, *start), bits), *stop)


def grow(x, bit, start=(), stop=()):
    return assemble([(side(bit), x), (1 - side(bit), move(x, bit, start, stop))])


def in_order(x, bits):
    done = bits[::-1]
    axes = [done.index(b) for b in sorted(done, reverse=True)]
    x = x.transpose(axes + list(range(len(done), x.ndim)))
    return x.reshape((-1,) + x.shape[len(done) :])


def grown(bits):
    at = [0]
    for bit in bits[::-1]:
        at = [i + j for i in at for j in (0, bit)]
    return at


class Scatter:
    def __init__(self, make, bits):
        self.make, self.bits, self.bit = make, bits, bits[-1]

    def send(self, *start):
        self.sent = after(self.make(1 - side(self.bit)), *start)
        self.here = flip(self.sent, self.bit)

    def keep(self, *gate):
        self.kept = self.make(after(side(self.bit), *gate))
        return self.kept

    def hold(self, x, *gate):
        x, self.here = lax.optimization_barrier((x, after(self.here, *gate)))
        return x

    def step(self, *gate):
        kept, here = self.kept, after(self.here, *gate)
        self.bits = self.bits[:-1]
        if not self.bits:
            return (kept.astype(f32) + here.astype(f32))[0]
        bit = self.bits[-1]

        def half(index):
            return sum(pick(a.reshape((-1, 2) + a.shape[1:]), index, 1).astype(f32) for a in (kept, here))

        self.sent = half(1 - side(bit)).astype(bf16)
        self.kept = half(side(bit))
        self.here = flip(self.sent, bit)
        return self.sent

    def finish(self, *gate):
        while len(self.bits) > 1:
            self.step(*gate)
        return self.step(*gate)


def join(both):
    out = Scatter(None, both[0].bits[:-1] + [0])
    out.kept = jnp.concatenate([part.kept for part in both], axis=2)
    out.here = jnp.concatenate([part.here for part in both], axis=2)
    return out


MESH = pl.DeviceIdType.MESH
INV = pl.BlockSpec(memory_space=pltpu.VMEM)


def across(me, bits):
    for bit in (1, 2, 4, 8, 16):
        if bits & bit:
            me = me + bit - 2 * bit * ((me // bit) % 2)
    return me


def meet(me, partners):
    barrier = pltpu.get_barrier_semaphore()
    for bits in partners:
        pl.semaphore_signal(barrier, inc=1, device_id=(across(me, bits),), device_id_type=MESH)
    pl.semaphore_wait(barrier, len(partners))


class Mail:
    def __init__(self, me, sems):
        self.me, self.sems, self.count, self.open = me, sems, 0, []
    def send(self, source, target, bits):
        at = self.count
        self.count += 1
        copy = pltpu.make_async_remote_copy(src_ref=source, dst_ref=target, send_sem=self.sems.at[0, at],
            recv_sem=self.sems.at[1, at], device_id=(across(self.me, bits),), device_id_type=MESH)
        copy.start()
        self.open.append(copy)
        return copy
    def local(self, source, target):
        at = self.count
        self.count += 1
        copy = pltpu.make_async_copy(source, target, self.sems.at[0, at])
        copy.start()
        return copy
    def close(self):
        for copy in self.open:
            copy.wait_send()


def first_body(gains_in, gate_in, up_in, mine, theirs, down_in, gains, gate, up, z4, down, chip, sems):
    me = lax.axis_index("tok")
    core, z = me % 2, me // 8
    meet(me, (1, 2, 4, 8, 9, 16))
    mail = Mail(me, sems)
    size = mine.shape[0]
    swap = mail.send(theirs, chip.at[pl.ds(core * size, size)], 1)
    own = mail.local(mine, chip.at[pl.ds(core * size, size)])
    gains[pl.ds(me, 1)] = gains_in[...]

    def member(d):
        return ((d // 8) % 2) * 2 + d % 2

    place = (me // 2) % 4
    cut = down_in.shape[1] // 2
    a, b = pl.ds(0, cut), pl.ds(cut, cut)
    xa = mail.send(down_in.at[:, a], down.at[place, :, a], 2)
    yb = mail.send(down_in.at[:, b], down.at[place, :, b], 4)
    to_gate = [mail.send(gate_in.at[member(across(me, k))], gate.at[member(me)], k) for k in (9, 8, 1)]
    own.wait()
    swap.wait_recv()
    high = mail.send(chip, z4.at[z], 16)
    low = mail.send(chip, z4.at[z], 8)
    to_up = [mail.send(up_in.at[member(across(me, k))], up.at[member(me)], k) for k in (9, 8, 1)]
    ya = mail.send(down_in.at[:, a], down.at[place, :, a], 4)
    xb = mail.send(down_in.at[:, b], down.at[place, :, b], 2)
    kept = [
        mail.local(down_in, down.at[place]),
        mail.local(chip, z4.at[z]),
        mail.local(gate_in.at[member(me)], gate.at[member(me)]),
        mail.local(up_in.at[member(me)], up.at[member(me)]),
    ]
    for bit in (1, 2, 4):
        at = pl.ds((me // bit) * bit, bit)
        mail.send(gains.at[at], gains.at[at], bit).wait_recv()
    high.wait_recv()
    zh = across(me, 16) // 8
    low2 = mail.send(z4.at[zh], z4.at[zh], 8)
    across_x, across_y = across(place, 1), across(place, 2)
    xa.wait_recv()
    ya2 = mail.send(down.at[across_x, :, a], down.at[across_x, :, a], 4)
    yb.wait_recv()
    xb2 = mail.send(down.at[across_y, :, b], down.at[across_y, :, b], 2)
    for bit in (8, 16):
        at = pl.ds((me // bit) * bit, bit)
        mail.send(gains.at[at], gains.at[at], bit).wait_recv()
    for c in to_gate + to_up + [low, low2, ya, xb, ya2, xb2]:
        c.wait_recv()
    for c in kept:
        c.wait()
    mail.close()


def spread_first(gains, gate, up, mine, theirs, down):
    rows, cols = mine.shape
    return pl.pallas_call(
        first_body,
        out_shape=[
            jax.ShapeDtypeStruct((32,) + gains.shape[1:], f32),
            jax.ShapeDtypeStruct(gate.shape, bf16),
            jax.ShapeDtypeStruct(up.shape, bf16),
            jax.ShapeDtypeStruct((4, 2 * rows, cols), bf16),
            jax.ShapeDtypeStruct((4,) + down.shape, bf16),
        ],
        in_specs=[INV] * 6,
        out_specs=[INV] * 5,
        scratch_shapes=[pltpu.VMEM((2 * rows, cols), bf16), pltpu.SemaphoreType.DMA((2, 28))],
        compiler_params=pltpu.CompilerParams(collective_id=1, has_side_effects=True, vmem_limit_bytes=20 * MIB),
    )(gains, gate, up, mine, theirs, down)


def second_body(z4, out_mine, out_theirs, gate, whole, out4, gate2, chip, sems):
    me = lax.axis_index("tok")
    core, z, place = me % 2, me // 8, (me // 2) % 4
    across_y, across_x = across(place, 2), across(place, 1)
    meet(me, (1, 2, 4, 8, 16))
    mail = Mail(me, sems)
    size, cut = out_mine.shape[0], z4.shape[2] // 2
    a, b = pl.ds(0, cut), pl.ds(cut, cut)
    ya = mail.send(z4.at[:, :, a], whole.at[:, place, :, a], 4)
    xb = mail.send(z4.at[:, :, b], whole.at[:, place, :, b], 2)
    swap = mail.send(out_theirs, chip.at[pl.ds(core * size, size)], 1)
    own = mail.local(out_mine, chip.at[pl.ds(core * size, size)])
    kept = [mail.local(z4, whole.at[:, place]), mail.local(gate, gate2.at[z // 2])]
    xa = mail.send(z4.at[:, :, a], whole.at[:, place, :, a], 2)
    yb = mail.send(z4.at[:, :, b], whole.at[:, place, :, b], 4)
    own.wait()
    swap.wait_recv()
    high = mail.send(chip, out4.at[z], 16)
    low = mail.send(chip, out4.at[z], 8)
    kept.append(mail.local(chip, out4.at[z]))
    gate_high = mail.send(gate, gate2.at[z // 2], 16)
    ya.wait_recv()
    xa2 = mail.send(whole.at[:, across_y, :, a], whole.at[:, across_y, :, a], 2)
    xb.wait_recv()
    yb2 = mail.send(whole.at[:, across_x, :, b], whole.at[:, across_x, :, b], 4)
    high.wait_recv()
    zh = across(me, 16) // 8
    low2 = mail.send(out4.at[zh], out4.at[zh], 8)
    for c in (xa, yb, xa2, yb2, low, low2, gate_high):
        c.wait_recv()
    for c in kept:
        c.wait()
    mail.close()


def spread_second(z4, out_mine, out_theirs, gate):
    rows, cols = out_mine.shape
    return pl.pallas_call(
        second_body,
        out_shape=[
            jax.ShapeDtypeStruct((4, 4) + z4.shape[1:], bf16),
            jax.ShapeDtypeStruct((4, 2 * rows, cols), bf16),
            jax.ShapeDtypeStruct((2,) + gate.shape, bf16),
        ],
        in_specs=[INV] * 4,
        out_specs=[INV] * 3,
        scratch_shapes=[pltpu.VMEM((2 * rows, cols), bf16), pltpu.SemaphoreType.DMA((2, 16))],
        compiler_params=pltpu.CompilerParams(collective_id=2, has_side_effects=True, vmem_limit_bytes=20 * MIB),
    )(z4, out_mine, out_theirs, gate)


def scan_body(sign, s_ref, o_ref, stage, here, whole, zhere, back, bhere, sems):
    me = lax.axis_index("tok")
    z, plane = me // 8, (me // 2) % 4
    barrier = pltpu.get_barrier_semaphore()
    for k in (1, 2, 3):
        for to in (across(me, 2 * k), lax.rem(me + 8 * k, 32)):
            pl.semaphore_signal(barrier, inc=1, device_id=(to,), device_id_type=MESH)
    pl.semaphore_wait(barrier, 6)

    def slot(k):
        return (across(me, 2 * k) // 2) % 4

    def copy(source, target, sem, i, to):
        return pltpu.make_async_remote_copy(
            src_ref=source,
            dst_ref=target,
            send_sem=sems.at[sem, 0, i],
            recv_sem=sems.at[sem, 1, i],
            device_id=(to,),
            device_id_type=MESH,
        )

    def receives(k):
        return z - k >= 0 if sign > 0 else z + k < 4

    def sends(k):
        return z + k < 4 if sign > 0 else z - k >= 0

    copies = []
    for k in (3, 1, 2):
        stage[k - 1] = s_ref[pl.ds(2 * slot(k), 2)].astype(stage.dtype)
        copies.append(copy(stage.at[k - 1], here.at[k - 1], 0, k - 1, across(me, 2 * k)))
        copies[-1].start()
    mine = [s_ref[pl.ds(2 * plane, 2)]]
    for c in copies:
        c.wait()
    mine += [here[k - 1].astype(f32) for k in (1, 2, 3)]
    whole[...] = sum(mine).astype(whole.dtype)
    for k in (2, 1, 3):

        @pl.when(sends(k))
        def _(k=k):
            copy(whole, zhere.at[k - 1], 1, k - 1, me + 8 * k * sign).start()

    for k in (1, 2, 3):

        @pl.when(receives(k))
        def _(k=k):
            copy(whole, zhere.at[k - 1], 1, k - 1, me).wait_recv()

        @pl.when(jnp.logical_not(receives(k)))
        def _(k=k):
            zhere[k - 1] = jnp.zeros_like(whole)

    for k in (1, 2, 3):

        @pl.when(sends(k))
        def _(k=k):
            copy(whole, zhere.at[k - 1], 1, k - 1, me).wait_send()

    beyond = sum(zhere[k].astype(f32) for k in range(3))
    copies = []
    for k in (3, 1, 2, 0):
        before = beyond
        for j in range(4):
            if j != k:
                before = before + (sign * (slot(k) - slot(j)) > 0).astype(f32) * mine[j]
        if k == 0:
            o_ref[pl.ds(2 * plane, 2)] = before
        else:
            back[k - 1] = before.astype(back.dtype)
            copies.append(copy(back.at[k - 1], bhere.at[k - 1], 2, k - 1, across(me, 2 * k)))
            copies[-1].start()
    for c in copies:
        c.wait()
    for k in (1, 2, 3):
        o_ref[pl.ds(2 * slot(k), 2)] = bhere[k - 1].astype(f32)


def spans_of(cols, most=512):
    return [(s, min(most, cols - s)) for s in range(0, cols, most)]


def ffn_body(order, sides, x_ref, g_ref, *refs):
    gates, ups, downs = refs[0:4], refs[4:8], refs[8:11]
    y_ref, act_ref, d_ref, dh_ref, w_gate_up, w_down, sem = refs[11:]
    cols = w_down.shape[0]

    @pl.when(pl.program_id(0) == 0)
    def _():
        size, part, rest = downs[0].shape[0], downs[1].shape[1], downs[2].shape[1]
        far = pl.ds(pl.multiple_of((1 - sides[4]) * size, 16), size)
        targets = [
            w_down.at[pl.ds(pl.multiple_of(sides[4] * size, 16), size)],
            w_down.at[far, pl.ds(0, part)],
            w_down.at[far, pl.ds(part, rest)],
        ]
        copies = [pltpu.make_async_copy(a, b, sem.at[i]) for i, (a, b) in enumerate(zip(downs, targets))]
        size = gates[0].shape[1]
        for j, pieces in enumerate((gates, ups)):
            for k, piece in enumerate(pieces):
                for i, at in enumerate(order):
                    rows = pl.ds(pl.multiple_of((at + sides[k]) * size, 16), size)
                    target = w_gate_up.at[rows, pl.ds(j * cols, cols)]
                    copies.append(pltpu.make_async_copy(piece.at[i], target, sem.at[len(copies)]))
        for copy in copies:
            copy.start()
        for copy in copies:
            copy.wait()

    x, g = x_ref[...], g_ref[...]
    for s, w in spans_of(cols):
        gate, upper = dot(x, w_gate_up[:, s : s + w]), dot(x, w_gate_up[:, cols + s : cols + s + w])
        d_act = dot_cols(g, w_down[s : s + w, :])
        sigma = jax.nn.sigmoid(gate)
        smooth = gate * sigma
        act_ref[:, s : s + w] = (smooth * upper).astype(bf16)
        d_ref[:, s : s + w] = (d_act * upper * sigma * (1.0 + gate * (1.0 - sigma))).astype(bf16)
        d_ref[:, cols + s : cols + s + w] = (d_act * smooth).astype(bf16)
    y_ref[...] = dot(act_ref[...], w_down[...]).astype(bf16)
    dh_ref[...] = dot_cols(d_ref[...], w_gate_up[...]).astype(bf16)


def ffn(x, g, gate, up, down, order, sides, tile=256):
    tokens, width = x.shape
    cols = 2 * down[0].shape[0]

    def block(w):
        return pl.BlockSpec((tile, w), lambda i: (i, 0))

    return pl.pallas_call(
        lambda *refs: ffn_body(order, *refs),
        out_shape=[jax.ShapeDtypeStruct((tokens, w), bf16) for w in (width, cols, 2 * cols, width)],
        grid=(tokens // tile,),
        in_specs=[pl.BlockSpec(memory_space=pltpu.SMEM), block(width), block(width)] + [pl.BlockSpec(memory_space=pl.ANY)] * 11,
        out_specs=[block(width), block(cols), block(2 * cols), block(width)],
        scratch_shapes=[
            pltpu.VMEM((width, 2 * cols), bf16),
            pltpu.VMEM((cols, width), bf16),
            pltpu.SemaphoreType.DMA((8 * len(order) + 3,)),
        ],
        compiler_params=pltpu.CompilerParams(vmem_limit_bytes=48 * MIB),
        cost_estimate=pl.CostEstimate(flops=0, bytes_accessed=0, transcendentals=0),
    )(sides, x, g, *gate, *up, *down)


def product_body(count, group, index, *refs):
    left, right, out = refs[: count * group], refs[count * group : -1], refs[-1]
    acc = 0.0
    for i in range(count):
        rows = jnp.concatenate([a[...] for a in left[i * group : (i + 1) * group]], axis=1)
        acc = acc + dot_rows(rows, right[i][...])
    out[...] = acc.astype(out.dtype)


def row_blocks(left, right, index, size, half=None):
    count = index.shape[0]
    group = 4 if count % 4 == 0 else 1
    cols = right[0].shape[1] // (1 if half is None else 2)
    at_col = half or 0

    def block(tokens, j):
        return pl.BlockSpec((tokens, size), lambda i, at: (0, at[i * group + j]))

    return pl.pallas_call(
        lambda *refs: product_body(len(left), group, *refs),
        out_shape=jax.ShapeDtypeStruct((count * size, cols), bf16),
        grid_spec=pltpu.PrefetchScalarGridSpec(
            num_scalar_prefetch=1,
            grid=(count // group,),
            in_specs=[block(a.shape[0], j) for a in left for j in range(group)]
            + [pl.BlockSpec((b.shape[0], cols), lambda i, at: (0, at_col)) for b in right],
            out_specs=pl.BlockSpec((group * size, cols), lambda i, at: (i, 0)),
        ),
        compiler_params=pltpu.CompilerParams(vmem_limit_bytes=56 * MIB),
        cost_estimate=pl.CostEstimate(flops=0, bytes_accessed=0, transcendentals=0),
    )(index.astype(jnp.int32), *[a for a in left for _ in range(group)], *right)


def wide_body(d_ref, w_ref, out_ref):
    out_ref[...] = dot_cols(d_ref[...], w_ref[...]).astype(bf16)


def times_transposed(d, w, tile=256):
    return pl.pallas_call(
        wide_body,
        out_shape=jax.ShapeDtypeStruct((d.shape[0], w.shape[0]), bf16),
        grid=(d.shape[0] // tile,),
        in_specs=[
            pl.BlockSpec((tile, d.shape[1]), lambda i: (i, 0)),
            pl.BlockSpec(w.shape, lambda i: (0, 0)),
        ],
        out_specs=pl.BlockSpec((tile, w.shape[0]), lambda i: (i, 0)),
        compiler_params=pltpu.CompilerParams(vmem_limit_bytes=48 * MIB),
        cost_estimate=pl.CostEstimate(flops=0, bytes_accessed=0, transcendentals=0),
    )(d, w)


def part_maker(left, right, bits, within=(0,), half=None):
    n = lax.axis_size("tok")
    size = left[0].shape[1] * 2 // n
    cols = right[0].shape[1] // (1 if half is None else 2)
    ids = np.asarray([(at + more) // 2 for at in grown(bits[:-1][::-1]) for more in within], np.int32)

    def make(index):
        index = jnp.asarray(ids) + index * (bits[-1] // 2)
        if size % 128 == 0:
            out = row_blocks(left, right, index, size, half)
        else:
            out = sum(dot_rows(a, b) for a, b in zip(left, right)).astype(bf16).reshape(n // 2, size, -1)
            out = out[index][..., (half or 0) * cols : (half or 0) * cols + cols]
        return out.reshape(-1, size * len(within), cols)

    return make


def feature_tables(heads):
    pairs = [(a, b) for a in range(QK + 1) for b in range(a, QK + 1)]
    one = np.zeros((heads, heads * QK, FEATS), np.float32)
    two = np.zeros((heads, heads * QK, FEATS), np.float32)
    rows = np.zeros((8, FEATS), np.float32)
    for f, (a, b) in enumerate(pairs):
        for h in range(heads):
            if a < QK:
                one[h, h * QK + a, f] = 1
            if b < QK:
                two[h, h * QK + b, f] = 1
        rows[0, f] = a == QK
        rows[1, f] = b == QK
        if a == QK:
            rows[2, f] = 1.0
        elif b == QK:
            rows[2, f] = QK**-0.5
        else:
            rows[2, f] = (0.5 if a == b else 1.0) / QK
    return jnp.asarray(one, bf16), jnp.asarray(two, bf16), jnp.asarray(rows)


def dot(a, b):
    return lax.dot_general(a, b, (((1,), (0,)), ((), ())), preferred_element_type=f32)


def dot_rows(a, b):
    return lax.dot_general(a, b, (((0,), (0,)), ((), ())), preferred_element_type=f32)


def dot_cols(a, b):
    return lax.dot_general(a, b, (((1,), (1,)), ((), ())), preferred_element_type=f32)


def halves(x):
    high = x.astype(bf16)
    return high, (x - high.astype(f32)).astype(bf16)


def features(x, one, two, rows):
    return dot(x, one) + rows[0:1], dot(x, two) + rows[1:2]


def total_row(state):
    return jnp.concatenate([state[FEATS : FEATS + 1], state[FEATS + 1 : FEATS + 2, : FEATS - 128]], axis=1)


def store_state(ref, state, row):
    ref[0, 0, :FEATS, :] = state
    ref[0, 0, FEATS:, :] = jnp.zeros((ROWS - FEATS, state.shape[1]), f32)
    ref[0, 0, FEATS : FEATS + 1, :] = row[:, :128]
    ref[0, 0, FEATS + 1 : FEATS + 2, : FEATS - 128] = row[:, 128:]


def kept_rows(scal, tile, tokens):
    index = lax.broadcasted_iota(jnp.int32, (tokens, 1), 0) + tile * tokens
    return index >= scal[tile]


def state_body(scal, k_ref, v_ref, one, two, rows, out_ref):
    tile = pl.program_id(0)
    a, b = features(k_ref[...], one[0], two[0], rows)
    phi = jnp.where(kept_rows(scal, tile, a.shape[0]), a * b, 0.0)
    high, low = halves(phi)
    v = v_ref[...]
    store_state(out_ref, dot_rows(high, v) + dot_rows(low, v), jnp.sum(phi, axis=0, keepdims=True))


def weights(q_ref, k_ref, lo_ref, tile, head):
    tokens, lanes = q_ref.shape
    lane = lax.broadcasted_iota(jnp.int32, (tokens, lanes), 1) // QK == head
    q = jnp.where(lane, q_ref[...], jnp.zeros((), bf16))
    score = dot_cols(q, k_ref[...]) * QK**-0.5
    row = lax.broadcasted_iota(jnp.int32, score.shape, 0)
    col = lax.broadcasted_iota(jnp.int32, score.shape, 1)
    lo = lo_ref[...] - tile * tokens
    mask = (col <= row) & (col >= lo)
    weight = jnp.where(mask, 1.0 + score + 0.5 * score * score, 0.0)
    return lane, score, mask, weight, lo < 0


def forward_body(q_ref, k_ref, v_ref, lo_ref, carry_ref, one, two, rows, y_ref, mixed_ref):
    tile, head = pl.program_id(0), pl.program_id(1)
    _, _, _, weight, alive = weights(q_ref, k_ref, lo_ref, tile, head)
    a, b = features(q_ref[...], one[0], two[0], rows)
    phi = jnp.where(alive, a * b * rows[2:3], 0.0)
    high, low = halves(phi)
    carry = carry_ref[0, 0]
    s_high, s_low = halves(carry[:FEATS])
    numer = dot(weight.astype(bf16), v_ref[...])
    numer = numer + (dot(high, s_high) + dot(high, s_low) + dot(low, s_high))
    denom = jnp.sum(weight, axis=1, keepdims=True) + jnp.sum(phi * total_row(carry), axis=1, keepdims=True)
    y = numer / denom
    y_ref[...] = y
    mixed_ref[...] = y.astype(bf16)


def spread(t, a, b, one, two):
    first_high, first_low = halves(t * b)
    second_high, second_low = halves(t * a)
    return (
        dot_cols(first_high, one) + dot_cols(first_low, one) + dot_cols(second_high, two) + dot_cols(second_low, two)
    )


def backward_body(
    q_ref, k_ref, v_ref, lo_ref, carry_ref, one, two, rows, y_ref, d_ref, dq_ref, dk_ref, dv_ref, ds_ref, dq_acc, dk_acc
):
    tile, head = pl.program_id(0), pl.program_id(1)
    lane, score, mask, weight, alive = weights(q_ref, k_ref, lo_ref, tile, head)
    a, b = features(q_ref[...], one[0], two[0], rows)
    phi = jnp.where(alive, a * b * rows[2:3], 0.0)
    high, low = halves(phi)
    carry = carry_ref[0, 0]
    s_high, s_low = halves(carry[:FEATS])
    row = total_row(carry)
    denom = jnp.sum(weight, axis=1, keepdims=True) + jnp.sum(phi * row, axis=1, keepdims=True)
    d = d_ref[...].astype(f32)
    g = d / denom
    c = -jnp.sum(d * y_ref[...], axis=1, keepdims=True) / denom
    g_high, g_low = halves(g)
    v = v_ref[...]
    dk = dot_cols(g_high, v) + dot_cols(g_low, v) + c
    ds = jnp.where(mask, dk * (1.0 + score) * QK**-0.5, 0.0).astype(bf16)
    dv_ref[...] = dot_rows(weight.astype(bf16), g_high)
    dphi = dot_cols(g_high, s_high) + dot_cols(g_high, s_low) + dot_cols(g_low, s_high) + c * row
    t = jnp.where(alive, dphi * rows[2:3], 0.0)
    dq = jnp.where(lane, dot(ds, k_ref[...]), 0.0) + spread(t, a, b, one[0], two[0])
    dkeys = jnp.where(lane, dot_rows(ds, q_ref[...]), 0.0)

    @pl.when(head == 0)
    def _():
        dq_acc[...] = dq
        dk_acc[...] = dkeys

    @pl.when(head > 0)
    def _():
        dq_acc[...] += dq
        dk_acc[...] += dkeys

    @pl.when(head == pl.num_programs(1) - 1)
    def _():
        dq_ref[...] = dq_acc[...].astype(bf16)
        dk_ref[...] = dk_acc[...]

    state = dot_rows(high, g_high) + dot_rows(high, g_low) + dot_rows(low, g_high)
    store_state(ds_ref, state, jnp.sum(phi * c, axis=0, keepdims=True))


def carried_body(scal, k_ref, v_ref, one, two, rows, grad_ref, dk_in, dv_in, dk_ref, dv_ref, acc):
    tile, head = pl.program_id(0), pl.program_id(1)
    a, b = features(k_ref[...], one[0], two[0], rows)
    keep = kept_rows(scal, tile, a.shape[0])
    high, low = halves(jnp.where(keep, a * b, 0.0))
    grad = grad_ref[0, 0]
    g_high, g_low = halves(grad[:FEATS])
    v = v_ref[...]
    dv = dv_in[...] + dot(high, g_high) + dot(high, g_low) + dot(low, g_high)
    dv_ref[...] = dv.astype(bf16)
    t = jnp.where(keep, dot_cols(v, g_high) + dot_cols(v, g_low) + total_row(grad), 0.0)
    dk = spread(t, a, b, one[0], two[0])

    @pl.when(head == 0)
    def _():
        acc[...] = dk_in[...] + dk

    @pl.when(head > 0)
    def _():
        acc[...] += dk

    @pl.when(head == pl.num_programs(1) - 1)
    def _():
        dk_ref[...] = acc[...].astype(bf16)


class Attention:
    def __init__(self, qkv, lo, heads, tokens):
        self.qkv, self.heads, self.tokens = qkv, heads, tokens
        self.lo = lo[:, None]
        self.scal = jnp.stack([lo[tokens - 1], lo[2 * tokens - 1]])
        self.tables = feature_tables(heads)
        lanes = heads * QK
        self.value = (qkv.shape[1] - 2 * lanes) // heads
        skip = 2 * lanes // self.value
        self.q = pl.BlockSpec((tokens, lanes), lambda t, h: (t, 0))
        self.k = pl.BlockSpec((tokens, lanes), lambda t, h: (t, 1))
        self.v = pl.BlockSpec((tokens, self.value), lambda t, h: (t, h + skip))
        self.o = pl.BlockSpec((tokens, self.value), lambda t, h: (t, h))
        self.l = pl.BlockSpec((tokens, 1), lambda t, h: (t, 0))
        self.s = pl.BlockSpec((1, 1, ROWS, self.value), lambda t, h: (h, t, 0, 0))
        self.e = pl.BlockSpec((1, lanes, FEATS), lambda t, h: (h, 0, 0))
        self.r = pl.BlockSpec((8, FEATS), lambda t, h: (0, 0))
        self.m = pl.BlockSpec(memory_space=pltpu.SMEM)
        self.table_specs = [self.e, self.e, self.r]
        self.acc = pltpu.VMEM((tokens, lanes), f32)
        self.state_shape = jax.ShapeDtypeStruct((heads, 2, ROWS, self.value), f32)

    def wide(self, kind):
        return jax.ShapeDtypeStruct((2 * self.tokens, self.heads * self.value), kind)

    def narrow(self, kind):
        return jax.ShapeDtypeStruct((2 * self.tokens, self.heads * QK), kind)

    def call(self, body, ins, outs, shapes, scratch, limit, args):
        return pl.pallas_call(
            body,
            grid=(2, self.heads),
            in_specs=ins,
            out_specs=outs,
            out_shape=shapes,
            scratch_shapes=scratch,
            compiler_params=pltpu.CompilerParams(vmem_limit_bytes=limit * MIB),
            cost_estimate=pl.CostEstimate(flops=0, bytes_accessed=0, transcendentals=0),
        )(*args)

    def states(self):
        (out,) = self.call(
            state_body,
            [self.m, self.k, self.v] + self.table_specs,
            [self.s],
            [self.state_shape],
            [],
            24,
            (self.scal, self.qkv, self.qkv, *self.tables),
        )
        return out

    def forward(self, carry):
        return self.call(
            forward_body,
            [self.q, self.k, self.v, self.l, self.s] + self.table_specs,
            [self.o, self.o],
            [self.wide(f32), self.wide(bf16)],
            [],
            48,
            (self.qkv, self.qkv, self.qkv, self.lo, carry, *self.tables),
        )

    def backward(self, carry, y, d_heads):
        return self.call(
            backward_body,
            [self.q, self.k, self.v, self.l, self.s] + self.table_specs + [self.o, self.o],
            [self.q, self.q, self.o, self.s],
            [self.narrow(bf16), self.narrow(f32), self.wide(f32), self.state_shape],
            [self.acc, self.acc],
            48,
            (self.qkv, self.qkv, self.qkv, self.lo, carry, *self.tables, y, d_heads),
        )

    def carried(self, grad, dk, dv):
        return self.call(
            carried_body,
            [self.m, self.k, self.v] + self.table_specs + [self.s, self.q, self.o],
            [self.q, self.o],
            [self.narrow(bf16), self.wide(bf16)],
            [self.acc],
            48,
            (self.scal, self.qkv, self.qkv, *self.tables, grad, dk, dv),
        )


def others(state, earlier, kind):
    n = lax.axis_size("tok")
    me = lax.axis_index("tok")
    sign = 1 if earlier else -1
    if n != 32:
        parts = lax.all_gather(state.astype(kind), "tok").astype(f32)
        index = jnp.arange(n)
        before = (sign * (me // 2 - index // 2) > 0) & (index % 2 == me % 2)
        out = jnp.sum(jnp.where(before.reshape((n,) + (1,) * state.ndim), parts, 0.0), axis=0)
        return out
    block = (state.shape[0] // 4,) + state.shape[1:]
    slots = pltpu.VMEM((3,) + block, kind)
    return pl.pallas_call(
        lambda *refs: scan_body(sign, *refs),
        out_shape=jax.ShapeDtypeStruct(state.shape, f32),
        in_specs=[INV],
        out_specs=INV,
        scratch_shapes=[slots, slots, pltpu.VMEM(block, kind), slots, slots, slots, pltpu.SemaphoreType.DMA((3, 2, 3))],
        compiler_params=pltpu.CompilerParams(
            collective_id=3 if earlier else 4, has_side_effects=True, vmem_limit_bytes=16 * MIB
        ),
        cost_estimate=pl.CostEstimate(flops=0, bytes_accessed=0, transcendentals=0),
    )(state)


def row_starts(positions, lengths, offsets):
    inside = (positions[:, None] >= offsets[None, :]) & (positions[:, None] < offsets[None, :] + lengths[None, :])
    return jnp.sum(jnp.where(inside, offsets[None, :], 0), axis=1)


def side_by_side(core, mine, theirs, axis=0):
    size = mine.shape[axis]
    shape = list(mine.shape)
    shape[axis] *= 2
    out = jnp.zeros(shape, mine.dtype)
    out = lax.dynamic_update_slice_in_dim(out, mine, core * size, axis)
    return lax.dynamic_update_slice_in_dim(out, theirs, (1 - core) * size, axis)


def shards(
    block_input,
    lengths,
    offsets,
    norm1_gain,
    w_query,
    w_key,
    w_value,
    w_out,
    norm2_gain,
    w_gate,
    w_up,
    w_down,
    out_grad,
):
    n = lax.axis_size("tok")
    me = lax.axis_index("tok")
    core, member = me % 2, side(PAIR) * 2 + me % 2
    cbits = bits_from(n, 2)
    qbits = [bit for bit in cbits if bit != PAIR]
    swapped = qbits[:-2] + [qbits[-1], qbits[-2]]
    chips, quads = n // 2, n // 4
    above, below = n // (2 * PAIR), PAIR // 2
    groups = [
        [i * 2 * PAIR + p * PAIR + j * 2 + c for i in range(above) for j in range(below)] for p in (0, 1) for c in (0, 1)
    ]
    to_member = {1: 1, 2: PAIR, 3: PAIR + 1}
    tokens, width = block_input.shape
    rows = w_query.shape[0]
    heads = w_query.shape[1] // QK // 2
    half = width // 2
    lanes = heads * QK
    def column_half(w, which):
        return lax.dynamic_slice_in_dim(w, which * (w.shape[1] // 2), w.shape[1] // 2, 1)

    def row_half(w, which):
        return lax.dynamic_slice_in_dim(w, which * (w.shape[0] // 2), w.shape[0] // 2, 0)

    unit = w_down.shape[0]
    padded = -(-unit // 16) * 16
    cols = quads * padded

    def by_quad(w):
        w = w.reshape(rows, above, 2, below, 2, unit)
        w = jnp.pad(w, ((0, 0),) * 5 + ((0, padded - unit),))
        return w.transpose(2, 4, 0, 1, 3, 5).reshape(4, rows, cols)

    gate, up = by_quad(w_gate), by_quad(w_up)
    down = jnp.pad(w_down, ((0, padded - unit), (0, 0)))
    near_grad = flip(out_grad, 1)

    def by_core(which):
        return jnp.concatenate([column_half(w, which) for w in (w_query, w_key, w_value)], axis=1)

    gains = jnp.stack([norm1_gain, norm2_gain]).astype(f32)
    if n == 32:
        gains = jnp.pad(gains, ((0, 6), (0, 128 - rows)))[None]
        gains = after(gains, near_grad)
        gains, gate, up, qkv_all, down = spread_first(gains, gate, up, by_core(core), by_core(1 - core), down)
        gains = gains[:, :2, :rows].transpose(1, 0, 2).reshape(2, 1, width)
        z4 = qkv_all
        qkv_all, out_half, gate = spread_second(z4, column_half(w_out, core), column_half(w_out, 1 - core), gate)
        qkv_all = qkv_all.reshape(width, -1)
    else:

        def to_group(x):
            pieces = [(member, pick(x, member))]
            for k in range(1, 4):
                pieces.append((member ^ k, flip(pick(x, member ^ k), to_member[k])))
            return assemble_all(pieces)

        gate, up = to_group(gate), to_group(up)
        qkv_all = side_by_side(core, by_core(core), flip(by_core(1 - core), 1))
        gains = grow(gains, 1)
        for bit in cbits:
            gains, qkv_all = grow(gains, bit), grow(qkv_all, bit)
        gains = in_order(gains, [1] + cbits).transpose(1, 0, 2).reshape(2, 1, width)
        qkv_all = in_order(qkv_all, cbits).reshape(width, -1)
        out_half = side_by_side(core, column_half(w_out, core), flip(column_half(w_out, 1 - core), 1))
        for bit in cbits[:-2]:
            out_half = grow(out_half, bit)
        out_half = in_order(out_half, cbits[:-2])
        gate = grow(gate, qbits[0])
        for bit in qbits[1:]:
            down = grow(down, bit)
        down = in_order(down, qbits[1:])
    gain_one, gain_two = gains[0], gains[1]

    inputs32 = block_input.astype(f32)
    ratio_one = lax.rsqrt(jnp.mean(inputs32 * inputs32, axis=1, keepdims=True) + eps)
    normed_one = inputs32 * ratio_one
    hidden_one = (normed_one * gain_one).astype(bf16)
    hidden_chip = side_by_side(core, hidden_one, move(hidden_one, 1, (), (qkv_all,)))
    qkv = dot(hidden_chip, qkv_all).astype(bf16)

    first = (me // 2) * 2 * tokens
    positions = first + jnp.arange(2 * tokens, dtype=jnp.int32)
    lo = row_starts(positions, lengths, offsets) - first
    attention = Attention(qkv, lo, heads, tokens)
    states = attention.states()
    fresh0 = (lo[tokens - 1] >= 0).astype(f32)
    fresh1 = (lo[2 * tokens - 1] >= tokens).astype(f32)

    start, stop = (qkv_all,), (states,)
    for bit in qbits[1:-2]:
        gate = grow(gate, bit)
    gate_x = move(gate, 2, start, stop)
    up = grow(up, qbits[0], start, stop)
    for bit in qbits[1:-2]:
        up = grow(up, bit)
    out_y = move(out_half, 4, start, stop)
    leaving = states[:, 1] + (1.0 - fresh1) * states[:, 0]
    leaving, gate_x, up, out_y = lax.optimization_barrier((leaving, gate_x, up, out_y))
    entering = others(leaving, True, f32)
    start, stop = (leaving,), (entering,)
    down = down.reshape(cols // 2, width)
    down_a, down_b = down[:, : width * 3 // 4], down[:, width * 3 // 4 :]
    out_both = jnp.stack([out_half, out_y])
    gate_up = jnp.concatenate([gate, up], axis=-1)
    flows = [(out_both, 2), (gate_up, 4), (up, 2), (down_a, qbits[0]), (out_grad, PAIR)]
    flows = [move(w, bit, start, stop) for w, bit in flows]
    entering, out_x, gate_up, up_x, down_a, far_grad = lax.optimization_barrier((entering, *flows))
    gate_y, up_y = gate_up[..., :cols], gate_up[..., cols:]
    carry = jnp.stack([entering, states[:, 0] + (1.0 - fresh0) * entering], axis=1)
    place = (me // 2) % 4
    out_pieces = [(place, out_half), (place ^ 1, out_x[0]), (place ^ 2, out_y), (place ^ 3, out_x[1])]
    out_half = jnp.zeros((chips // 4, 4, 2 * rows, half), bf16)
    for index, piece in out_pieces:
        out_half = lax.dynamic_update_index_in_dim(out_half, piece, index, 1)
    out_half = out_half.reshape(width, half)
    carry = after(carry, out_half)
    y_heads, mixed_heads = attention.forward(carry)
    start, stop = (carry,), (mixed_heads,)
    flows = [move(w, bit, start, stop) for w, bit in [(gate_x, 4), (up_y, 2), (down_b, qbits[0])]]
    out_there = move(out_half, 1, start, stop)
    mixed_heads, out_there, *flows = lax.optimization_barrier((mixed_heads, out_there, *flows))
    gate_xy, up_xy, down_b = flows
    down = [down, down_a, down_b]
    near_grad = jnp.concatenate([out_grad, near_grad])
    out_all = side_by_side(core, out_half, out_there, 1)
    mixed_chip = side_by_side(core, mixed_heads, flip(mixed_heads, 1), 1)
    middle = inputs32 + dot(row_half(mixed_chip, core), out_all)
    ratio_two = lax.rsqrt(jnp.mean(middle * middle, axis=1, keepdims=True) + eps)
    normed_two = middle * ratio_two
    hidden_two = (normed_two * gain_two).astype(bf16)

    far_hidden = flip(hidden_two, PAIR)
    near_hidden = jnp.concatenate([hidden_two, flip(hidden_two, 1)])
    gate = [w.reshape(-1, 2 * rows, cols) for w in (gate, gate_x, gate_y, gate_xy)]
    up = [w.reshape(-1, 2 * rows, cols) for w in (up, up_x, up_y, up_xy)]
    order = [(at + more) // 2 for at in grown(qbits[:-2]) for more in (0, PAIR)]
    sides = jnp.stack([place, place ^ 1, place ^ 2, place ^ 3, side(qbits[0])])
    near = ffn(near_hidden, near_grad, gate, up, down, order, sides)
    far_hidden, far_there = after(far_hidden, *near), move(far_grad, 1, (near_hidden,), (near[0],))
    far_grad = jnp.concatenate([far_grad, far_there])
    far_hidden = jnp.concatenate([far_hidden, flip(far_hidden, 1)])
    far = ffn(far_hidden, far_grad, gate, up, down, order, sides)
    start, stop = (near[0], far_hidden), (far[0],)
    near_parts = [move(near[i][tokens:], 1, start, stop) for i in (3, 0)]
    far, near_parts = lax.optimization_barrier((far, near_parts))

    right = [near[2], far[2]]
    sum_gate = Scatter(part_maker([near_hidden, far_hidden], right, qbits, (0, PAIR), 0), qbits)
    sum_gate.send()
    start, stop = (far[0],), (sum_gate.sent,)
    far_parts = [move(far[i][tokens:], 1, start, stop) for i in (3, 0)]
    sent, far_parts = lax.optimization_barrier((sum_gate.sent, far_parts))
    d_far = (far[3][:tokens].astype(f32) + far_parts[0].astype(f32)).astype(bf16)
    y_far = (far[0][:tokens].astype(f32) + far_parts[1].astype(f32)).astype(bf16)
    sum_up = Scatter(part_maker([after(near_hidden, sent, d_far, y_far), far_hidden], right, swapped, (0, PAIR), 1), swapped)
    sum_up.send()
    sum_gate.keep(sum_up.sent)
    sum_up.keep(sum_gate.kept)
    term = row_blocks([near[1], far[1]], [after(near_grad, sum_up.kept), far_grad], jnp.arange(cols // 128), 128)
    d_far = move(d_far, PAIR, (), (term,))
    d_far = sum_gate.hold(d_far, term)
    near_parts = after(near_parts, d_far)
    d_near = near[3][:tokens].astype(f32) + near_parts[0].astype(f32)
    y_near = near[0][:tokens].astype(f32) + near_parts[1].astype(f32)
    d_hidden_two = d_near + d_far.astype(f32)
    term_norm_two = jnp.sum(d_hidden_two * normed_two, axis=0)
    scaled_two = d_hidden_two * gain_two
    d_middle = out_grad.astype(f32) + ratio_two * (
        scaled_two - normed_two * jnp.mean(scaled_two * normed_two, axis=1, keepdims=True)
    )
    d_mixed = d_middle.astype(bf16)
    d_mixed_chip = side_by_side(core, d_mixed, flip(d_mixed, 1))
    d_heads = dot_cols(d_mixed_chip, row_half(out_all, core)).astype(bf16)

    d_heads = sum_up.hold(d_heads, d_mixed)
    d_heads = after(d_heads, sum_gate.step(), sum_up.step())
    dq, dk, dv, d_states = attention.backward(carry, y_heads, d_heads)
    flows = (sum_gate.here, sum_up.here, move(y_far, PAIR, (d_heads,)))
    flows = [after(flow, d_states) for flow in flows]
    d_states, sum_gate.here, sum_up.here, y_far = lax.optimization_barrier((d_states, *flows))
    sum_both = join([sum_gate, sum_up])
    sent = [sum_both.step()]

    def down_x(index):
        return pick(term.reshape(quads // 2, 2, padded, width)[..., :half], index, 1)

    def down_y(index):
        return pick(term.reshape(quads // 4, 2, 2, padded, width)[..., half:], index, 1).reshape(-1, padded, half)

    sum_down = [Scatter(down_x, qbits), Scatter(down_y, swapped)]
    for part in sum_down:
        part.send(d_states)
        part.keep()
    sent += [part.sent for part in sum_down]
    d_mixed_half = column_half(d_mixed_chip, core)
    out_sums = []
    for h, bits in ((0, cbits), (1, cbits[:-2] + [cbits[-1], cbits[-2]])):
        out_sums.append(Scatter(part_maker([after(mixed_chip, *sent)], [d_mixed_half], bits, (0,), h), bits))
        out_sums[-1].send()
    leaving = d_states[:, 0] + (1.0 - fresh0) * d_states[:, 1]
    leaving = others(after(leaving, *(part.sent for part in out_sums)), False, bf16)
    for part in out_sums:
        leaving = after(leaving, part.keep(leaving))
    for part in [sum_both] + sum_down + out_sums:
        leaving = part.hold(leaving, leaving)
    leaving = after(leaving, *(part.step() for part in sum_down + out_sums))
    d_states = jnp.stack([d_states[:, 1] + (1.0 - fresh1) * leaving, leaving], axis=1)
    dk, dv = attention.carried(d_states, dk, dv)
    for part in out_sums + sum_down:
        dk = part.hold(dk, dk)
    sum_down = join(sum_down)
    dk = after(dk, sum_down.step())
    d_qkv = jnp.concatenate([dq, dk, dv], axis=1)

    cut = d_qkv.shape[1] // 2
    sums = []
    for h, bits in ((0, cbits), (1, cbits[:-2] + [cbits[-1], cbits[-2]])):
        sums.append(Scatter(part_maker([after(hidden_chip, *(p.sent for p in sums))], [d_qkv], bits, (0,), h), bits))
        sums[-1].send()
    start = tuple(part.sent for part in sums)
    for part in sums:
        part.keep(*start)
        start = (part.kept,)
    d_hidden_one = times_transposed(after(d_qkv, *start), qkv_all)
    rest_out = join(out_sums)
    for part in [sum_down] + sums:
        d_hidden_one = part.hold(d_hidden_one, d_hidden_one)
    sent = [part.step() for part in sums] + [rest_out.step()]
    d_hidden_one = after(d_hidden_one, *sent)
    theirs = flip(row_half(d_hidden_one, 1 - core), 1)
    gate_sum = after(sum_both.finish(), *sent).reshape(4, rows, 2, cols).transpose(0, 2, 1, 3)
    parts = [flip(pick(gate_sum, member ^ k).astype(bf16), to_member[k]) for k in range(1, 4)]
    d_hidden_one = row_half(d_hidden_one, core).astype(f32) + theirs.astype(f32)
    term_norm_one = jnp.sum(d_hidden_one * normed_one, axis=0)
    scaled_one = d_hidden_one * gain_one
    mean_one = jnp.mean(scaled_one * normed_one, axis=1, keepdims=True)
    norms = jnp.stack([term_norm_one, term_norm_two])
    for part in sums + [rest_out]:
        norms = part.hold(norms, theirs)
    rest = join(sums)
    sent = [rest.step()] + [rest_out.step() for _ in rest_out.bits[1:]]
    norms = after(norms, *sent)
    norms = norms + flip(norms, 1)
    norms = norms + flip(norms, cbits[-1])
    norms = norms + flip(norms, cbits[-2])
    norms = norms + flip(norms, cbits[-3])
    norms = rest.hold(norms, norms)
    norms, parts = lax.optimization_barrier((norms, parts))
    while len(rest.bits) > 1:
        sent = [rest.step()]
    norms = after(norms, *sent)
    gate_sum = assemble_all([(member, pick(gate_sum, member))] + [(member ^ k, p.astype(f32)) for k, p in enumerate(parts, 1)])
    gate_sum = after(gate_sum, *sent).reshape(2, 2, 2, rows, above, below, padded)[..., :unit]
    gate_sum = gate_sum.transpose(2, 3, 4, 0, 5, 1, 6).reshape(2, rows, n * unit)
    grad_gate, grad_up = gate_sum[0], gate_sum[1]
    for bit in cbits[:-3]:
        norms = norms + flip(norms, bit)
    norms = pick(norms.reshape(2, n, rows), me, 1)
    input_grad = d_middle + ratio_one * (after(scaled_one, *sent) - normed_one * mean_one)
    output = (after(middle, *sent) + y_near + y_far.astype(f32)).astype(bf16)
    grad_down = sum_down.finish()[:unit]
    rest.kept = jnp.concatenate([rest.kept, rest_out.kept], axis=2)
    rest.here = jnp.concatenate([rest.here, rest_out.here], axis=2)
    total = rest.step()
    mine, theirs = row_half(total, core), flip(row_half(total, 1 - core), 1)
    spans = [(0, lanes), (lanes, 2 * lanes), (2 * lanes, 2 * lanes + half), (2 * cut, 2 * cut + half)]
    grad_query, grad_key, grad_value, grad_out = (
        side_by_side(core, mine[:, a:b], theirs[:, a:b], 1) for a, b in spans
    )

    return (
        output,
        input_grad,
        norms[0],
        grad_query,
        grad_key,
        grad_value,
        grad_out,
        norms[1],
        grad_gate,
        grad_up,
        grad_down,
    )


def solution(mesh):
    return jax.shard_map(
        shards,
        mesh=mesh,
        in_specs=(
            P("tok", None),
            P(),
            P(),
            P("tok"),
            P("tok", None),
            P("tok", None),
            P("tok", None),
            P("tok", None),
            P("tok"),
            P("tok", None),
            P("tok", None),
            P("tok", None),
            P("tok", None),
        ),
        out_specs=(
            P("tok", None),
            P("tok", None),
            P("tok"),
            P("tok", None),
            P("tok", None),
            P("tok", None),
            P("tok", None),
            P("tok"),
            P("tok", None),
            P("tok", None),
            P("tok", None),
        ),
        check_vma=False,
    )
```

```python
import jax
import jax.numpy as jnp
import numpy as np
from jax import lax
from jax.experimental import pallas as pl
from jax.experimental.pallas import tpu as pltpu
from jax.sharding import PartitionSpec as P

QK = 16
PAIR = 8
FEATS = 160
ROWS = 168
MIB = 1024 * 1024
eps = 1e-06
f32 = jnp.float32
bf16 = jnp.bfloat16


def bits_from(n, low):
    bits = []
    while low < n:
        bits.insert(0, low)
        low *= 2
    return bits


def flip(x, bits):
    n = lax.axis_size("tok")
    return lax.ppermute(x, "tok", [(i, i ^ bits) for i in range(n)])


def side(bit):
    return (lax.axis_index("tok") // bit) % 2


def pick(x, index, axis=0):
    return lax.dynamic_index_in_dim(x, index, axis, False)


def assemble(pieces):
    out = jnp.broadcast_to(pieces[0][1][None], (len(pieces),) + pieces[0][1].shape)
    for index, block in pieces[1:]:
        out = lax.dynamic_update_index_in_dim(out, block, index, 0)
    return out


def assemble_all(pieces):
    out = jnp.zeros((len(pieces),) + pieces[0][1].shape, pieces[0][1].dtype)
    for index, block in pieces:
        out = lax.dynamic_update_index_in_dim(out, block, index, 0)
    return out


def after(x, *others):
    return lax.optimization_barrier((x,) + others)[0] if others else x


def move(x, bits, start=(), stop=()):
    return after(flip(after(x, *start), bits), *stop)


def grow(x, bit, start=(), stop=()):
    return assemble([(side(bit), x), (1 - side(bit), move(x, bit, start, stop))])


def in_order(x, bits):
    done = bits[::-1]
    axes = [done.index(b) for b in sorted(done, reverse=True)]
    x = x.transpose(axes + list(range(len(done), x.ndim)))
    return x.reshape((-1,) + x.shape[len(done) :])


def grown(bits):
    at = [0]
    for bit in bits[::-1]:
        at = [i + j for i in at for j in (0, bit)]
    return at


class Scatter:
    def __init__(self, make, bits):
        self.make, self.bits, self.bit = make, bits, bits[-1]

    def send(self, *start):
        self.sent = after(self.make(1 - side(self.bit), *start), *start)
        self.here = flip(self.sent, self.bit)

    def keep(self, *gate):
        self.kept = self.make(side(self.bit), *gate)
        return self.kept

    def gated(self, gate):
        self.here = after(self.here, *gate)
        return self

    def hold(self, x, *gate):
        x, self.here = lax.optimization_barrier((x, after(self.here, *gate)))
        return x

    def step(self, *gate):
        kept, here = self.kept, after(self.here, *gate)
        self.bits = self.bits[:-1]
        if not self.bits:
            return (kept.astype(f32) + here.astype(f32))[0]
        bit = self.bits[-1]

        def half(index):
            return sum(pick(a.reshape((-1, 2) + a.shape[1:]), index, 1).astype(f32) for a in (kept, here))

        self.sent = half(1 - side(bit)).astype(bf16)
        self.kept = half(side(bit))
        self.here = flip(self.sent, bit)
        return self.sent

    def finish(self, *gate):
        while len(self.bits) > 1:
            self.step(*gate)
        return self.step(*gate)


def join(both):
    out = Scatter(None, both[0].bits[:-1] + [0])
    out.kept = jnp.concatenate([part.kept for part in both], axis=2)
    out.here = jnp.concatenate([part.here for part in both], axis=2)
    return out


MESH = pl.DeviceIdType.MESH
INV = pl.BlockSpec(memory_space=pltpu.VMEM)


def across(me, bits):
    for bit in (1, 2, 4, 8, 16):
        if bits & bit:
            me = me + bit - 2 * bit * ((me // bit) % 2)
    return me


def meet(me, partners):
    barrier = pltpu.get_barrier_semaphore()
    for bits in partners:
        pl.semaphore_signal(barrier, inc=1, device_id=(across(me, bits),), device_id_type=MESH)
    pl.semaphore_wait(barrier, len(partners))


class Mail:
    def __init__(self, me, sems):
        self.me, self.sems, self.count, self.open = me, sems, 0, []
    def send(self, source, target, bits):
        at = self.count
        self.count += 1
        copy = pltpu.make_async_remote_copy(src_ref=source, dst_ref=target, send_sem=self.sems.at[0, at],
            recv_sem=self.sems.at[1, at], device_id=(across(self.me, bits),), device_id_type=MESH)
        copy.start()
        self.open.append(copy)
        return copy
    def local(self, source, target):
        at = self.count
        self.count += 1
        copy = pltpu.make_async_copy(source, target, self.sems.at[0, at])
        copy.start()
        return copy
    def close(self):
        for copy in self.open:
            copy.wait_send()


def first_body(gains_in, gate_in, up_in, mine, theirs, down_in, gains, gate, up, z4, down, chip, sems):
    me = lax.axis_index("tok")
    core, z = me % 2, me // 8
    meet(me, (1, 2, 4, 8, 9, 16))
    mail = Mail(me, sems)
    size = mine.shape[0]
    swap = mail.send(theirs, chip.at[pl.ds(core * size, size)], 1)
    own = mail.local(mine, chip.at[pl.ds(core * size, size)])
    gains[pl.ds(me, 1)] = gains_in[...]

    def member(d):
        return ((d // 8) % 2) * 2 + d % 2

    place = (me // 2) % 4
    cut = down_in.shape[1] // 2
    a, b = pl.ds(0, cut), pl.ds(cut, cut)
    xa = mail.send(down_in.at[:, a], down.at[place, :, a], 2)
    yb = mail.send(down_in.at[:, b], down.at[place, :, b], 4)
    to_gate = [mail.send(gate_in.at[member(across(me, k))], gate.at[member(me)], k) for k in (9, 8, 1)]
    own.wait()
    swap.wait_recv()
    high = mail.send(chip, z4.at[z], 16)
    low = mail.send(chip, z4.at[z], 8)
    to_up = [mail.send(up_in.at[member(across(me, k))], up.at[member(me)], k) for k in (9, 8, 1)]
    ya = mail.send(down_in.at[:, a], down.at[place, :, a], 4)
    xb = mail.send(down_in.at[:, b], down.at[place, :, b], 2)
    kept = [
        mail.local(down_in, down.at[place]),
        mail.local(chip, z4.at[z]),
        mail.local(gate_in.at[member(me)], gate.at[member(me)]),
        mail.local(up_in.at[member(me)], up.at[member(me)]),
    ]
    for bit in (1, 2, 4):
        at = pl.ds((me // bit) * bit, bit)
        mail.send(gains.at[at], gains.at[at], bit).wait_recv()
    high.wait_recv()
    zh = across(me, 16) // 8
    low2 = mail.send(z4.at[zh], z4.at[zh], 8)
    across_x, across_y = across(place, 1), across(place, 2)
    xa.wait_recv()
    ya2 = mail.send(down.at[across_x, :, a], down.at[across_x, :, a], 4)
    yb.wait_recv()
    xb2 = mail.send(down.at[across_y, :, b], down.at[across_y, :, b], 2)
    for bit in (8, 16):
        at = pl.ds((me // bit) * bit, bit)
        mail.send(gains.at[at], gains.at[at], bit).wait_recv()
    for c in to_gate + to_up + [low, low2, ya, xb, ya2, xb2]:
        c.wait_recv()
    for c in kept:
        c.wait()
    mail.close()


def spread_first(gains, gate, up, mine, theirs, down):
    rows, cols = mine.shape
    return pl.pallas_call(
        first_body,
        out_shape=[
            jax.ShapeDtypeStruct((32,) + gains.shape[1:], f32),
            jax.ShapeDtypeStruct(gate.shape, bf16),
            jax.ShapeDtypeStruct(up.shape, bf16),
            jax.ShapeDtypeStruct((4, 2 * rows, cols), bf16),
            jax.ShapeDtypeStruct((4,) + down.shape, bf16),
        ],
        in_specs=[INV] * 6,
        out_specs=[INV] * 5,
        scratch_shapes=[pltpu.VMEM((2 * rows, cols), bf16), pltpu.SemaphoreType.DMA((2, 28))],
        compiler_params=pltpu.CompilerParams(collective_id=1, has_side_effects=True, vmem_limit_bytes=20 * MIB),
    )(gains, gate, up, mine, theirs, down)


def second_body(z4, out_mine, out_theirs, gate, whole, out4, gate2, chip, sems):
    me = lax.axis_index("tok")
    core, z, place = me % 2, me // 8, (me // 2) % 4
    across_y, across_x = across(place, 2), across(place, 1)
    meet(me, (1, 2, 4, 8, 16))
    mail = Mail(me, sems)
    size, cut = out_mine.shape[0], z4.shape[2] // 2
    a, b = pl.ds(0, cut), pl.ds(cut, cut)
    ya = mail.send(z4.at[:, :, a], whole.at[:, place, :, a], 4)
    xb = mail.send(z4.at[:, :, b], whole.at[:, place, :, b], 2)
    swap = mail.send(out_theirs, chip.at[pl.ds(core * size, size)], 1)
    own = mail.local(out_mine, chip.at[pl.ds(core * size, size)])
    kept = [mail.local(z4, whole.at[:, place]), mail.local(gate, gate2.at[z // 2])]
    xa = mail.send(z4.at[:, :, a], whole.at[:, place, :, a], 2)
    yb = mail.send(z4.at[:, :, b], whole.at[:, place, :, b], 4)
    own.wait()
    swap.wait_recv()
    high = mail.send(chip, out4.at[z], 16)
    low = mail.send(chip, out4.at[z], 8)
    kept.append(mail.local(chip, out4.at[z]))
    gate_high = mail.send(gate, gate2.at[z // 2], 16)
    ya.wait_recv()
    xa2 = mail.send(whole.at[:, across_y, :, a], whole.at[:, across_y, :, a], 2)
    xb.wait_recv()
    yb2 = mail.send(whole.at[:, across_x, :, b], whole.at[:, across_x, :, b], 4)
    high.wait_recv()
    zh = across(me, 16) // 8
    low2 = mail.send(out4.at[zh], out4.at[zh], 8)
    for c in (xa, yb, xa2, yb2, low, low2, gate_high):
        c.wait_recv()
    for c in kept:
        c.wait()
    mail.close()


def spread_second(z4, out_mine, out_theirs, gate):
    rows, cols = out_mine.shape
    return pl.pallas_call(
        second_body,
        out_shape=[
            jax.ShapeDtypeStruct((4, 4) + z4.shape[1:], bf16),
            jax.ShapeDtypeStruct((4, 2 * rows, cols), bf16),
            jax.ShapeDtypeStruct((2,) + gate.shape, bf16),
        ],
        in_specs=[INV] * 4,
        out_specs=[INV] * 3,
        scratch_shapes=[pltpu.VMEM((2 * rows, cols), bf16), pltpu.SemaphoreType.DMA((2, 16))],
        compiler_params=pltpu.CompilerParams(collective_id=2, has_side_effects=True, vmem_limit_bytes=20 * MIB),
    )(z4, out_mine, out_theirs, gate)


def scan_body(sign, s_ref, o_ref, stage, here, whole, zhere, back, bhere, sems):
    me = lax.axis_index("tok")
    z, plane = me // 8, (me // 2) % 4
    barrier = pltpu.get_barrier_semaphore()
    for k in (1, 2, 3):
        for to in (across(me, 2 * k), lax.rem(me + 8 * k, 32)):
            pl.semaphore_signal(barrier, inc=1, device_id=(to,), device_id_type=MESH)
    pl.semaphore_wait(barrier, 6)

    def slot(k):
        return (across(me, 2 * k) // 2) % 4

    def copy(source, target, sem, i, to):
        return pltpu.make_async_remote_copy(
            src_ref=source,
            dst_ref=target,
            send_sem=sems.at[sem, 0, i],
            recv_sem=sems.at[sem, 1, i],
            device_id=(to,),
            device_id_type=MESH,
        )

    def receives(k):
        return z - k >= 0 if sign > 0 else z + k < 4

    def sends(k):
        return z + k < 4 if sign > 0 else z - k >= 0

    copies = []
    for k in (3, 1, 2):
        stage[k - 1] = s_ref[pl.ds(2 * slot(k), 2)].astype(stage.dtype)
        copies.append(copy(stage.at[k - 1], here.at[k - 1], 0, k - 1, across(me, 2 * k)))
        copies[-1].start()
    mine = [s_ref[pl.ds(2 * plane, 2)]]
    for c in copies:
        c.wait()
    mine += [here[k - 1].astype(f32) for k in (1, 2, 3)]
    whole[...] = sum(mine).astype(whole.dtype)
    for k in (2, 1, 3):

        @pl.when(sends(k))
        def _(k=k):
            copy(whole, zhere.at[k - 1], 1, k - 1, me + 8 * k * sign).start()

    for k in (1, 2, 3):

        @pl.when(receives(k))
        def _(k=k):
            copy(whole, zhere.at[k - 1], 1, k - 1, me).wait_recv()

        @pl.when(jnp.logical_not(receives(k)))
        def _(k=k):
            zhere[k - 1] = jnp.zeros_like(whole)

    for k in (1, 2, 3):

        @pl.when(sends(k))
        def _(k=k):
            copy(whole, zhere.at[k - 1], 1, k - 1, me).wait_send()

    beyond = sum(zhere[k].astype(f32) for k in range(3))
    copies = []
    for k in (3, 1, 2, 0):
        before = beyond
        for j in range(4):
            if j != k:
                before = before + (sign * (slot(k) - slot(j)) > 0).astype(f32) * mine[j]
        if k == 0:
            o_ref[pl.ds(2 * plane, 2)] = before
        else:
            back[k - 1] = before.astype(back.dtype)
            copies.append(copy(back.at[k - 1], bhere.at[k - 1], 2, k - 1, across(me, 2 * k)))
            copies[-1].start()
    for c in copies:
        c.wait()
    for k in (1, 2, 3):
        o_ref[pl.ds(2 * slot(k), 2)] = bhere[k - 1].astype(f32)


def spans_of(cols, most=512):
    return [(s, min(most, cols - s)) for s in range(0, cols, most)]


def ffn_body(order, sides, x_ref, g_ref, *refs):
    gates, ups, downs = refs[0:4], refs[4:8], refs[8:11]
    y_ref, act_ref, d_ref, dh_ref, w_gate_up, w_down, sem = refs[11:]
    cols = w_down.shape[0]

    @pl.when(pl.program_id(0) == 0)
    def _():
        size, part, rest = downs[0].shape[0], downs[1].shape[1], downs[2].shape[1]
        far = pl.ds(pl.multiple_of((1 - sides[4]) * size, 16), size)
        targets = [
            w_down.at[pl.ds(pl.multiple_of(sides[4] * size, 16), size)],
            w_down.at[far, pl.ds(0, part)],
            w_down.at[far, pl.ds(part, rest)],
        ]
        copies = [pltpu.make_async_copy(a, b, sem.at[i]) for i, (a, b) in enumerate(zip(downs, targets))]
        size = gates[0].shape[1]
        for j, pieces in enumerate((gates, ups)):
            for k, piece in enumerate(pieces):
                for i, at in enumerate(order):
                    rows = pl.ds(pl.multiple_of((at + sides[k]) * size, 16), size)
                    target = w_gate_up.at[rows, pl.ds(j * cols, cols)]
                    copies.append(pltpu.make_async_copy(piece.at[i], target, sem.at[len(copies)]))
        for copy in copies:
            copy.start()
        for copy in copies:
            copy.wait()

    x, g = x_ref[...], g_ref[...]
    for s, w in spans_of(cols):
        gate, upper = dot(x, w_gate_up[:, s : s + w]), dot(x, w_gate_up[:, cols + s : cols + s + w])
        d_act = dot_cols(g, w_down[s : s + w, :])
        sigma = jax.nn.sigmoid(gate)
        smooth = gate * sigma
        act_ref[:, s : s + w] = (smooth * upper).astype(bf16)
        d_ref[:, s : s + w] = (d_act * upper * sigma * (1.0 + gate * (1.0 - sigma))).astype(bf16)
        d_ref[:, cols + s : cols + s + w] = (d_act * smooth).astype(bf16)
    y_ref[...] = dot(act_ref[...], w_down[...]).astype(bf16)
    dh_ref[...] = dot_cols(d_ref[...], w_gate_up[...]).astype(bf16)


def ffn(x, g, gate, up, down, order, sides, tile=256):
    tokens, width = x.shape
    cols = 2 * down[0].shape[0]

    def block(w):
        return pl.BlockSpec((tile, w), lambda i: (i, 0))

    return pl.pallas_call(
        lambda *refs: ffn_body(order, *refs),
        out_shape=[jax.ShapeDtypeStruct((tokens, w), bf16) for w in (width, cols, 2 * cols, width)],
        grid=(tokens // tile,),
        in_specs=[pl.BlockSpec(memory_space=pltpu.SMEM), block(width), block(width)] + [pl.BlockSpec(memory_space=pl.ANY)] * 11,
        out_specs=[block(width), block(cols), block(2 * cols), block(width)],
        scratch_shapes=[
            pltpu.VMEM((width, 2 * cols), bf16),
            pltpu.VMEM((cols, width), bf16),
            pltpu.SemaphoreType.DMA((8 * len(order) + 3,)),
        ],
        compiler_params=pltpu.CompilerParams(vmem_limit_bytes=48 * MIB),
        cost_estimate=pl.CostEstimate(flops=0, bytes_accessed=0, transcendentals=0),
    )(sides, x, g, *gate, *up, *down)


def product_body(count, group, index, *refs):
    left, right, out = refs[: count * group], refs[count * group : count * (group + 1)], refs[-1]
    acc = 0.0
    for i in range(count):
        rows = jnp.concatenate([a[...] for a in left[i * group : (i + 1) * group]], axis=1)
        acc = acc + dot_rows(rows, right[i][...])
    out[...] = acc.astype(out.dtype)


def row_blocks(left, right, index, size, half=None, deps=()):
    count = index.shape[0]
    group = 4 if count % 4 == 0 else 1
    cols = right[0].shape[1] // (1 if half is None else 2)
    at_col = half or 0

    def block(tokens, j):
        return pl.BlockSpec((tokens, size), lambda i, at: (0, at[i * group + j]))

    return pl.pallas_call(
        lambda *refs: product_body(len(left), group, *refs),
        out_shape=jax.ShapeDtypeStruct((count * size, cols), bf16),
        grid_spec=pltpu.PrefetchScalarGridSpec(
            num_scalar_prefetch=1,
            grid=(count // group,),
            in_specs=[block(a.shape[0], j) for a in left for j in range(group)]
            + [pl.BlockSpec((b.shape[0], cols), lambda i, at: (0, at_col)) for b in right]
            + [pl.BlockSpec(memory_space=pl.ANY)] * len(deps),
            out_specs=pl.BlockSpec((group * size, cols), lambda i, at: (i, 0)),
        ),
        compiler_params=pltpu.CompilerParams(vmem_limit_bytes=56 * MIB),
        cost_estimate=pl.CostEstimate(flops=0, bytes_accessed=0, transcendentals=0),
    )(index.astype(jnp.int32), *[a for a in left for _ in range(group)], *right, *deps)


def apart_body(places, padded, w_ref, out_ref):
    w = w_ref[...].astype(f32)
    unit = w.shape[1] // sum(len(p) for p in places)
    gap = [jnp.zeros((w.shape[0], padded - unit), f32)] if padded > unit else []
    for q, place in enumerate(places):
        blocks = []
        for d in place:
            blocks += [w[:, d * unit : (d + 1) * unit]] + gap
        out_ref[q] = jnp.concatenate(blocks, axis=1).astype(bf16)


def apart(w, places, padded):
    rows, cols = w.shape[0], len(places[0]) * padded
    return pl.pallas_call(
        lambda *refs: apart_body(places, padded, *refs),
        out_shape=jax.ShapeDtypeStruct((len(places), rows, cols), bf16),
        in_specs=[INV],
        out_specs=INV,
        compiler_params=pltpu.CompilerParams(vmem_limit_bytes=24 * MIB),
        cost_estimate=pl.CostEstimate(flops=0, bytes_accessed=0, transcendentals=0),
    )(w)


def together_body(places, padded, unit, member, *refs):
    pieces, outs, held = refs[:4], refs[4:6], refs[6]
    for k, piece in enumerate(pieces):
        held[k] = piece[...].astype(f32)
    cols = len(places[0]) * padded
    for j, out in enumerate(outs):
        blocks = {}
        for q, place in enumerate(places):
            for i, d in enumerate(place):
                at = j * cols + i * padded
                blocks[d] = held[member[0] ^ q][:, at : at + unit]
        out[...] = jnp.concatenate([blocks[d] for d in sorted(blocks)], axis=1)


def together(pieces, places, padded, unit, member):
    rows = pieces[0].shape[0]
    whole = jax.ShapeDtypeStruct((rows, unit * sum(len(p) for p in places)), f32)
    return pl.pallas_call(
        lambda *refs: together_body(places, padded, unit, *refs),
        out_shape=[whole, whole],
        in_specs=[pl.BlockSpec(memory_space=pltpu.SMEM)] + [INV] * 4,
        out_specs=[INV, INV],
        scratch_shapes=[pltpu.VMEM((4,) + pieces[0].shape, f32)],
        compiler_params=pltpu.CompilerParams(vmem_limit_bytes=40 * MIB),
        cost_estimate=pl.CostEstimate(flops=0, bytes_accessed=0, transcendentals=0),
    )(jnp.reshape(member, (1,)).astype(jnp.int32), *pieces)


def wide_body(d_ref, w_ref, out_ref):
    out_ref[...] = dot_cols(d_ref[...], w_ref[...]).astype(bf16)


def times_transposed(d, w, tile=256):
    return pl.pallas_call(
        wide_body,
        out_shape=jax.ShapeDtypeStruct((d.shape[0], w.shape[0]), bf16),
        grid=(d.shape[0] // tile,),
        in_specs=[
            pl.BlockSpec((tile, d.shape[1]), lambda i: (i, 0)),
            pl.BlockSpec(w.shape, lambda i: (0, 0)),
        ],
        out_specs=pl.BlockSpec((tile, w.shape[0]), lambda i: (i, 0)),
        compiler_params=pltpu.CompilerParams(vmem_limit_bytes=48 * MIB),
        cost_estimate=pl.CostEstimate(flops=0, bytes_accessed=0, transcendentals=0),
    )(d, w)


def part_maker(left, right, bits, within=(0,), half=None):
    n = lax.axis_size("tok")
    size = left[0].shape[1] * 2 // n
    cols = right[0].shape[1] // (1 if half is None else 2)
    ids = np.asarray([(at + more) // 2 for at in grown(bits[:-1][::-1]) for more in within], np.int32)

    def make(index, *deps):
        index = jnp.asarray(ids) + index * (bits[-1] // 2)
        if size % 128 == 0:
            out = row_blocks(left, right, index, size, half, deps)
        else:
            out = sum(dot_rows(a, b) for a, b in zip(left, right)).astype(bf16).reshape(n // 2, size, -1)
            out = out[index][..., (half or 0) * cols : (half or 0) * cols + cols]
        return out.reshape(-1, size * len(within), cols)

    return make


def feature_tables(heads):
    pairs = [(a, b) for a in range(QK + 1) for b in range(a, QK + 1)]
    one = np.zeros((heads, heads * QK, FEATS), np.float32)
    two = np.zeros((heads, heads * QK, FEATS), np.float32)
    rows = np.zeros((8, FEATS), np.float32)
    for f, (a, b) in enumerate(pairs):
        for h in range(heads):
            if a < QK:
                one[h, h * QK + a, f] = 1
            if b < QK:
                two[h, h * QK + b, f] = 1
        rows[0, f] = a == QK
        rows[1, f] = b == QK
        if a == QK:
            rows[2, f] = 1.0
        elif b == QK:
            rows[2, f] = QK**-0.5
        else:
            rows[2, f] = (0.5 if a == b else 1.0) / QK
    return jnp.asarray(one, bf16), jnp.asarray(two, bf16), jnp.asarray(rows)


def dot(a, b):
    return lax.dot_general(a, b, (((1,), (0,)), ((), ())), preferred_element_type=f32)


def dot_rows(a, b):
    return lax.dot_general(a, b, (((0,), (0,)), ((), ())), preferred_element_type=f32)


def dot_cols(a, b):
    return lax.dot_general(a, b, (((1,), (1,)), ((), ())), preferred_element_type=f32)


def halves(x):
    high = x.astype(bf16)
    return high, (x - high.astype(f32)).astype(bf16)


def features(x, one, two, rows):
    return dot(x, one) + rows[0:1], dot(x, two) + rows[1:2]


def total_row(state):
    return jnp.concatenate([state[FEATS : FEATS + 1], state[FEATS + 1 : FEATS + 2, : FEATS - 128]], axis=1)


def store_state(ref, state, row):
    ref[0, 0, :FEATS, :] = state
    ref[0, 0, FEATS:, :] = jnp.zeros((ROWS - FEATS, state.shape[1]), f32)
    ref[0, 0, FEATS : FEATS + 1, :] = row[:, :128]
    ref[0, 0, FEATS + 1 : FEATS + 2, : FEATS - 128] = row[:, 128:]


def kept_rows(scal, tile, tokens):
    index = lax.broadcasted_iota(jnp.int32, (tokens, 1), 0) + tile * tokens
    return index >= scal[tile]


def state_body(scal, k_ref, v_ref, one, two, rows, out_ref):
    tile = pl.program_id(0)
    a, b = features(k_ref[...], one[0], two[0], rows)
    phi = jnp.where(kept_rows(scal, tile, a.shape[0]), a * b, 0.0)
    high, low = halves(phi)
    v = v_ref[...]
    store_state(out_ref, dot_rows(high, v) + dot_rows(low, v), jnp.sum(phi, axis=0, keepdims=True))


def weights(q_ref, k_ref, lo_ref, tile, head):
    tokens, lanes = q_ref.shape
    lane = lax.broadcasted_iota(jnp.int32, (tokens, lanes), 1) // QK == head
    q = jnp.where(lane, q_ref[...], jnp.zeros((), bf16))
    score = dot_cols(q, k_ref[...]) * QK**-0.5
    row = lax.broadcasted_iota(jnp.int32, score.shape, 0)
    col = lax.broadcasted_iota(jnp.int32, score.shape, 1)
    lo = lo_ref[...] - tile * tokens
    mask = (col <= row) & (col >= lo)
    weight = jnp.where(mask, 1.0 + score + 0.5 * score * score, 0.0)
    return lane, score, mask, weight, lo < 0


def forward_body(q_ref, k_ref, v_ref, lo_ref, carry_ref, one, two, rows, y_ref, mixed_ref):
    tile, head = pl.program_id(0), pl.program_id(1)
    _, _, _, weight, alive = weights(q_ref, k_ref, lo_ref, tile, head)
    a, b = features(q_ref[...], one[0], two[0], rows)
    phi = jnp.where(alive, a * b * rows[2:3], 0.0)
    high, low = halves(phi)
    carry = carry_ref[0, 0]
    s_high, s_low = halves(carry[:FEATS])
    numer = dot(weight.astype(bf16), v_ref[...])
    numer = numer + (dot(high, s_high) + dot(high, s_low) + dot(low, s_high))
    denom = jnp.sum(weight, axis=1, keepdims=True) + jnp.sum(phi * total_row(carry), axis=1, keepdims=True)
    y = numer / denom
    y_ref[...] = y
    mixed_ref[...] = y.astype(bf16)


def spread(t, a, b, one, two):
    first_high, first_low = halves(t * b)
    second_high, second_low = halves(t * a)
    return (
        dot_cols(first_high, one) + dot_cols(first_low, one) + dot_cols(second_high, two) + dot_cols(second_low, two)
    )


def backward_body(
    q_ref, k_ref, v_ref, lo_ref, carry_ref, one, two, rows, y_ref, d_ref, dq_ref, dk_ref, dv_ref, ds_ref, dq_acc, dk_acc
):
    tile, head = pl.program_id(0), pl.program_id(1)
    lane, score, mask, weight, alive = weights(q_ref, k_ref, lo_ref, tile, head)
    a, b = features(q_ref[...], one[0], two[0], rows)
    phi = jnp.where(alive, a * b * rows[2:3], 0.0)
    high, low = halves(phi)
    carry = carry_ref[0, 0]
    s_high, s_low = halves(carry[:FEATS])
    row = total_row(carry)
    denom = jnp.sum(weight, axis=1, keepdims=True) + jnp.sum(phi * row, axis=1, keepdims=True)
    d = d_ref[...].astype(f32)
    g = d / denom
    c = -jnp.sum(d * y_ref[...], axis=1, keepdims=True) / denom
    g_high, g_low = halves(g)
    v = v_ref[...]
    dk = dot_cols(g_high, v) + dot_cols(g_low, v) + c
    ds = jnp.where(mask, dk * (1.0 + score) * QK**-0.5, 0.0).astype(bf16)
    dv_ref[...] = dot_rows(weight.astype(bf16), g_high)
    dphi = dot_cols(g_high, s_high) + dot_cols(g_high, s_low) + dot_cols(g_low, s_high) + c * row
    t = jnp.where(alive, dphi * rows[2:3], 0.0)
    dq = jnp.where(lane, dot(ds, k_ref[...]), 0.0) + spread(t, a, b, one[0], two[0])
    dkeys = jnp.where(lane, dot_rows(ds, q_ref[...]), 0.0)

    @pl.when(head == 0)
    def _():
        dq_acc[...] = dq
        dk_acc[...] = dkeys

    @pl.when(head > 0)
    def _():
        dq_acc[...] += dq
        dk_acc[...] += dkeys

    @pl.when(head == pl.num_programs(1) - 1)
    def _():
        dq_ref[...] = dq_acc[...].astype(bf16)
        dk_ref[...] = dk_acc[...]

    state = dot_rows(high, g_high) + dot_rows(high, g_low) + dot_rows(low, g_high)
    store_state(ds_ref, state, jnp.sum(phi * c, axis=0, keepdims=True))


def carried_body(scal, k_ref, v_ref, one, two, rows, grad_ref, dk_in, dv_in, dk_ref, dv_ref, acc):
    tile, head = pl.program_id(0), pl.program_id(1)
    a, b = features(k_ref[...], one[0], two[0], rows)
    keep = kept_rows(scal, tile, a.shape[0])
    high, low = halves(jnp.where(keep, a * b, 0.0))
    grad = grad_ref[0, 0]
    g_high, g_low = halves(grad[:FEATS])
    v = v_ref[...]
    dv = dv_in[...] + dot(high, g_high) + dot(high, g_low) + dot(low, g_high)
    dv_ref[...] = dv.astype(bf16)
    t = jnp.where(keep, dot_cols(v, g_high) + dot_cols(v, g_low) + total_row(grad), 0.0)
    dk = spread(t, a, b, one[0], two[0])

    @pl.when(head == 0)
    def _():
        acc[...] = dk_in[...] + dk

    @pl.when(head > 0)
    def _():
        acc[...] += dk

    @pl.when(head == pl.num_programs(1) - 1)
    def _():
        dk_ref[...] = acc[...].astype(bf16)


class Attention:
    def __init__(self, qkv, lo, heads, tokens):
        self.qkv, self.heads, self.tokens = qkv, heads, tokens
        self.lo = lo[:, None]
        self.scal = jnp.stack([lo[tokens - 1], lo[2 * tokens - 1]])
        self.tables = feature_tables(heads)
        lanes = heads * QK
        self.value = (qkv.shape[1] - 2 * lanes) // heads
        skip = 2 * lanes // self.value
        self.q = pl.BlockSpec((tokens, lanes), lambda t, h: (t, 0))
        self.k = pl.BlockSpec((tokens, lanes), lambda t, h: (t, 1))
        self.v = pl.BlockSpec((tokens, self.value), lambda t, h: (t, h + skip))
        self.o = pl.BlockSpec((tokens, self.value), lambda t, h: (t, h))
        self.l = pl.BlockSpec((tokens, 1), lambda t, h: (t, 0))
        self.s = pl.BlockSpec((1, 1, ROWS, self.value), lambda t, h: (h, t, 0, 0))
        self.e = pl.BlockSpec((1, lanes, FEATS), lambda t, h: (h, 0, 0))
        self.r = pl.BlockSpec((8, FEATS), lambda t, h: (0, 0))
        self.m = pl.BlockSpec(memory_space=pltpu.SMEM)
        self.table_specs = [self.e, self.e, self.r]
        self.acc = pltpu.VMEM((tokens, lanes), f32)
        self.state_shape = jax.ShapeDtypeStruct((heads, 2, ROWS, self.value), f32)

    def wide(self, kind):
        return jax.ShapeDtypeStruct((2 * self.tokens, self.heads * self.value), kind)

    def narrow(self, kind):
        return jax.ShapeDtypeStruct((2 * self.tokens, self.heads * QK), kind)

    def call(self, body, ins, outs, shapes, scratch, limit, args):
        return pl.pallas_call(
            body,
            grid=(2, self.heads),
            in_specs=ins,
            out_specs=outs,
            out_shape=shapes,
            scratch_shapes=scratch,
            compiler_params=pltpu.CompilerParams(vmem_limit_bytes=limit * MIB),
            cost_estimate=pl.CostEstimate(flops=0, bytes_accessed=0, transcendentals=0),
        )(*args)

    def states(self):
        (out,) = self.call(
            state_body,
            [self.m, self.k, self.v] + self.table_specs,
            [self.s],
            [self.state_shape],
            [],
            24,
            (self.scal, self.qkv, self.qkv, *self.tables),
        )
        return out

    def forward(self, carry):
        return self.call(
            forward_body,
            [self.q, self.k, self.v, self.l, self.s] + self.table_specs,
            [self.o, self.o],
            [self.wide(f32), self.wide(bf16)],
            [],
            48,
            (self.qkv, self.qkv, self.qkv, self.lo, carry, *self.tables),
        )

    def backward(self, carry, y, d_heads):
        return self.call(
            backward_body,
            [self.q, self.k, self.v, self.l, self.s] + self.table_specs + [self.o, self.o],
            [self.q, self.q, self.o, self.s],
            [self.narrow(bf16), self.narrow(f32), self.wide(f32), self.state_shape],
            [self.acc, self.acc],
            48,
            (self.qkv, self.qkv, self.qkv, self.lo, carry, *self.tables, y, d_heads),
        )

    def carried(self, grad, dk, dv):
        return self.call(
            carried_body,
            [self.m, self.k, self.v] + self.table_specs + [self.s, self.q, self.o],
            [self.q, self.o],
            [self.narrow(bf16), self.wide(bf16)],
            [self.acc],
            48,
            (self.scal, self.qkv, self.qkv, *self.tables, grad, dk, dv),
        )


def others(state, earlier, kind):
    n = lax.axis_size("tok")
    me = lax.axis_index("tok")
    sign = 1 if earlier else -1
    if n != 32:
        parts = lax.all_gather(state.astype(kind), "tok").astype(f32)
        index = jnp.arange(n)
        before = (sign * (me // 2 - index // 2) > 0) & (index % 2 == me % 2)
        out = jnp.sum(jnp.where(before.reshape((n,) + (1,) * state.ndim), parts, 0.0), axis=0)
        return out
    block = (state.shape[0] // 4,) + state.shape[1:]
    slots = pltpu.VMEM((3,) + block, kind)
    return pl.pallas_call(
        lambda *refs: scan_body(sign, *refs),
        out_shape=jax.ShapeDtypeStruct(state.shape, f32),
        in_specs=[INV],
        out_specs=INV,
        scratch_shapes=[slots, slots, pltpu.VMEM(block, kind), slots, slots, slots, pltpu.SemaphoreType.DMA((3, 2, 3))],
        compiler_params=pltpu.CompilerParams(
            collective_id=3 if earlier else 4, has_side_effects=True, vmem_limit_bytes=16 * MIB
        ),
        cost_estimate=pl.CostEstimate(flops=0, bytes_accessed=0, transcendentals=0),
    )(state)


def row_starts(positions, lengths, offsets):
    inside = (positions[:, None] >= offsets[None, :]) & (positions[:, None] < offsets[None, :] + lengths[None, :])
    return jnp.sum(jnp.where(inside, offsets[None, :], 0), axis=1)


def side_by_side(core, mine, theirs, axis=0):
    size = mine.shape[axis]
    shape = list(mine.shape)
    shape[axis] *= 2
    out = jnp.zeros(shape, mine.dtype)
    out = lax.dynamic_update_slice_in_dim(out, mine, core * size, axis)
    return lax.dynamic_update_slice_in_dim(out, theirs, (1 - core) * size, axis)


def shards(
    block_input,
    lengths,
    offsets,
    norm1_gain,
    w_query,
    w_key,
    w_value,
    w_out,
    norm2_gain,
    w_gate,
    w_up,
    w_down,
    out_grad,
):
    n = lax.axis_size("tok")
    me = lax.axis_index("tok")
    core, member = me % 2, side(PAIR) * 2 + me % 2
    cbits = bits_from(n, 2)
    qbits = [bit for bit in cbits if bit != PAIR]
    swapped = qbits[:-2] + [qbits[-1], qbits[-2]]
    chips, quads = n // 2, n // 4
    above, below = n // (2 * PAIR), PAIR // 2
    groups = [
        [i * 2 * PAIR + p * PAIR + j * 2 + c for i in range(above) for j in range(below)] for p in (0, 1) for c in (0, 1)
    ]
    to_member = {1: 1, 2: PAIR, 3: PAIR + 1}
    tokens, width = block_input.shape
    rows = w_query.shape[0]
    heads = w_query.shape[1] // QK // 2
    half = width // 2
    lanes = heads * QK
    def column_half(w, which):
        return lax.dynamic_slice_in_dim(w, which * (w.shape[1] // 2), w.shape[1] // 2, 1)

    def row_half(w, which):
        return lax.dynamic_slice_in_dim(w, which * (w.shape[0] // 2), w.shape[0] // 2, 0)

    unit = w_down.shape[0]
    padded = -(-unit // 16) * 16
    cols = quads * padded

    gate, up = apart(w_gate, groups, padded), apart(w_up, groups, padded)
    down = jnp.pad(w_down, ((0, padded - unit), (0, 0)))
    near_grad = side_by_side(core, out_grad, flip(out_grad, 1))

    def by_core(which):
        return jnp.concatenate([column_half(w, which) for w in (w_query, w_key, w_value)], axis=1)

    gains = jnp.stack([norm1_gain, norm2_gain]).astype(f32)
    if n == 32:
        gains = jnp.pad(gains, ((0, 6), (0, 128 - rows)))[None]
        gains = after(gains, near_grad)
        gains, gate, up, qkv_all, down = spread_first(gains, gate, up, by_core(core), by_core(1 - core), down)
        gains = gains[:, :2, :rows].transpose(1, 0, 2).reshape(2, 1, width)
        z4 = qkv_all
        qkv_all, out_half, gate = spread_second(z4, column_half(w_out, core), column_half(w_out, 1 - core), gate)
        qkv_all = qkv_all.reshape(width, -1)
    else:

        def to_group(x):
            pieces = [(member, pick(x, member))]
            for k in range(1, 4):
                pieces.append((member ^ k, flip(pick(x, member ^ k), to_member[k])))
            return assemble_all(pieces)

        gate, up = to_group(gate), to_group(up)
        qkv_all = side_by_side(core, by_core(core), flip(by_core(1 - core), 1))
        gains = grow(gains, 1)
        for bit in cbits:
            gains, qkv_all = grow(gains, bit), grow(qkv_all, bit)
        gains = in_order(gains, [1] + cbits).transpose(1, 0, 2).reshape(2, 1, width)
        qkv_all = in_order(qkv_all, cbits).reshape(width, -1)
        out_half = side_by_side(core, column_half(w_out, core), flip(column_half(w_out, 1 - core), 1))
        for bit in cbits[:-2]:
            out_half = grow(out_half, bit)
        out_half = in_order(out_half, cbits[:-2])
        gate = grow(gate, qbits[0])
        for bit in qbits[1:]:
            down = grow(down, bit)
        down = in_order(down, qbits[1:])
    gain_one, gain_two = gains[0], gains[1]

    inputs32 = block_input.astype(f32)
    ratio_one = lax.rsqrt(jnp.mean(inputs32 * inputs32, axis=1, keepdims=True) + eps)
    normed_one = inputs32 * ratio_one
    hidden_one = (normed_one * gain_one).astype(bf16)
    hidden_chip = side_by_side(core, hidden_one, move(hidden_one, 1, (), (qkv_all,)))
    qkv = dot(hidden_chip, qkv_all).astype(bf16)

    first = (me // 2) * 2 * tokens
    positions = first + jnp.arange(2 * tokens, dtype=jnp.int32)
    lo = row_starts(positions, lengths, offsets) - first
    attention = Attention(qkv, lo, heads, tokens)
    states = attention.states()
    fresh0 = (lo[tokens - 1] >= 0).astype(f32)
    fresh1 = (lo[2 * tokens - 1] >= tokens).astype(f32)

    start, stop = (qkv_all,), (states,)
    for bit in qbits[1:-2]:
        gate = grow(gate, bit)
    gate_x = move(gate, 2, start, stop)
    up = grow(up, qbits[0], start, stop)
    for bit in qbits[1:-2]:
        up = grow(up, bit)
    out_y = move(out_half, 4, start, stop)
    leaving = states[:, 1] + (1.0 - fresh1) * states[:, 0]
    leaving, gate_x, up, out_y = lax.optimization_barrier((leaving, gate_x, up, out_y))
    entering = others(leaving, True, f32)
    start, stop = (leaving,), (entering,)
    down = down.reshape(cols // 2, width)
    down_a, down_b = down[:, : width * 3 // 4], down[:, width * 3 // 4 :]
    out_both = jnp.stack([out_half, out_y])
    gate_up = jnp.concatenate([gate, up], axis=-1)
    flows = [(out_both, 2), (gate_up, 4), (up, 2), (down_a, qbits[0]), (out_grad, PAIR)]
    flows = [move(w, bit, start, stop) for w, bit in flows]
    entering, out_x, gate_up, up_x, down_a, far_grad = lax.optimization_barrier((entering, *flows))
    gate_y, up_y = gate_up[..., :cols], gate_up[..., cols:]
    carry = jnp.stack([entering, states[:, 0] + (1.0 - fresh0) * entering], axis=1)
    place = (me // 2) % 4
    out_pieces = [(place, out_half), (place ^ 1, out_x[0]), (place ^ 2, out_y), (place ^ 3, out_x[1])]
    out_half = jnp.zeros((chips // 4, 4, 2 * rows, half), bf16)
    for index, piece in out_pieces:
        out_half = lax.dynamic_update_index_in_dim(out_half, piece, index, 1)
    out_half = out_half.reshape(width, half)
    carry = after(carry, out_half)
    y_heads, mixed_heads = attention.forward(carry)
    start, stop = (carry,), (mixed_heads,)
    flows = [move(w, bit, start, stop) for w, bit in [(gate_x, 4), (up_y, 2), (down_b, qbits[0])]]
    out_there = move(out_half, 1, start, stop)
    mixed_heads, out_there, *flows = lax.optimization_barrier((mixed_heads, out_there, *flows))
    gate_xy, up_xy, down_b = flows
    down = [down, down_a, down_b]
    out_all = side_by_side(core, out_half, out_there, 1)
    mixed_chip = side_by_side(core, mixed_heads, flip(mixed_heads, 1), 1)
    middle = inputs32 + dot(row_half(mixed_chip, core), out_all)
    ratio_two = lax.rsqrt(jnp.mean(middle * middle, axis=1, keepdims=True) + eps)
    normed_two = middle * ratio_two
    hidden_two = (normed_two * gain_two).astype(bf16)

    far_hidden = flip(hidden_two, PAIR)
    near_hidden = side_by_side(core, hidden_two, flip(hidden_two, 1))
    gate = [w.reshape(-1, 2 * rows, cols) for w in (gate, gate_x, gate_y, gate_xy)]
    up = [w.reshape(-1, 2 * rows, cols) for w in (up, up_x, up_y, up_xy)]
    order = [(at + more) // 2 for at in grown(qbits[:-2]) for more in (0, PAIR)]
    sides = jnp.stack([place, place ^ 1, place ^ 2, place ^ 3, side(qbits[0])])
    near = ffn(near_hidden, near_grad, gate, up, down, order, sides)
    far_hidden, far_there = after(far_hidden, *near), move(far_grad, 1, (near_hidden,), (near[0],))
    far_grad = side_by_side(core, far_grad, far_there)
    far_hidden = side_by_side(core, far_hidden, flip(far_hidden, 1))
    far = ffn(far_hidden, far_grad, gate, up, down, order, sides)
    start, stop = (near[0], far_hidden), (far[0],)
    near_parts = [move(row_half(near[i], 1 - core), 1, start, stop) for i in (3, 0)]
    far, near_parts = lax.optimization_barrier((far, near_parts))

    right = [near[2], far[2]]
    sum_gate = Scatter(part_maker([near_hidden, far_hidden], right, qbits, (0, PAIR), 0), qbits)
    sum_gate.send()
    start, stop = (far[0],), (sum_gate.sent,)
    far_parts = [move(row_half(far[i], 1 - core), 1, start, stop) for i in (3, 0)]
    sent, far_parts = lax.optimization_barrier((sum_gate.sent, far_parts))
    d_far = (row_half(far[3], core).astype(f32) + far_parts[0].astype(f32)).astype(bf16)
    y_far = (row_half(far[0], core).astype(f32) + far_parts[1].astype(f32)).astype(bf16)
    sum_up = Scatter(part_maker([near_hidden, far_hidden], right, swapped, (0, PAIR), 1), swapped)
    sum_up.send(sent, d_far, y_far)
    sum_gate.keep(sum_up.sent)
    sum_up.keep(sum_gate.kept)
    term = row_blocks([near[1], far[1]], [near_grad, far_grad], jnp.arange(cols // 128), 128, None, (sum_up.kept,))
    d_far = move(d_far, PAIR, (), (term,))
    d_far = sum_gate.hold(d_far, term)
    near_parts = after(near_parts, d_far)
    d_near = row_half(near[3], core).astype(f32) + near_parts[0].astype(f32)
    y_near = row_half(near[0], core).astype(f32) + near_parts[1].astype(f32)
    d_hidden_two = d_near + d_far.astype(f32)
    term_norm_two = jnp.sum(d_hidden_two * normed_two, axis=0)
    scaled_two = d_hidden_two * gain_two
    d_middle = out_grad.astype(f32) + ratio_two * (
        scaled_two - normed_two * jnp.mean(scaled_two * normed_two, axis=1, keepdims=True)
    )
    d_mixed = d_middle.astype(bf16)
    d_mixed_chip = side_by_side(core, d_mixed, flip(d_mixed, 1))
    d_heads = dot_cols(d_mixed_chip, row_half(out_all, core)).astype(bf16)

    d_heads = sum_up.hold(d_heads, d_mixed)
    d_heads = after(d_heads, sum_gate.step(), sum_up.step())
    dq, dk, dv, d_states = attention.backward(carry, y_heads, d_heads)
    flows = (sum_gate.here, sum_up.here, move(y_far, PAIR, (d_heads,)))
    flows = [after(flow, d_states) for flow in flows]
    d_states, sum_gate.here, sum_up.here, y_far = lax.optimization_barrier((d_states, *flows))
    sum_both = join([sum_gate, sum_up])
    sent = [sum_both.step()]

    def down_x(index, *_):
        return pick(term.reshape(quads // 2, 2, padded, width)[..., :half], index, 1)

    def down_y(index, *_):
        return pick(term.reshape(quads // 4, 2, 2, padded, width)[..., half:], index, 1).reshape(-1, padded, half)

    sum_down = [Scatter(down_x, qbits), Scatter(down_y, swapped)]
    for part in sum_down:
        part.send(d_states)
        part.keep()
    sent += [part.sent for part in sum_down]
    d_mixed_half = column_half(d_mixed_chip, core)
    out_sums = []
    for h, bits in ((0, cbits), (1, cbits[:-2] + [cbits[-1], cbits[-2]])):
        out_sums.append(Scatter(part_maker([after(mixed_chip, *sent)], [d_mixed_half], bits, (0,), h), bits))
        out_sums[-1].send()
    leaving = d_states[:, 0] + (1.0 - fresh0) * d_states[:, 1]
    leaving = others(after(leaving, *(part.sent for part in out_sums)), False, bf16)
    for part in out_sums:
        leaving = after(leaving, part.keep(leaving))
    for part in [sum_both] + sum_down + out_sums:
        leaving = part.hold(leaving, leaving)
    leaving = after(leaving, *(part.step() for part in sum_down + out_sums))
    d_states = jnp.stack([d_states[:, 1] + (1.0 - fresh1) * leaving, leaving], axis=1)
    dk, dv = attention.carried(d_states, dk, dv)
    for part in out_sums + sum_down:
        dk = part.hold(dk, dk)
    sum_down = join(sum_down)
    dk = after(dk, sum_down.step())
    d_qkv = jnp.concatenate([dq, dk, dv], axis=1)

    cut = d_qkv.shape[1] // 2
    sums = []
    for h, bits in ((0, cbits), (1, cbits[:-2] + [cbits[-1], cbits[-2]])):
        sums.append(Scatter(part_maker([hidden_chip], [d_qkv], bits, (0,), h), bits))
        sums[-1].send(*(p.sent for p in sums[:-1]))
    start = tuple(part.sent for part in sums)
    for part in sums:
        part.keep(*start)
        start = (part.kept,)
    rest_out = join([part.gated(start) for part in out_sums])
    start = start + (rest_out.step(),)
    d_hidden_one = times_transposed(after(d_qkv, *start), qkv_all)
    for part in [sum_down, rest_out] + sums:
        d_hidden_one = part.hold(d_hidden_one, d_hidden_one)
    sent = [part.step() for part in sums]
    d_hidden_one = after(d_hidden_one, *sent)
    theirs = flip(row_half(d_hidden_one, 1 - core), 1)
    gate_sum = after(sum_both.finish(), *sent).astype(bf16).reshape(4, rows, 2 * cols)
    parts = [flip(after(pick(gate_sum, member ^ k), theirs), to_member[k]) for k in range(1, 4)]
    d_hidden_one = row_half(d_hidden_one, core).astype(f32) + theirs.astype(f32)
    term_norm_one = jnp.sum(d_hidden_one * normed_one, axis=0)
    scaled_one = d_hidden_one * gain_one
    mean_one = jnp.mean(scaled_one * normed_one, axis=1, keepdims=True)
    norms = jnp.stack([term_norm_one, term_norm_two])
    for part in sums:
        norms = part.hold(norms, theirs)
    norms, parts = lax.optimization_barrier((norms, parts))
    rest = join(sums)
    sent = [rest.step()] + [rest_out.step() for _ in rest_out.bits[1:]]
    norms = after(norms, *sent)
    norms = norms + flip(norms, 1)
    norms = norms + flip(norms, cbits[-1])
    norms = norms + flip(norms, cbits[-2])
    norms = norms + flip(norms, cbits[-3])
    norms = rest_out.hold(rest.hold(norms, norms), norms)
    while len(rest.bits) > 1:
        sent = [rest.step()]
    norms = after(norms, *sent)
    grad_gate, grad_up = together([pick(gate_sum, member), *parts], groups, padded, unit, member)
    for bit in cbits[:-3]:
        norms = norms + flip(norms, bit)
    norms = pick(norms.reshape(2, n, rows), me, 1)
    input_grad = d_middle + ratio_one * (after(scaled_one, *sent) - normed_one * mean_one)
    output = (after(middle, *sent) + y_near + y_far.astype(f32)).astype(bf16)
    grad_down = sum_down.finish()[:unit]
    rest.kept = jnp.concatenate([rest.kept, rest_out.kept], axis=2)
    rest.here = jnp.concatenate([rest.here, rest_out.here], axis=2)
    total = rest.step()
    mine, theirs = row_half(total, core), flip(row_half(total, 1 - core), 1)
    spans = [(0, lanes), (lanes, 2 * lanes), (2 * lanes, 2 * lanes + half), (2 * cut, 2 * cut + half)]
    grad_query, grad_key, grad_value, grad_out = (
        side_by_side(core, mine[:, a:b], theirs[:, a:b], 1) for a, b in spans
    )

    return (
        output,
        input_grad,
        norms[0],
        grad_query,
        grad_key,
        grad_value,
        grad_out,
        norms[1],
        grad_gate,
        grad_up,
        grad_down,
    )


def solution(mesh):
    return jax.shard_map(
        shards,
        mesh=mesh,
        in_specs=(
            P("tok", None),
            P(),
            P(),
            P("tok"),
            P("tok", None),
            P("tok", None),
            P("tok", None),
            P("tok", None),
            P("tok"),
            P("tok", None),
            P("tok", None),
            P("tok", None),
            P("tok", None),
        ),
        out_specs=(
            P("tok", None),
            P("tok", None),
            P("tok"),
            P("tok", None),
            P("tok", None),
            P("tok", None),
            P("tok", None),
            P("tok"),
            P("tok", None),
            P("tok", None),
            P("tok", None),
        ),
        check_vma=False,
    )
```

```python
import jax
import jax.numpy as jnp
import numpy as np
from jax import lax
from jax.experimental import pallas as pl
from jax.experimental.pallas import tpu as pltpu
from jax.sharding import PartitionSpec as P

QK = 16
PAIR = 8
FEATS = 160
ROWS = 168
MIB = 1024 * 1024
eps = 1e-06
f32 = jnp.float32
bf16 = jnp.bfloat16


def bits_from(n, low):
    bits = []
    while low < n:
        bits.insert(0, low)
        low *= 2
    return bits


def flip(x, bits):
    n = lax.axis_size("tok")
    return lax.ppermute(x, "tok", [(i, i ^ bits) for i in range(n)])


def side(bit):
    return (lax.axis_index("tok") // bit) % 2


def pick(x, index, axis=0):
    return lax.dynamic_index_in_dim(x, index, axis, False)


def assemble(pieces):
    out = jnp.broadcast_to(pieces[0][1][None], (len(pieces),) + pieces[0][1].shape)
    for index, block in pieces[1:]:
        out = lax.dynamic_update_index_in_dim(out, block, index, 0)
    return out


def assemble_all(pieces):
    out = jnp.zeros((len(pieces),) + pieces[0][1].shape, pieces[0][1].dtype)
    for index, block in pieces:
        out = lax.dynamic_update_index_in_dim(out, block, index, 0)
    return out


def after(x, *others):
    return lax.optimization_barrier((x,) + others)[0] if others else x


def move(x, bits, start=(), stop=()):
    return after(flip(after(x, *start), bits), *stop)


def grow(x, bit, start=(), stop=()):
    return assemble([(side(bit), x), (1 - side(bit), move(x, bit, start, stop))])


def in_order(x, bits):
    done = bits[::-1]
    axes = [done.index(b) for b in sorted(done, reverse=True)]
    x = x.transpose(axes + list(range(len(done), x.ndim)))
    return x.reshape((-1,) + x.shape[len(done) :])


def grown(bits):
    at = [0]
    for bit in bits[::-1]:
        at = [i + j for i in at for j in (0, bit)]
    return at


class Scatter:
    def __init__(self, make, bits):
        self.make, self.bits, self.bit = make, bits, bits[-1]

    def send(self, *start):
        self.sent = after(self.make(1 - side(self.bit), *start), *start)
        self.here = flip(self.sent, self.bit)

    def keep(self, *gate):
        self.kept = self.make(side(self.bit), *gate)
        return self.kept

    def gated(self, gate):
        self.here = after(self.here, *gate)
        return self

    def hold(self, x, *gate):
        x, self.here = lax.optimization_barrier((x, after(self.here, *gate)))
        return x

    def step(self, *gate):
        kept, here = self.kept, after(self.here, *gate)
        self.bits = self.bits[:-1]
        if not self.bits:
            return (kept.astype(f32) + here.astype(f32))[0]
        bit = self.bits[-1]

        def half(index):
            return sum(pick(a.reshape((-1, 2) + a.shape[1:]), index, 1).astype(f32) for a in (kept, here))

        self.sent = half(1 - side(bit)).astype(bf16)
        self.kept = half(side(bit))
        self.here = flip(self.sent, bit)
        return self.sent

    def finish(self, *gate):
        while len(self.bits) > 1:
            self.step(*gate)
        return self.step(*gate)


def join(both):
    out = Scatter(None, both[0].bits[:-1] + [0])
    out.kept = jnp.concatenate([part.kept for part in both], axis=2)
    out.here = jnp.concatenate([part.here for part in both], axis=2)
    return out


MESH = pl.DeviceIdType.MESH
INV = pl.BlockSpec(memory_space=pltpu.VMEM)


def across(me, bits):
    for bit in (1, 2, 4, 8, 16):
        if bits & bit:
            me = me + bit - 2 * bit * ((me // bit) % 2)
    return me


def meet(me, partners):
    barrier = pltpu.get_barrier_semaphore()
    for bits in partners:
        pl.semaphore_signal(barrier, inc=1, device_id=(across(me, bits),), device_id_type=MESH)
    pl.semaphore_wait(barrier, len(partners))


class Mail:
    def __init__(self, me, sems):
        self.me, self.sems, self.count, self.open = me, sems, 0, []
    def send(self, source, target, bits):
        at = self.count
        self.count += 1
        copy = pltpu.make_async_remote_copy(src_ref=source, dst_ref=target, send_sem=self.sems.at[0, at],
            recv_sem=self.sems.at[1, at], device_id=(across(self.me, bits),), device_id_type=MESH)
        copy.start()
        self.open.append(copy)
        return copy
    def local(self, source, target):
        at = self.count
        self.count += 1
        copy = pltpu.make_async_copy(source, target, self.sems.at[0, at])
        copy.start()
        return copy
    def close(self):
        for copy in self.open:
            copy.wait_send()


def first_body(gains_in, gate_in, up_in, mine, theirs, down_in, gains, gate, up, z4, down, chip, sems):
    me = lax.axis_index("tok")
    core, z = me % 2, me // 8
    meet(me, (1, 2, 4, 8, 9, 16))
    mail = Mail(me, sems)
    size = mine.shape[0]
    swap = mail.send(theirs, chip.at[pl.ds(core * size, size)], 1)
    own = mail.local(mine, chip.at[pl.ds(core * size, size)])
    gains[pl.ds(me, 1)] = gains_in[...]

    def member(d):
        return ((d // 8) % 2) * 2 + d % 2

    place = (me // 2) % 4
    cut = down_in.shape[1] // 2
    a, b = pl.ds(0, cut), pl.ds(cut, cut)
    xa = mail.send(down_in.at[:, a], down.at[place, :, a], 2)
    yb = mail.send(down_in.at[:, b], down.at[place, :, b], 4)
    to_gate = [mail.send(gate_in.at[member(across(me, k))], gate.at[member(me)], k) for k in (9, 8, 1)]
    own.wait()
    swap.wait_recv()
    high = mail.send(chip, z4.at[z], 16)
    low = mail.send(chip, z4.at[z], 8)
    to_up = [mail.send(up_in.at[member(across(me, k))], up.at[member(me)], k) for k in (9, 8, 1)]
    ya = mail.send(down_in.at[:, a], down.at[place, :, a], 4)
    xb = mail.send(down_in.at[:, b], down.at[place, :, b], 2)
    kept = [
        mail.local(down_in, down.at[place]),
        mail.local(chip, z4.at[z]),
        mail.local(gate_in.at[member(me)], gate.at[member(me)]),
        mail.local(up_in.at[member(me)], up.at[member(me)]),
    ]
    for bit in (1, 2, 4):
        at = pl.ds((me // bit) * bit, bit)
        mail.send(gains.at[at], gains.at[at], bit).wait_recv()
    high.wait_recv()
    zh = across(me, 16) // 8
    low2 = mail.send(z4.at[zh], z4.at[zh], 8)
    across_x, across_y = across(place, 1), across(place, 2)
    xa.wait_recv()
    ya2 = mail.send(down.at[across_x, :, a], down.at[across_x, :, a], 4)
    yb.wait_recv()
    xb2 = mail.send(down.at[across_y, :, b], down.at[across_y, :, b], 2)
    for bit in (8, 16):
        at = pl.ds((me // bit) * bit, bit)
        mail.send(gains.at[at], gains.at[at], bit).wait_recv()
    for c in to_gate + to_up + [low, low2, ya, xb, ya2, xb2]:
        c.wait_recv()
    for c in kept:
        c.wait()
    mail.close()


def spread_first(gains, gate, up, mine, theirs, down):
    rows, cols = mine.shape
    return pl.pallas_call(
        first_body,
        out_shape=[
            jax.ShapeDtypeStruct((32,) + gains.shape[1:], f32),
            jax.ShapeDtypeStruct(gate.shape, bf16),
            jax.ShapeDtypeStruct(up.shape, bf16),
            jax.ShapeDtypeStruct((4, 2 * rows, cols), bf16),
            jax.ShapeDtypeStruct((4,) + down.shape, bf16),
        ],
        in_specs=[INV] * 6,
        out_specs=[INV] * 5,
        scratch_shapes=[pltpu.VMEM((2 * rows, cols), bf16), pltpu.SemaphoreType.DMA((2, 28))],
        compiler_params=pltpu.CompilerParams(collective_id=1, has_side_effects=True, vmem_limit_bytes=20 * MIB),
    )(gains, gate, up, mine, theirs, down)


def second_body(z4, out_mine, out_theirs, gate, whole, out4, gate2, chip, sems):
    me = lax.axis_index("tok")
    core, z, place = me % 2, me // 8, (me // 2) % 4
    across_y, across_x = across(place, 2), across(place, 1)
    meet(me, (1, 2, 4, 8, 16))
    mail = Mail(me, sems)
    size, cut = out_mine.shape[0], z4.shape[2] // 2
    a, b = pl.ds(0, cut), pl.ds(cut, cut)
    ya = mail.send(z4.at[:, :, a], whole.at[:, place, :, a], 4)
    xb = mail.send(z4.at[:, :, b], whole.at[:, place, :, b], 2)
    swap = mail.send(out_theirs, chip.at[pl.ds(core * size, size)], 1)
    own = mail.local(out_mine, chip.at[pl.ds(core * size, size)])
    kept = [mail.local(z4, whole.at[:, place]), mail.local(gate, gate2.at[z // 2])]
    xa = mail.send(z4.at[:, :, a], whole.at[:, place, :, a], 2)
    yb = mail.send(z4.at[:, :, b], whole.at[:, place, :, b], 4)
    own.wait()
    swap.wait_recv()
    high = mail.send(chip, out4.at[z], 16)
    low = mail.send(chip, out4.at[z], 8)
    kept.append(mail.local(chip, out4.at[z]))
    gate_high = mail.send(gate, gate2.at[z // 2], 16)
    ya.wait_recv()
    xa2 = mail.send(whole.at[:, across_y, :, a], whole.at[:, across_y, :, a], 2)
    xb.wait_recv()
    yb2 = mail.send(whole.at[:, across_x, :, b], whole.at[:, across_x, :, b], 4)
    high.wait_recv()
    zh = across(me, 16) // 8
    low2 = mail.send(out4.at[zh], out4.at[zh], 8)
    for c in (xa, yb, xa2, yb2, low, low2, gate_high):
        c.wait_recv()
    for c in kept:
        c.wait()
    mail.close()


def spread_second(z4, out_mine, out_theirs, gate):
    rows, cols = out_mine.shape
    return pl.pallas_call(
        second_body,
        out_shape=[
            jax.ShapeDtypeStruct((4, 4) + z4.shape[1:], bf16),
            jax.ShapeDtypeStruct((4, 2 * rows, cols), bf16),
            jax.ShapeDtypeStruct((2,) + gate.shape, bf16),
        ],
        in_specs=[INV] * 4,
        out_specs=[INV] * 3,
        scratch_shapes=[pltpu.VMEM((2 * rows, cols), bf16), pltpu.SemaphoreType.DMA((2, 16))],
        compiler_params=pltpu.CompilerParams(collective_id=2, has_side_effects=True, vmem_limit_bytes=20 * MIB),
    )(z4, out_mine, out_theirs, gate)


def scan_body(sign, s_ref, o_ref, stage, here, whole, zhere, back, bhere, sems):
    me = lax.axis_index("tok")
    z, plane = me // 8, (me // 2) % 4
    barrier = pltpu.get_barrier_semaphore()
    for k in (1, 2, 3):
        for to in (across(me, 2 * k), lax.rem(me + 8 * k, 32)):
            pl.semaphore_signal(barrier, inc=1, device_id=(to,), device_id_type=MESH)
    pl.semaphore_wait(barrier, 6)

    def slot(k):
        return (across(me, 2 * k) // 2) % 4

    def copy(source, target, sem, i, to):
        return pltpu.make_async_remote_copy(
            src_ref=source,
            dst_ref=target,
            send_sem=sems.at[sem, 0, i],
            recv_sem=sems.at[sem, 1, i],
            device_id=(to,),
            device_id_type=MESH,
        )

    def receives(k):
        return z - k >= 0 if sign > 0 else z + k < 4

    def sends(k):
        return z + k < 4 if sign > 0 else z - k >= 0

    copies = []
    for k in (3, 1, 2):
        stage[k - 1] = s_ref[pl.ds(2 * slot(k), 2)].astype(stage.dtype)
        copies.append(copy(stage.at[k - 1], here.at[k - 1], 0, k - 1, across(me, 2 * k)))
        copies[-1].start()
    mine = [s_ref[pl.ds(2 * plane, 2)]]
    for c in copies:
        c.wait()
    mine += [here[k - 1].astype(f32) for k in (1, 2, 3)]
    whole[...] = sum(mine).astype(whole.dtype)
    for k in (2, 1, 3):

        @pl.when(sends(k))
        def _(k=k):
            copy(whole, zhere.at[k - 1], 1, k - 1, me + 8 * k * sign).start()

    for k in (1, 2, 3):

        @pl.when(receives(k))
        def _(k=k):
            copy(whole, zhere.at[k - 1], 1, k - 1, me).wait_recv()

        @pl.when(jnp.logical_not(receives(k)))
        def _(k=k):
            zhere[k - 1] = jnp.zeros_like(whole)

    for k in (1, 2, 3):

        @pl.when(sends(k))
        def _(k=k):
            copy(whole, zhere.at[k - 1], 1, k - 1, me).wait_send()

    beyond = sum(zhere[k].astype(f32) for k in range(3))
    copies = []
    for k in (3, 1, 2, 0):
        before = beyond
        for j in range(4):
            if j != k:
                before = before + (sign * (slot(k) - slot(j)) > 0).astype(f32) * mine[j]
        if k == 0:
            o_ref[pl.ds(2 * plane, 2)] = before
        else:
            back[k - 1] = before.astype(back.dtype)
            copies.append(copy(back.at[k - 1], bhere.at[k - 1], 2, k - 1, across(me, 2 * k)))
            copies[-1].start()
    for c in copies:
        c.wait()
    for k in (1, 2, 3):
        o_ref[pl.ds(2 * slot(k), 2)] = bhere[k - 1].astype(f32)


def spans_of(cols, most=512):
    return [(s, min(most, cols - s)) for s in range(0, cols, most)]


def ffn_body(order, sides, x_ref, g_ref, *refs):
    gates, ups, downs = refs[0:4], refs[4:8], refs[8:11]
    y_ref, act_ref, d_ref, dh_ref, w_gate_up, w_down, sem = refs[11:]
    cols = w_down.shape[0]

    @pl.when(pl.program_id(0) == 0)
    def _():
        size, part, rest = downs[0].shape[0], downs[1].shape[1], downs[2].shape[1]
        far = pl.ds(pl.multiple_of((1 - sides[4]) * size, 16), size)
        targets = [
            w_down.at[pl.ds(pl.multiple_of(sides[4] * size, 16), size)],
            w_down.at[far, pl.ds(0, part)],
            w_down.at[far, pl.ds(part, rest)],
        ]
        copies = [pltpu.make_async_copy(a, b, sem.at[i]) for i, (a, b) in enumerate(zip(downs, targets))]
        size = gates[0].shape[1]
        for j, pieces in enumerate((gates, ups)):
            for k, piece in enumerate(pieces):
                for i, at in enumerate(order):
                    rows = pl.ds(pl.multiple_of((at + sides[k]) * size, 16), size)
                    target = w_gate_up.at[rows, pl.ds(j * cols, cols)]
                    copies.append(pltpu.make_async_copy(piece.at[i], target, sem.at[len(copies)]))
        for copy in copies:
            copy.start()
        for copy in copies:
            copy.wait()

    x, g = x_ref[...], g_ref[...]
    for s, w in spans_of(cols):
        gate, upper = dot(x, w_gate_up[:, s : s + w]), dot(x, w_gate_up[:, cols + s : cols + s + w])
        d_act = dot_cols(g, w_down[s : s + w, :])
        sigma = jax.nn.sigmoid(gate)
        smooth = gate * sigma
        act_ref[:, s : s + w] = (smooth * upper).astype(bf16)
        d_ref[:, s : s + w] = (d_act * upper * sigma * (1.0 + gate * (1.0 - sigma))).astype(bf16)
        d_ref[:, cols + s : cols + s + w] = (d_act * smooth).astype(bf16)
    y_ref[...] = dot(act_ref[...], w_down[...]).astype(bf16)
    dh_ref[...] = dot_cols(d_ref[...], w_gate_up[...]).astype(bf16)


def ffn(x, g, gate, up, down, order, sides, tile=256):
    tokens, width = x.shape
    cols = 2 * down[0].shape[0]

    def block(w):
        return pl.BlockSpec((tile, w), lambda i: (i, 0))

    return pl.pallas_call(
        lambda *refs: ffn_body(order, *refs),
        out_shape=[jax.ShapeDtypeStruct((tokens, w), bf16) for w in (width, cols, 2 * cols, width)],
        grid=(tokens // tile,),
        in_specs=[pl.BlockSpec(memory_space=pltpu.SMEM), block(width), block(width)] + [pl.BlockSpec(memory_space=pl.ANY)] * 11,
        out_specs=[block(width), block(cols), block(2 * cols), block(width)],
        scratch_shapes=[
            pltpu.VMEM((width, 2 * cols), bf16),
            pltpu.VMEM((cols, width), bf16),
            pltpu.SemaphoreType.DMA((8 * len(order) + 3,)),
        ],
        compiler_params=pltpu.CompilerParams(vmem_limit_bytes=48 * MIB),
        cost_estimate=pl.CostEstimate(flops=0, bytes_accessed=0, transcendentals=0),
    )(sides, x, g, *gate, *up, *down)


def product_body(count, group, index, *refs):
    left, right, out = refs[: count * group], refs[count * group : count * (group + 1)], refs[-1]
    acc = 0.0
    for i in range(count):
        rows = jnp.concatenate([a[...] for a in left[i * group : (i + 1) * group]], axis=1)
        acc = acc + dot_rows(rows, right[i][...])
    out[...] = acc.astype(out.dtype)


def row_blocks(left, right, index, size, half=None, deps=()):
    count = index.shape[0]
    group = 4 if count % 4 == 0 else 1
    cols = right[0].shape[1] // (1 if half is None else 2)
    at_col = half or 0

    def block(tokens, j):
        return pl.BlockSpec((tokens, size), lambda i, at: (0, at[i * group + j]))

    return pl.pallas_call(
        lambda *refs: product_body(len(left), group, *refs),
        out_shape=jax.ShapeDtypeStruct((count * size, cols), bf16),
        grid_spec=pltpu.PrefetchScalarGridSpec(
            num_scalar_prefetch=1,
            grid=(count // group,),
            in_specs=[block(a.shape[0], j) for a in left for j in range(group)]
            + [pl.BlockSpec((b.shape[0], cols), lambda i, at: (0, at_col)) for b in right]
            + [pl.BlockSpec(memory_space=pl.ANY)] * len(deps),
            out_specs=pl.BlockSpec((group * size, cols), lambda i, at: (i, 0)),
        ),
        compiler_params=pltpu.CompilerParams(vmem_limit_bytes=56 * MIB),
        cost_estimate=pl.CostEstimate(flops=0, bytes_accessed=0, transcendentals=0),
    )(index.astype(jnp.int32), *[a for a in left for _ in range(group)], *right, *deps)


def apart_body(places, padded, w_ref, out_ref):
    w = w_ref[...].astype(f32)
    unit = w.shape[1] // sum(len(p) for p in places)
    gap = [jnp.zeros((w.shape[0], padded - unit), f32)] if padded > unit else []
    for q, place in enumerate(places):
        blocks = []
        for d in place:
            blocks += [w[:, d * unit : (d + 1) * unit]] + gap
        out_ref[q] = jnp.concatenate(blocks, axis=1).astype(bf16)


def apart(w, places, padded):
    rows, cols = w.shape[0], len(places[0]) * padded
    return pl.pallas_call(
        lambda *refs: apart_body(places, padded, *refs),
        out_shape=jax.ShapeDtypeStruct((len(places), rows, cols), bf16),
        in_specs=[INV],
        out_specs=INV,
        compiler_params=pltpu.CompilerParams(vmem_limit_bytes=24 * MIB),
        cost_estimate=pl.CostEstimate(flops=0, bytes_accessed=0, transcendentals=0),
    )(w)


def together_body(places, padded, unit, member, *refs):
    pieces, outs, held = refs[:4], refs[4:6], refs[6]
    for k, piece in enumerate(pieces):
        held[k] = piece[...].astype(f32)
    cols = len(places[0]) * padded
    for j, out in enumerate(outs):
        blocks = {}
        for q, place in enumerate(places):
            for i, d in enumerate(place):
                at = j * cols + i * padded
                blocks[d] = held[member[0] ^ q][:, at : at + unit]
        out[...] = jnp.concatenate([blocks[d] for d in sorted(blocks)], axis=1)


def together(pieces, places, padded, unit, member):
    rows = pieces[0].shape[0]
    whole = jax.ShapeDtypeStruct((rows, unit * sum(len(p) for p in places)), f32)
    return pl.pallas_call(
        lambda *refs: together_body(places, padded, unit, *refs),
        out_shape=[whole, whole],
        in_specs=[pl.BlockSpec(memory_space=pltpu.SMEM)] + [INV] * 4,
        out_specs=[INV, INV],
        scratch_shapes=[pltpu.VMEM((4,) + pieces[0].shape, f32)],
        compiler_params=pltpu.CompilerParams(vmem_limit_bytes=40 * MIB),
        cost_estimate=pl.CostEstimate(flops=0, bytes_accessed=0, transcendentals=0),
    )(jnp.reshape(member, (1,)).astype(jnp.int32), *pieces)


def wide_body(d_ref, w_ref, out_ref):
    out_ref[...] = dot_cols(d_ref[...], w_ref[...]).astype(bf16)


def times_transposed(d, w, tile=256):
    return pl.pallas_call(
        wide_body,
        out_shape=jax.ShapeDtypeStruct((d.shape[0], w.shape[0]), bf16),
        grid=(d.shape[0] // tile,),
        in_specs=[
            pl.BlockSpec((tile, d.shape[1]), lambda i: (i, 0)),
            pl.BlockSpec(w.shape, lambda i: (0, 0)),
        ],
        out_specs=pl.BlockSpec((tile, w.shape[0]), lambda i: (i, 0)),
        compiler_params=pltpu.CompilerParams(vmem_limit_bytes=48 * MIB),
        cost_estimate=pl.CostEstimate(flops=0, bytes_accessed=0, transcendentals=0),
    )(d, w)


def part_maker(left, right, bits, within=(0,), half=None):
    n = lax.axis_size("tok")
    size = left[0].shape[1] * 2 // n
    cols = right[0].shape[1] // (1 if half is None else 2)
    ids = np.asarray([(at + more) // 2 for at in grown(bits[:-1][::-1]) for more in within], np.int32)

    def make(index, *deps):
        index = jnp.asarray(ids) + index * (bits[-1] // 2)
        if size % 128 == 0:
            out = row_blocks(left, right, index, size, half, deps)
        else:
            out = sum(dot_rows(a, b) for a, b in zip(left, right)).astype(bf16).reshape(n // 2, size, -1)
            out = out[index][..., (half or 0) * cols : (half or 0) * cols + cols]
        return out.reshape(-1, size * len(within), cols)

    return make


def feature_tables(heads):
    pairs = [(a, b) for a in range(QK + 1) for b in range(a, QK + 1)]
    one = np.zeros((heads, heads * QK, FEATS), np.float32)
    two = np.zeros((heads, heads * QK, FEATS), np.float32)
    rows = np.zeros((8, FEATS), np.float32)
    for f, (a, b) in enumerate(pairs):
        for h in range(heads):
            if a < QK:
                one[h, h * QK + a, f] = 1
            if b < QK:
                two[h, h * QK + b, f] = 1
        rows[0, f] = a == QK
        rows[1, f] = b == QK
        if a == QK:
            rows[2, f] = 1.0
        elif b == QK:
            rows[2, f] = QK**-0.5
        else:
            rows[2, f] = (0.5 if a == b else 1.0) / QK
    return jnp.asarray(one, bf16), jnp.asarray(two, bf16), jnp.asarray(rows)


def dot(a, b):
    return lax.dot_general(a, b, (((1,), (0,)), ((), ())), preferred_element_type=f32)


def dot_rows(a, b):
    return lax.dot_general(a, b, (((0,), (0,)), ((), ())), preferred_element_type=f32)


def dot_cols(a, b):
    return lax.dot_general(a, b, (((1,), (1,)), ((), ())), preferred_element_type=f32)


def halves(x):
    high = x.astype(bf16)
    return high, (x - high.astype(f32)).astype(bf16)


def features(x, one, two, rows):
    return dot(x, one) + rows[0:1], dot(x, two) + rows[1:2]


def total_row(state):
    return jnp.concatenate([state[FEATS : FEATS + 1], state[FEATS + 1 : FEATS + 2, : FEATS - 128]], axis=1)


def store_state(ref, state, row):
    ref[0, 0, :FEATS, :] = state
    ref[0, 0, FEATS:, :] = jnp.zeros((ROWS - FEATS, state.shape[1]), f32)
    ref[0, 0, FEATS : FEATS + 1, :] = row[:, :128]
    ref[0, 0, FEATS + 1 : FEATS + 2, : FEATS - 128] = row[:, 128:]


def kept_rows(scal, tile, tokens):
    index = lax.broadcasted_iota(jnp.int32, (tokens, 1), 0) + tile * tokens
    return index >= scal[tile]


def state_body(scal, k_ref, v_ref, one, two, rows, out_ref):
    tile = pl.program_id(0)
    a, b = features(k_ref[...], one[0], two[0], rows)
    phi = jnp.where(kept_rows(scal, tile, a.shape[0]), a * b, 0.0)
    high, low = halves(phi)
    v = v_ref[...]
    store_state(out_ref, dot_rows(high, v) + dot_rows(low, v), jnp.sum(phi, axis=0, keepdims=True))


def weights(q_ref, k_ref, lo_ref, tile, head):
    tokens, lanes = q_ref.shape
    lane = lax.broadcasted_iota(jnp.int32, (tokens, lanes), 1) // QK == head
    q = jnp.where(lane, q_ref[...], jnp.zeros((), bf16))
    lo = lo_ref[...] - tile * tokens
    parts = []
    for start in (0, tokens // 2):
        end = start + tokens // 2
        score = dot_cols(q[start:end], k_ref[:end]) * QK**-0.5
        row = lax.broadcasted_iota(jnp.int32, score.shape, 0) + start
        col = lax.broadcasted_iota(jnp.int32, score.shape, 1)
        mask = (col <= row) & (col >= lo[start:end])
        parts.append((start, end, score, mask, jnp.where(mask, 1.0 + score + 0.5 * score * score, 0.0)))
    return lane, parts, lo < 0


def over_halves(first, second):
    size = first.shape[0]
    return jnp.concatenate([first + second[:size], second[size:]], axis=0)


def forward_body(q_ref, k_ref, v_ref, lo_ref, carry_ref, one, two, rows, y_ref, mixed_ref):
    tile, head = pl.program_id(0), pl.program_id(1)
    _, parts, alive = weights(q_ref, k_ref, lo_ref, tile, head)
    a, b = features(q_ref[...], one[0], two[0], rows)
    phi = jnp.where(alive, a * b * rows[2:3], 0.0)
    high, low = halves(phi)
    carry = carry_ref[0, 0]
    s_high, s_low = halves(carry[:FEATS])
    numer = jnp.concatenate([dot(weight.astype(bf16), v_ref[:end]) for _, end, _, _, weight in parts], axis=0)
    numer = numer + (dot(high, s_high) + dot(high, s_low) + dot(low, s_high))
    denom = jnp.concatenate([jnp.sum(part[4], axis=1, keepdims=True) for part in parts], axis=0)
    denom = denom + jnp.sum(phi * total_row(carry), axis=1, keepdims=True)
    y = numer / denom
    y_ref[...] = y
    mixed_ref[...] = y.astype(bf16)


def spread(t, a, b, one, two):
    first_high, first_low = halves(t * b)
    second_high, second_low = halves(t * a)
    return (
        dot_cols(first_high, one) + dot_cols(first_low, one) + dot_cols(second_high, two) + dot_cols(second_low, two)
    )


def backward_body(
    q_ref, k_ref, v_ref, lo_ref, carry_ref, one, two, rows, y_ref, d_ref, dq_ref, dk_ref, dv_ref, ds_ref, dq_acc, dk_acc
):
    tile, head = pl.program_id(0), pl.program_id(1)
    lane, parts, alive = weights(q_ref, k_ref, lo_ref, tile, head)
    a, b = features(q_ref[...], one[0], two[0], rows)
    phi = jnp.where(alive, a * b * rows[2:3], 0.0)
    high, low = halves(phi)
    carry = carry_ref[0, 0]
    s_high, s_low = halves(carry[:FEATS])
    row = total_row(carry)
    denom = jnp.concatenate([jnp.sum(part[4], axis=1, keepdims=True) for part in parts], axis=0)
    denom = denom + jnp.sum(phi * row, axis=1, keepdims=True)
    d = d_ref[...].astype(f32)
    g = d / denom
    c = -jnp.sum(d * y_ref[...], axis=1, keepdims=True) / denom
    g_high, g_low = halves(g)
    dq, dkeys, dv = [], [], []
    for start, end, score, mask, weight in parts:
        v = v_ref[:end]
        dk = dot_cols(g_high[start:end], v) + dot_cols(g_low[start:end], v) + c[start:end]
        ds = jnp.where(mask, dk * (1.0 + score) * QK**-0.5, 0.0).astype(bf16)
        dv.append(dot_rows(weight.astype(bf16), g_high[start:end]))
        dq.append(dot(ds, k_ref[:end]))
        dkeys.append(dot_rows(ds, q_ref[start:end]))
    dv_ref[...] = over_halves(*dv)
    dphi = dot_cols(g_high, s_high) + dot_cols(g_high, s_low) + dot_cols(g_low, s_high) + c * row
    t = jnp.where(alive, dphi * rows[2:3], 0.0)
    dq = jnp.where(lane, jnp.concatenate(dq, axis=0), 0.0) + spread(t, a, b, one[0], two[0])
    dkeys = jnp.where(lane, over_halves(*dkeys), 0.0)

    @pl.when(head == 0)
    def _():
        dq_acc[...] = dq
        dk_acc[...] = dkeys

    @pl.when(head > 0)
    def _():
        dq_acc[...] += dq
        dk_acc[...] += dkeys

    @pl.when(head == pl.num_programs(1) - 1)
    def _():
        dq_ref[...] = dq_acc[...].astype(bf16)
        dk_ref[...] = dk_acc[...]

    state = dot_rows(high, g_high) + dot_rows(high, g_low) + dot_rows(low, g_high)
    store_state(ds_ref, state, jnp.sum(phi * c, axis=0, keepdims=True))


def carried_body(scal, k_ref, v_ref, one, two, rows, grad_ref, dk_in, dv_in, dk_ref, dv_ref, acc):
    tile, head = pl.program_id(0), pl.program_id(1)
    a, b = features(k_ref[...], one[0], two[0], rows)
    keep = kept_rows(scal, tile, a.shape[0])
    high, low = halves(jnp.where(keep, a * b, 0.0))
    grad = grad_ref[0, 0]
    g_high, g_low = halves(grad[:FEATS])
    v = v_ref[...]
    dv = dv_in[...] + dot(high, g_high) + dot(high, g_low) + dot(low, g_high)
    dv_ref[...] = dv.astype(bf16)
    t = jnp.where(keep, dot_cols(v, g_high) + dot_cols(v, g_low) + total_row(grad), 0.0)
    dk = spread(t, a, b, one[0], two[0])

    @pl.when(head == 0)
    def _():
        acc[...] = dk_in[...] + dk

    @pl.when(head > 0)
    def _():
        acc[...] += dk

    @pl.when(head == pl.num_programs(1) - 1)
    def _():
        dk_ref[...] = acc[...].astype(bf16)


class Attention:
    def __init__(self, qkv, lo, heads, tokens):
        self.qkv, self.heads, self.tokens = qkv, heads, tokens
        self.lo = lo[:, None]
        self.scal = jnp.stack([lo[tokens - 1], lo[2 * tokens - 1]])
        self.tables = feature_tables(heads)
        lanes = heads * QK
        self.value = (qkv.shape[1] - 2 * lanes) // heads
        skip = 2 * lanes // self.value
        self.q = pl.BlockSpec((tokens, lanes), lambda t, h: (t, 0))
        self.k = pl.BlockSpec((tokens, lanes), lambda t, h: (t, 1))
        self.v = pl.BlockSpec((tokens, self.value), lambda t, h: (t, h + skip))
        self.o = pl.BlockSpec((tokens, self.value), lambda t, h: (t, h))
        self.l = pl.BlockSpec((tokens, 1), lambda t, h: (t, 0))
        self.s = pl.BlockSpec((1, 1, ROWS, self.value), lambda t, h: (h, t, 0, 0))
        self.e = pl.BlockSpec((1, lanes, FEATS), lambda t, h: (h, 0, 0))
        self.r = pl.BlockSpec((8, FEATS), lambda t, h: (0, 0))
        self.m = pl.BlockSpec(memory_space=pltpu.SMEM)
        self.table_specs = [self.e, self.e, self.r]
        self.acc = pltpu.VMEM((tokens, lanes), f32)
        self.state_shape = jax.ShapeDtypeStruct((heads, 2, ROWS, self.value), f32)

    def wide(self, kind):
        return jax.ShapeDtypeStruct((2 * self.tokens, self.heads * self.value), kind)

    def narrow(self, kind):
        return jax.ShapeDtypeStruct((2 * self.tokens, self.heads * QK), kind)

    def call(self, body, ins, outs, shapes, scratch, limit, args):
        return pl.pallas_call(
            body,
            grid=(2, self.heads),
            in_specs=ins,
            out_specs=outs,
            out_shape=shapes,
            scratch_shapes=scratch,
            compiler_params=pltpu.CompilerParams(vmem_limit_bytes=limit * MIB),
            cost_estimate=pl.CostEstimate(flops=0, bytes_accessed=0, transcendentals=0),
        )(*args)

    def states(self):
        (out,) = self.call(
            state_body,
            [self.m, self.k, self.v] + self.table_specs,
            [self.s],
            [self.state_shape],
            [],
            24,
            (self.scal, self.qkv, self.qkv, *self.tables),
        )
        return out

    def forward(self, carry):
        return self.call(
            forward_body,
            [self.q, self.k, self.v, self.l, self.s] + self.table_specs,
            [self.o, self.o],
            [self.wide(f32), self.wide(bf16)],
            [],
            48,
            (self.qkv, self.qkv, self.qkv, self.lo, carry, *self.tables),
        )

    def backward(self, carry, y, d_heads):
        return self.call(
            backward_body,
            [self.q, self.k, self.v, self.l, self.s] + self.table_specs + [self.o, self.o],
            [self.q, self.q, self.o, self.s],
            [self.narrow(bf16), self.narrow(f32), self.wide(f32), self.state_shape],
            [self.acc, self.acc],
            48,
            (self.qkv, self.qkv, self.qkv, self.lo, carry, *self.tables, y, d_heads),
        )

    def carried(self, grad, dk, dv):
        return self.call(
            carried_body,
            [self.m, self.k, self.v] + self.table_specs + [self.s, self.q, self.o],
            [self.q, self.o],
            [self.narrow(bf16), self.wide(bf16)],
            [self.acc],
            48,
            (self.scal, self.qkv, self.qkv, *self.tables, grad, dk, dv),
        )


def others(state, earlier, kind):
    n = lax.axis_size("tok")
    me = lax.axis_index("tok")
    sign = 1 if earlier else -1
    if n != 32:
        parts = lax.all_gather(state.astype(kind), "tok").astype(f32)
        index = jnp.arange(n)
        before = (sign * (me // 2 - index // 2) > 0) & (index % 2 == me % 2)
        out = jnp.sum(jnp.where(before.reshape((n,) + (1,) * state.ndim), parts, 0.0), axis=0)
        return out
    block = (state.shape[0] // 4,) + state.shape[1:]
    slots = pltpu.VMEM((3,) + block, kind)
    return pl.pallas_call(
        lambda *refs: scan_body(sign, *refs),
        out_shape=jax.ShapeDtypeStruct(state.shape, f32),
        in_specs=[INV],
        out_specs=INV,
        scratch_shapes=[slots, slots, pltpu.VMEM(block, kind), slots, slots, slots, pltpu.SemaphoreType.DMA((3, 2, 3))],
        compiler_params=pltpu.CompilerParams(
            collective_id=3 if earlier else 4, has_side_effects=True, vmem_limit_bytes=16 * MIB
        ),
        cost_estimate=pl.CostEstimate(flops=0, bytes_accessed=0, transcendentals=0),
    )(state)


def row_starts(positions, lengths, offsets):
    inside = (positions[:, None] >= offsets[None, :]) & (positions[:, None] < offsets[None, :] + lengths[None, :])
    return jnp.sum(jnp.where(inside, offsets[None, :], 0), axis=1)


def side_by_side(core, mine, theirs, axis=0):
    size = mine.shape[axis]
    shape = list(mine.shape)
    shape[axis] *= 2
    out = jnp.zeros(shape, mine.dtype)
    out = lax.dynamic_update_slice_in_dim(out, mine, core * size, axis)
    return lax.dynamic_update_slice_in_dim(out, theirs, (1 - core) * size, axis)


def shards(
    block_input,
    lengths,
    offsets,
    norm1_gain,
    w_query,
    w_key,
    w_value,
    w_out,
    norm2_gain,
    w_gate,
    w_up,
    w_down,
    out_grad,
):
    n = lax.axis_size("tok")
    me = lax.axis_index("tok")
    core, member = me % 2, side(PAIR) * 2 + me % 2
    cbits = bits_from(n, 2)
    qbits = [bit for bit in cbits if bit != PAIR]
    swapped = qbits[:-2] + [qbits[-1], qbits[-2]]
    chips, quads = n // 2, n // 4
    above, below = n // (2 * PAIR), PAIR // 2
    groups = [
        [i * 2 * PAIR + p * PAIR + j * 2 + c for i in range(above) for j in range(below)] for p in (0, 1) for c in (0, 1)
    ]
    to_member = {1: 1, 2: PAIR, 3: PAIR + 1}
    tokens, width = block_input.shape
    rows = w_query.shape[0]
    heads = w_query.shape[1] // QK // 2
    half = width // 2
    lanes = heads * QK
    def column_half(w, which):
        return lax.dynamic_slice_in_dim(w, which * (w.shape[1] // 2), w.shape[1] // 2, 1)

    def row_half(w, which):
        return lax.dynamic_slice_in_dim(w, which * (w.shape[0] // 2), w.shape[0] // 2, 0)

    unit = w_down.shape[0]
    padded = -(-unit // 16) * 16
    cols = quads * padded

    gate, up = apart(w_gate, groups, padded), apart(w_up, groups, padded)
    down = jnp.pad(w_down, ((0, padded - unit), (0, 0)))
    near_grad = side_by_side(core, out_grad, flip(out_grad, 1))

    def by_core(which):
        return jnp.concatenate([column_half(w, which) for w in (w_query, w_key, w_value)], axis=1)

    gains = jnp.stack([norm1_gain, norm2_gain]).astype(f32)
    if n == 32:
        gains = jnp.pad(gains, ((0, 6), (0, 128 - rows)))[None]
        gains = after(gains, near_grad)
        gains, gate, up, qkv_all, down = spread_first(gains, gate, up, by_core(core), by_core(1 - core), down)
        gains = gains[:, :2, :rows].transpose(1, 0, 2).reshape(2, 1, width)
        z4 = qkv_all
        qkv_all, out_half, gate = spread_second(z4, column_half(w_out, core), column_half(w_out, 1 - core), gate)
        qkv_all = qkv_all.reshape(width, -1)
    else:

        def to_group(x):
            pieces = [(member, pick(x, member))]
            for k in range(1, 4):
                pieces.append((member ^ k, flip(pick(x, member ^ k), to_member[k])))
            return assemble_all(pieces)

        gate, up = to_group(gate), to_group(up)
        qkv_all = side_by_side(core, by_core(core), flip(by_core(1 - core), 1))
        gains = grow(gains, 1)
        for bit in cbits:
            gains, qkv_all = grow(gains, bit), grow(qkv_all, bit)
        gains = in_order(gains, [1] + cbits).transpose(1, 0, 2).reshape(2, 1, width)
        qkv_all = in_order(qkv_all, cbits).reshape(width, -1)
        out_half = side_by_side(core, column_half(w_out, core), flip(column_half(w_out, 1 - core), 1))
        for bit in cbits[:-2]:
            out_half = grow(out_half, bit)
        out_half = in_order(out_half, cbits[:-2])
        gate = grow(gate, qbits[0])
        for bit in qbits[1:]:
            down = grow(down, bit)
        down = in_order(down, qbits[1:])
    gain_one, gain_two = gains[0], gains[1]

    inputs32 = block_input.astype(f32)
    ratio_one = lax.rsqrt(jnp.mean(inputs32 * inputs32, axis=1, keepdims=True) + eps)
    normed_one = inputs32 * ratio_one
    hidden_one = (normed_one * gain_one).astype(bf16)
    hidden_chip = side_by_side(core, hidden_one, move(hidden_one, 1, (), (qkv_all,)))
    qkv = dot(hidden_chip, qkv_all).astype(bf16)

    first = (me // 2) * 2 * tokens
    positions = first + jnp.arange(2 * tokens, dtype=jnp.int32)
    lo = row_starts(positions, lengths, offsets) - first
    attention = Attention(qkv, lo, heads, tokens)
    states = attention.states()
    fresh0 = (lo[tokens - 1] >= 0).astype(f32)
    fresh1 = (lo[2 * tokens - 1] >= tokens).astype(f32)

    start, stop = (qkv_all,), (states,)
    for bit in qbits[1:-2]:
        gate = grow(gate, bit)
    gate_x = move(gate, 2, start, stop)
    up = grow(up, qbits[0], start, stop)
    for bit in qbits[1:-2]:
        up = grow(up, bit)
    out_y = move(out_half, 4, start, stop)
    leaving = states[:, 1] + (1.0 - fresh1) * states[:, 0]
    leaving, gate_x, up, out_y = lax.optimization_barrier((leaving, gate_x, up, out_y))
    entering = others(leaving, True, f32)
    start, stop = (leaving,), (entering,)
    down = down.reshape(cols // 2, width)
    down_a, down_b = down[:, : width * 3 // 4], down[:, width * 3 // 4 :]
    out_both = jnp.stack([out_half, out_y])
    gate_up = jnp.concatenate([gate, up], axis=-1)
    flows = [(out_both, 2), (gate_up, 4), (up, 2), (down_a, qbits[0]), (out_grad, PAIR)]
    flows = [move(w, bit, start, stop) for w, bit in flows]
    entering, out_x, gate_up, up_x, down_a, far_grad = lax.optimization_barrier((entering, *flows))
    gate_y, up_y = gate_up[..., :cols], gate_up[..., cols:]
    carry = jnp.stack([entering, states[:, 0] + (1.0 - fresh0) * entering], axis=1)
    place = (me // 2) % 4
    out_pieces = [(place, out_half), (place ^ 1, out_x[0]), (place ^ 2, out_y), (place ^ 3, out_x[1])]
    out_half = jnp.zeros((chips // 4, 4, 2 * rows, half), bf16)
    for index, piece in out_pieces:
        out_half = lax.dynamic_update_index_in_dim(out_half, piece, index, 1)
    out_half = out_half.reshape(width, half)
    carry = after(carry, out_half)
    y_heads, mixed_heads = attention.forward(carry)
    start, stop = (carry,), (mixed_heads,)
    flows = [move(w, bit, start, stop) for w, bit in [(gate_x, 4), (up_y, 2), (down_b, qbits[0])]]
    out_there = move(out_half, 1, start, stop)
    mixed_heads, out_there, *flows = lax.optimization_barrier((mixed_heads, out_there, *flows))
    gate_xy, up_xy, down_b = flows
    down = [down, down_a, down_b]
    out_all = side_by_side(core, out_half, out_there, 1)
    mixed_chip = side_by_side(core, mixed_heads, flip(mixed_heads, 1), 1)
    middle = inputs32 + dot(row_half(mixed_chip, core), out_all)
    ratio_two = lax.rsqrt(jnp.mean(middle * middle, axis=1, keepdims=True) + eps)
    normed_two = middle * ratio_two
    hidden_two = (normed_two * gain_two).astype(bf16)

    far_hidden = flip(hidden_two, PAIR)
    near_hidden = side_by_side(core, hidden_two, flip(hidden_two, 1))
    gate = [w.reshape(-1, 2 * rows, cols) for w in (gate, gate_x, gate_y, gate_xy)]
    up = [w.reshape(-1, 2 * rows, cols) for w in (up, up_x, up_y, up_xy)]
    order = [(at + more) // 2 for at in grown(qbits[:-2]) for more in (0, PAIR)]
    sides = jnp.stack([place, place ^ 1, place ^ 2, place ^ 3, side(qbits[0])])
    near = ffn(near_hidden, near_grad, gate, up, down, order, sides)
    far_hidden, far_there = after(far_hidden, *near), move(far_grad, 1, (near_hidden,), (near[0],))
    far_grad = side_by_side(core, far_grad, far_there)
    far_hidden = side_by_side(core, far_hidden, flip(far_hidden, 1))
    far = ffn(far_hidden, far_grad, gate, up, down, order, sides)
    start, stop = (near[0], far_hidden), (far[0],)
    near_parts = [move(row_half(near[i], 1 - core), 1, start, stop) for i in (3, 0)]
    far, near_parts = lax.optimization_barrier((far, near_parts))

    right = [near[2], far[2]]
    sum_gate = Scatter(part_maker([near_hidden, far_hidden], right, qbits, (0, PAIR), 0), qbits)
    sum_gate.send()
    start, stop = (far[0],), (sum_gate.sent,)
    far_parts = [move(row_half(far[i], 1 - core), 1, start, stop) for i in (3, 0)]
    sent, far_parts = lax.optimization_barrier((sum_gate.sent, far_parts))
    d_far = (row_half(far[3], core).astype(f32) + far_parts[0].astype(f32)).astype(bf16)
    y_far = (row_half(far[0], core).astype(f32) + far_parts[1].astype(f32)).astype(bf16)
    sum_up = Scatter(part_maker([near_hidden, far_hidden], right, swapped, (0, PAIR), 1), swapped)
    sum_up.send(sent, d_far, y_far)
    sum_gate.keep(sum_up.sent)
    sum_up.keep(sum_gate.kept)
    term = row_blocks([near[1], far[1]], [near_grad, far_grad], jnp.arange(cols // 128), 128, None, (sum_up.kept,))
    d_far = move(d_far, PAIR, (), (term,))
    d_far = sum_gate.hold(d_far, term)
    near_parts = after(near_parts, d_far)
    d_near = row_half(near[3], core).astype(f32) + near_parts[0].astype(f32)
    y_near = row_half(near[0], core).astype(f32) + near_parts[1].astype(f32)
    d_hidden_two = d_near + d_far.astype(f32)
    term_norm_two = jnp.sum(d_hidden_two * normed_two, axis=0)
    scaled_two = d_hidden_two * gain_two
    d_middle = out_grad.astype(f32) + ratio_two * (
        scaled_two - normed_two * jnp.mean(scaled_two * normed_two, axis=1, keepdims=True)
    )
    d_mixed = d_middle.astype(bf16)
    d_mixed_chip = side_by_side(core, d_mixed, flip(d_mixed, 1))
    d_heads = dot_cols(d_mixed_chip, row_half(out_all, core)).astype(bf16)

    d_heads = sum_up.hold(d_heads, d_mixed)
    d_heads = after(d_heads, sum_gate.step(), sum_up.step())
    dq, dk, dv, d_states = attention.backward(carry, y_heads, d_heads)
    flows = (sum_gate.here, sum_up.here, move(y_far, PAIR, (d_heads,)))
    flows = [after(flow, d_states) for flow in flows]
    d_states, sum_gate.here, sum_up.here, y_far = lax.optimization_barrier((d_states, *flows))
    sum_both = join([sum_gate, sum_up])
    sent = [sum_both.step()]

    def down_x(index, *_):
        return pick(term.reshape(quads // 2, 2, padded, width)[..., :half], index, 1)

    def down_y(index, *_):
        return pick(term.reshape(quads // 4, 2, 2, padded, width)[..., half:], index, 1).reshape(-1, padded, half)

    sum_down = [Scatter(down_x, qbits), Scatter(down_y, swapped)]
    for part in sum_down:
        part.send(d_states)
        part.keep()
    sent += [part.sent for part in sum_down]
    d_mixed_half = column_half(d_mixed_chip, core)
    out_sums = []
    for h, bits in ((0, cbits), (1, cbits[:-2] + [cbits[-1], cbits[-2]])):
        out_sums.append(Scatter(part_maker([after(mixed_chip, *sent)], [d_mixed_half], bits, (0,), h), bits))
        out_sums[-1].send()
    leaving = d_states[:, 0] + (1.0 - fresh0) * d_states[:, 1]
    leaving = others(after(leaving, *(part.sent for part in out_sums)), False, bf16)
    for part in out_sums:
        leaving = after(leaving, part.keep(leaving))
    for part in [sum_both] + sum_down + out_sums:
        leaving = part.hold(leaving, leaving)
    leaving = after(leaving, *(part.step() for part in sum_down + out_sums))
    d_states = jnp.stack([d_states[:, 1] + (1.0 - fresh1) * leaving, leaving], axis=1)
    dk, dv = attention.carried(d_states, dk, dv)
    for part in out_sums + sum_down:
        dk = part.hold(dk, dk)
    sum_down = join(sum_down)
    dk = after(dk, sum_down.step())
    d_qkv = jnp.concatenate([dq, dk, dv], axis=1)

    cut = d_qkv.shape[1] // 2
    sums = []
    for h, bits in ((0, cbits), (1, cbits[:-2] + [cbits[-1], cbits[-2]])):
        sums.append(Scatter(part_maker([hidden_chip], [d_qkv], bits, (0,), h), bits))
        sums[-1].send(*(p.sent for p in sums[:-1]))
    start = tuple(part.sent for part in sums)
    for part in sums:
        part.keep(*start)
        start = (part.kept,)
    rest_out = join([part.gated(start) for part in out_sums])
    start = start + (rest_out.step(),)
    d_hidden_one = times_transposed(after(d_qkv, *start), qkv_all)
    for part in [sum_down, rest_out] + sums:
        d_hidden_one = part.hold(d_hidden_one, d_hidden_one)
    sent = [part.step() for part in sums]
    d_hidden_one = after(d_hidden_one, *sent)
    theirs = flip(row_half(d_hidden_one, 1 - core), 1)
    gate_sum = after(sum_both.finish(), *sent).astype(bf16).reshape(4, rows, 2 * cols)
    parts = [flip(after(pick(gate_sum, member ^ k), theirs), to_member[k]) for k in range(1, 4)]
    d_hidden_one = row_half(d_hidden_one, core).astype(f32) + theirs.astype(f32)
    term_norm_one = jnp.sum(d_hidden_one * normed_one, axis=0)
    scaled_one = d_hidden_one * gain_one
    mean_one = jnp.mean(scaled_one * normed_one, axis=1, keepdims=True)
    norms = jnp.stack([term_norm_one, term_norm_two])
    for part in sums:
        norms = part.hold(norms, theirs)
    norms, parts = lax.optimization_barrier((norms, parts))
    rest = join(sums)
    sent = [rest.step()] + [rest_out.step() for _ in rest_out.bits[1:]]
    norms = after(norms, *sent)
    norms = norms + flip(norms, 1)
    norms = norms + flip(norms, cbits[-1])
    norms = norms + flip(norms, cbits[-2])
    norms = norms + flip(norms, cbits[-3])
    norms = rest_out.hold(rest.hold(norms, norms), norms)
    while len(rest.bits) > 1:
        sent = [rest.step()]
    norms = after(norms, *sent)
    grad_gate, grad_up = together([pick(gate_sum, member), *parts], groups, padded, unit, member)
    for bit in cbits[:-3]:
        norms = norms + flip(norms, bit)
    norms = pick(norms.reshape(2, n, rows), me, 1)
    input_grad = d_middle + ratio_one * (after(scaled_one, *sent) - normed_one * mean_one)
    output = (after(middle, *sent) + y_near + y_far.astype(f32)).astype(bf16)
    grad_down = sum_down.finish()[:unit]
    rest.kept = jnp.concatenate([rest.kept, rest_out.kept], axis=2)
    rest.here = jnp.concatenate([rest.here, rest_out.here], axis=2)
    total = rest.step()
    mine, theirs = row_half(total, core), flip(row_half(total, 1 - core), 1)
    spans = [(0, lanes), (lanes, 2 * lanes), (2 * lanes, 2 * lanes + half), (2 * cut, 2 * cut + half)]
    grad_query, grad_key, grad_value, grad_out = (
        side_by_side(core, mine[:, a:b], theirs[:, a:b], 1) for a, b in spans
    )

    return (
        output,
        input_grad,
        norms[0],
        grad_query,
        grad_key,
        grad_value,
        grad_out,
        norms[1],
        grad_gate,
        grad_up,
        grad_down,
    )


def solution(mesh):
    return jax.shard_map(
        shards,
        mesh=mesh,
        in_specs=(
            P("tok", None),
            P(),
            P(),
            P("tok"),
            P("tok", None),
            P("tok", None),
            P("tok", None),
            P("tok", None),
            P("tok"),
            P("tok", None),
            P("tok", None),
            P("tok", None),
            P("tok", None),
        ),
        out_specs=(
            P("tok", None),
            P("tok", None),
            P("tok"),
            P("tok", None),
            P("tok", None),
            P("tok", None),
            P("tok", None),
            P("tok"),
            P("tok", None),
            P("tok", None),
            P("tok", None),
        ),
        check_vma=False,
    )
```

```python
import jax
import jax.numpy as jnp
import numpy as np
from jax import lax
from jax.experimental import pallas as pl
from jax.experimental.pallas import tpu as pltpu
from jax.sharding import PartitionSpec as P

QK = 16
PAIR = 8
FEATS = 160
ROWS = 168
MIB = 1024 * 1024
eps = 1e-06
f32 = jnp.float32
bf16 = jnp.bfloat16


def bits_from(n, low):
    bits = []
    while low < n:
        bits.insert(0, low)
        low *= 2
    return bits


def flip(x, bits):
    n = lax.axis_size("tok")
    return lax.ppermute(x, "tok", [(i, i ^ bits) for i in range(n)])


def side(bit):
    return (lax.axis_index("tok") // bit) % 2


def pick(x, index, axis=0):
    return lax.dynamic_index_in_dim(x, index, axis, False)


def assemble(pieces):
    out = jnp.broadcast_to(pieces[0][1][None], (len(pieces),) + pieces[0][1].shape)
    for index, block in pieces[1:]:
        out = lax.dynamic_update_index_in_dim(out, block, index, 0)
    return out


def assemble_all(pieces):
    out = jnp.zeros((len(pieces),) + pieces[0][1].shape, pieces[0][1].dtype)
    for index, block in pieces:
        out = lax.dynamic_update_index_in_dim(out, block, index, 0)
    return out


def after(x, *others):
    return lax.optimization_barrier((x,) + others)[0] if others else x


def move(x, bits, start=(), stop=()):
    return after(flip(after(x, *start), bits), *stop)


def grow(x, bit, start=(), stop=()):
    return assemble([(side(bit), x), (1 - side(bit), move(x, bit, start, stop))])


def in_order(x, bits):
    done = bits[::-1]
    axes = [done.index(b) for b in sorted(done, reverse=True)]
    x = x.transpose(axes + list(range(len(done), x.ndim)))
    return x.reshape((-1,) + x.shape[len(done) :])


def grown(bits):
    at = [0]
    for bit in bits[::-1]:
        at = [i + j for i in at for j in (0, bit)]
    return at


class Scatter:
    def __init__(self, make, bits):
        self.make, self.bits, self.bit = make, bits, bits[-1]

    def send(self, *start):
        self.sent = after(self.make(1 - side(self.bit), *start), *start)
        self.here = flip(self.sent, self.bit)

    def keep(self, *gate):
        self.kept = self.make(side(self.bit), *gate)
        return self.kept

    def gated(self, gate):
        self.here = after(self.here, *gate)
        return self

    def hold(self, x, *gate):
        x, self.here = lax.optimization_barrier((x, after(self.here, *gate)))
        return x

    def step(self, *gate):
        kept, here = self.kept, after(self.here, *gate)
        self.bits = self.bits[:-1]
        if not self.bits:
            return (kept.astype(f32) + here.astype(f32))[0]
        bit = self.bits[-1]

        def half(index):
            return sum(pick(a.reshape((-1, 2) + a.shape[1:]), index, 1).astype(f32) for a in (kept, here))

        self.sent = half(1 - side(bit)).astype(bf16)
        self.kept = half(side(bit))
        self.here = flip(self.sent, bit)
        return self.sent

    def finish(self, *gate):
        while len(self.bits) > 1:
            self.step(*gate)
        return self.step(*gate)


def join(both):
    out = Scatter(None, both[0].bits[:-1] + [0])
    out.kept = jnp.concatenate([part.kept for part in both], axis=2)
    out.here = jnp.concatenate([part.here for part in both], axis=2)
    return out


MESH = pl.DeviceIdType.MESH
INV = pl.BlockSpec(memory_space=pltpu.VMEM)


def across(me, bits):
    for bit in (1, 2, 4, 8, 16):
        if bits & bit:
            me = me + bit - 2 * bit * ((me // bit) % 2)
    return me


def meet(me, partners):
    barrier = pltpu.get_barrier_semaphore()
    for bits in partners:
        pl.semaphore_signal(barrier, inc=1, device_id=(across(me, bits),), device_id_type=MESH)
    pl.semaphore_wait(barrier, len(partners))


class Mail:
    def __init__(self, me, sems):
        self.me, self.sems, self.count, self.open = me, sems, 0, []
    def send(self, source, target, bits):
        at = self.count
        self.count += 1
        copy = pltpu.make_async_remote_copy(src_ref=source, dst_ref=target, send_sem=self.sems.at[0, at],
            recv_sem=self.sems.at[1, at], device_id=(across(self.me, bits),), device_id_type=MESH)
        copy.start()
        self.open.append(copy)
        return copy
    def local(self, source, target):
        at = self.count
        self.count += 1
        copy = pltpu.make_async_copy(source, target, self.sems.at[0, at])
        copy.start()
        return copy
    def close(self):
        for copy in self.open:
            copy.wait_send()


def first_body(gains_in, gate_in, up_in, mine, theirs, down_in, gains, gate, up, z4, down, chip, sems):
    me = lax.axis_index("tok")
    core, z = me % 2, me // 8
    meet(me, (1, 2, 4, 8, 9, 16))
    mail = Mail(me, sems)
    size = mine.shape[0]
    swap = mail.send(theirs, chip.at[pl.ds(core * size, size)], 1)
    own = mail.local(mine, chip.at[pl.ds(core * size, size)])
    gains[pl.ds(me, 1)] = gains_in[...]

    def member(d):
        return ((d // 8) % 2) * 2 + d % 2

    place = (me // 2) % 4
    cut = down_in.shape[1] // 2
    a, b = pl.ds(0, cut), pl.ds(cut, cut)
    xa = mail.send(down_in.at[:, a], down.at[place, :, a], 2)
    yb = mail.send(down_in.at[:, b], down.at[place, :, b], 4)
    to_gate = [mail.send(gate_in.at[member(across(me, k))], gate.at[member(me)], k) for k in (9, 8, 1)]
    own.wait()
    swap.wait_recv()
    high = mail.send(chip, z4.at[z], 16)
    low = mail.send(chip, z4.at[z], 8)
    to_up = [mail.send(up_in.at[member(across(me, k))], up.at[member(me)], k) for k in (9, 8, 1)]
    ya = mail.send(down_in.at[:, a], down.at[place, :, a], 4)
    xb = mail.send(down_in.at[:, b], down.at[place, :, b], 2)
    kept = [
        mail.local(down_in, down.at[place]),
        mail.local(chip, z4.at[z]),
        mail.local(gate_in.at[member(me)], gate.at[member(me)]),
        mail.local(up_in.at[member(me)], up.at[member(me)]),
    ]
    for bit in (1, 2, 4):
        at = pl.ds((me // bit) * bit, bit)
        mail.send(gains.at[at], gains.at[at], bit).wait_recv()
    high.wait_recv()
    zh = across(me, 16) // 8
    low2 = mail.send(z4.at[zh], z4.at[zh], 8)
    across_x, across_y = across(place, 1), across(place, 2)
    xa.wait_recv()
    ya2 = mail.send(down.at[across_x, :, a], down.at[across_x, :, a], 4)
    yb.wait_recv()
    xb2 = mail.send(down.at[across_y, :, b], down.at[across_y, :, b], 2)
    for bit in (8, 16):
        at = pl.ds((me // bit) * bit, bit)
        mail.send(gains.at[at], gains.at[at], bit).wait_recv()
    for c in to_gate + to_up + [low, low2, ya, xb, ya2, xb2]:
        c.wait_recv()
    for c in kept:
        c.wait()
    mail.close()


def spread_first(gains, gate, up, mine, theirs, down):
    rows, cols = mine.shape
    return pl.pallas_call(
        first_body,
        out_shape=[
            jax.ShapeDtypeStruct((32,) + gains.shape[1:], f32),
            jax.ShapeDtypeStruct(gate.shape, bf16),
            jax.ShapeDtypeStruct(up.shape, bf16),
            jax.ShapeDtypeStruct((4, 2 * rows, cols), bf16),
            jax.ShapeDtypeStruct((4,) + down.shape, bf16),
        ],
        in_specs=[INV] * 6,
        out_specs=[INV] * 5,
        scratch_shapes=[pltpu.VMEM((2 * rows, cols), bf16), pltpu.SemaphoreType.DMA((2, 28))],
        compiler_params=pltpu.CompilerParams(collective_id=1, has_side_effects=True, vmem_limit_bytes=20 * MIB),
    )(gains, gate, up, mine, theirs, down)


def second_body(z4, out_mine, out_theirs, gate, whole, out4, gate2, chip, sems):
    me = lax.axis_index("tok")
    core, z, place = me % 2, me // 8, (me // 2) % 4
    across_y, across_x = across(place, 2), across(place, 1)
    meet(me, (1, 2, 4, 8, 16))
    mail = Mail(me, sems)
    size, cut = out_mine.shape[0], z4.shape[2] // 2
    a, b = pl.ds(0, cut), pl.ds(cut, cut)
    ya = mail.send(z4.at[:, :, a], whole.at[:, place, :, a], 4)
    xb = mail.send(z4.at[:, :, b], whole.at[:, place, :, b], 2)
    swap = mail.send(out_theirs, chip.at[pl.ds(core * size, size)], 1)
    own = mail.local(out_mine, chip.at[pl.ds(core * size, size)])
    kept = [mail.local(z4, whole.at[:, place]), mail.local(gate, gate2.at[z // 2])]
    xa = mail.send(z4.at[:, :, a], whole.at[:, place, :, a], 2)
    yb = mail.send(z4.at[:, :, b], whole.at[:, place, :, b], 4)
    own.wait()
    swap.wait_recv()
    high = mail.send(chip, out4.at[z], 16)
    low = mail.send(chip, out4.at[z], 8)
    kept.append(mail.local(chip, out4.at[z]))
    gate_high = mail.send(gate, gate2.at[z // 2], 16)
    ya.wait_recv()
    xa2 = mail.send(whole.at[:, across_y, :, a], whole.at[:, across_y, :, a], 2)
    xb.wait_recv()
    yb2 = mail.send(whole.at[:, across_x, :, b], whole.at[:, across_x, :, b], 4)
    high.wait_recv()
    zh = across(me, 16) // 8
    low2 = mail.send(out4.at[zh], out4.at[zh], 8)
    for c in (xa, yb, xa2, yb2, low, low2, gate_high):
        c.wait_recv()
    for c in kept:
        c.wait()
    mail.close()


def spread_second(z4, out_mine, out_theirs, gate):
    rows, cols = out_mine.shape
    return pl.pallas_call(
        second_body,
        out_shape=[
            jax.ShapeDtypeStruct((4, 4) + z4.shape[1:], bf16),
            jax.ShapeDtypeStruct((4, 2 * rows, cols), bf16),
            jax.ShapeDtypeStruct((2,) + gate.shape, bf16),
        ],
        in_specs=[INV] * 4,
        out_specs=[INV] * 3,
        scratch_shapes=[pltpu.VMEM((2 * rows, cols), bf16), pltpu.SemaphoreType.DMA((2, 16))],
        compiler_params=pltpu.CompilerParams(collective_id=2, has_side_effects=True, vmem_limit_bytes=20 * MIB),
    )(z4, out_mine, out_theirs, gate)


def scan_body(sign, s_ref, o_ref, stage, here, whole, zhere, back, bhere, sems):
    me = lax.axis_index("tok")
    z, plane = me // 8, (me // 2) % 4
    barrier = pltpu.get_barrier_semaphore()
    for k in (1, 2, 3):
        for to in (across(me, 2 * k), lax.rem(me + 8 * k, 32)):
            pl.semaphore_signal(barrier, inc=1, device_id=(to,), device_id_type=MESH)
    pl.semaphore_wait(barrier, 6)

    def slot(k):
        return (across(me, 2 * k) // 2) % 4

    def copy(source, target, sem, i, to):
        return pltpu.make_async_remote_copy(
            src_ref=source,
            dst_ref=target,
            send_sem=sems.at[sem, 0, i],
            recv_sem=sems.at[sem, 1, i],
            device_id=(to,),
            device_id_type=MESH,
        )

    def receives(k):
        return z - k >= 0 if sign > 0 else z + k < 4

    def sends(k):
        return z + k < 4 if sign > 0 else z - k >= 0

    copies = []
    for k in (3, 1, 2):
        stage[k - 1] = s_ref[pl.ds(2 * slot(k), 2)].astype(stage.dtype)
        copies.append(copy(stage.at[k - 1], here.at[k - 1], 0, k - 1, across(me, 2 * k)))
        copies[-1].start()
    mine = [s_ref[pl.ds(2 * plane, 2)]]
    for c in copies:
        c.wait()
    mine += [here[k - 1].astype(f32) for k in (1, 2, 3)]
    whole[...] = sum(mine).astype(whole.dtype)
    for k in (2, 1, 3):

        @pl.when(sends(k))
        def _(k=k):
            copy(whole, zhere.at[k - 1], 1, k - 1, me + 8 * k * sign).start()

    for k in (1, 2, 3):

        @pl.when(receives(k))
        def _(k=k):
            copy(whole, zhere.at[k - 1], 1, k - 1, me).wait_recv()

        @pl.when(jnp.logical_not(receives(k)))
        def _(k=k):
            zhere[k - 1] = jnp.zeros_like(whole)

    for k in (1, 2, 3):

        @pl.when(sends(k))
        def _(k=k):
            copy(whole, zhere.at[k - 1], 1, k - 1, me).wait_send()

    beyond = sum(zhere[k].astype(f32) for k in range(3))
    copies = []
    for k in (3, 1, 2, 0):
        before = beyond
        for j in range(4):
            if j != k:
                before = before + (sign * (slot(k) - slot(j)) > 0).astype(f32) * mine[j]
        if k == 0:
            o_ref[pl.ds(2 * plane, 2)] = before
        else:
            back[k - 1] = before.astype(back.dtype)
            copies.append(copy(back.at[k - 1], bhere.at[k - 1], 2, k - 1, across(me, 2 * k)))
            copies[-1].start()
    for c in copies:
        c.wait()
    for k in (1, 2, 3):
        o_ref[pl.ds(2 * slot(k), 2)] = bhere[k - 1].astype(f32)


def spans_of(cols, most=512):
    return [(s, min(most, cols - s)) for s in range(0, cols, most)]


def ffn_body(order, sides, x_ref, g_ref, *refs):
    gates, ups, downs = refs[0:4], refs[4:8], refs[8:11]
    y_ref, act_ref, d_ref, dh_ref, y_there, dh_there, w_gate_up, w_down, sem = refs[11:]
    cols = w_down.shape[0]

    @pl.when(pl.program_id(0) == 0)
    def _():
        size, part, rest = downs[0].shape[0], downs[1].shape[1], downs[2].shape[1]
        far = pl.ds(pl.multiple_of((1 - sides[4]) * size, 16), size)
        targets = [
            w_down.at[pl.ds(pl.multiple_of(sides[4] * size, 16), size)],
            w_down.at[far, pl.ds(0, part)],
            w_down.at[far, pl.ds(part, rest)],
        ]
        copies = [pltpu.make_async_copy(a, b, sem.at[i]) for i, (a, b) in enumerate(zip(downs, targets))]
        size = gates[0].shape[1]
        for j, pieces in enumerate((gates, ups)):
            for k, piece in enumerate(pieces):
                for i, at in enumerate(order):
                    rows = pl.ds(pl.multiple_of((at + sides[k]) * size, 16), size)
                    target = w_gate_up.at[rows, pl.ds(j * cols, cols)]
                    copies.append(pltpu.make_async_copy(piece.at[i], target, sem.at[len(copies)]))
        for copy in copies:
            copy.start()
        for copy in copies:
            copy.wait()

    x, g = x_ref[...], g_ref[...]
    for s, w in spans_of(cols):
        gate, upper = dot(x, w_gate_up[:, s : s + w]), dot(x, w_gate_up[:, cols + s : cols + s + w])
        d_act = dot_cols(g, w_down[s : s + w, :])
        sigma = jax.nn.sigmoid(gate)
        smooth = gate * sigma
        act_ref[:, s : s + w] = (smooth * upper).astype(bf16)
        d_ref[:, s : s + w] = (d_act * upper * sigma * (1.0 + gate * (1.0 - sigma))).astype(bf16)
        d_ref[:, cols + s : cols + s + w] = (d_act * smooth).astype(bf16)
    mine = pl.program_id(0) // (pl.num_programs(0) // 2) == sides[5]
    y = dot(act_ref[...], w_down[...]).astype(bf16)
    dh = dot_cols(d_ref[...], w_gate_up[...]).astype(bf16)

    @pl.when(mine)
    def _():
        y_ref[...] = y
        dh_ref[...] = dh

    @pl.when(jnp.logical_not(mine))
    def _():
        y_there[...] = y
        dh_there[...] = dh


def ffn(x, g, gate, up, down, order, sides, tile=256):
    tokens, width = x.shape
    cols = 2 * down[0].shape[0]

    steps = tokens // tile // 2

    def block(w):
        return pl.BlockSpec((tile, w), lambda i, s: (i, 0))

    def half(of_mine):
        def at(i, s):
            return jnp.clip(i - steps * (s[5] if of_mine else 1 - s[5]), 0, steps - 1), 0

        return pl.BlockSpec((tile, width), at)

    shapes = [(tokens // 2, width), (tokens, cols), (tokens, 2 * cols)] + [(tokens // 2, width)] * 3
    return pl.pallas_call(
        lambda *refs: ffn_body(order, *refs),
        out_shape=[jax.ShapeDtypeStruct(shape, bf16) for shape in shapes],
        grid_spec=pltpu.PrefetchScalarGridSpec(
            num_scalar_prefetch=1,
            grid=(tokens // tile,),
            in_specs=[block(width), block(width)] + [pl.BlockSpec(memory_space=pl.ANY)] * 11,
            out_specs=[half(True), block(cols), block(2 * cols), half(True), half(False), half(False)],
            scratch_shapes=[
                pltpu.VMEM((width, 2 * cols), bf16),
                pltpu.VMEM((cols, width), bf16),
                pltpu.SemaphoreType.DMA((8 * len(order) + 3,)),
            ],
        ),
        compiler_params=pltpu.CompilerParams(vmem_limit_bytes=52 * MIB),
        cost_estimate=pl.CostEstimate(flops=0, bytes_accessed=0, transcendentals=0),
    )(sides, x, g, *gate, *up, *down)


def product_body(count, group, index, *refs):
    left, right, out = refs[: count * group], refs[count * group : count * (group + 1)], refs[-1]
    acc = 0.0
    for i in range(count):
        rows = jnp.concatenate([a[...] for a in left[i * group : (i + 1) * group]], axis=1)
        acc = acc + dot_rows(rows, right[i][...])
    out[...] = acc.astype(out.dtype)


def row_blocks(left, right, index, size, half=None, deps=()):
    count = index.shape[0]
    group = 4 if count % 4 == 0 else 1
    cols = right[0].shape[1] // (1 if half is None else 2)
    at_col = half or 0

    def block(tokens, j):
        return pl.BlockSpec((tokens, size), lambda i, at: (0, at[i * group + j]))

    return pl.pallas_call(
        lambda *refs: product_body(len(left), group, *refs),
        out_shape=jax.ShapeDtypeStruct((count * size, cols), bf16),
        grid_spec=pltpu.PrefetchScalarGridSpec(
            num_scalar_prefetch=1,
            grid=(count // group,),
            in_specs=[block(a.shape[0], j) for a in left for j in range(group)]
            + [pl.BlockSpec((b.shape[0], cols), lambda i, at: (0, at_col)) for b in right]
            + [pl.BlockSpec(memory_space=pl.ANY)] * len(deps),
            out_specs=pl.BlockSpec((group * size, cols), lambda i, at: (i, 0)),
        ),
        compiler_params=pltpu.CompilerParams(vmem_limit_bytes=56 * MIB),
        cost_estimate=pl.CostEstimate(flops=0, bytes_accessed=0, transcendentals=0),
    )(index.astype(jnp.int32), *[a for a in left for _ in range(group)], *right, *deps)


def apart_body(places, padded, w_ref, out_ref):
    w = w_ref[...].astype(f32)
    unit = w.shape[1] // sum(len(p) for p in places)
    gap = [jnp.zeros((w.shape[0], padded - unit), f32)] if padded > unit else []
    for q, place in enumerate(places):
        blocks = []
        for d in place:
            blocks += [w[:, d * unit : (d + 1) * unit]] + gap
        out_ref[q] = jnp.concatenate(blocks, axis=1).astype(bf16)


def apart(w, places, padded):
    rows, cols = w.shape[0], len(places[0]) * padded
    return pl.pallas_call(
        lambda *refs: apart_body(places, padded, *refs),
        out_shape=jax.ShapeDtypeStruct((len(places), rows, cols), bf16),
        in_specs=[INV],
        out_specs=INV,
        compiler_params=pltpu.CompilerParams(vmem_limit_bytes=24 * MIB),
        cost_estimate=pl.CostEstimate(flops=0, bytes_accessed=0, transcendentals=0),
    )(w)


def together_body(places, padded, unit, member, *refs):
    pieces, outs, held = refs[:4], refs[4:6], refs[6]
    for k, piece in enumerate(pieces):
        held[k] = piece[...].astype(f32)
    cols = len(places[0]) * padded
    for j, out in enumerate(outs):
        blocks = {}
        for q, place in enumerate(places):
            for i, d in enumerate(place):
                at = j * cols + i * padded
                blocks[d] = held[member[0] ^ q][:, at : at + unit]
        out[...] = jnp.concatenate([blocks[d] for d in sorted(blocks)], axis=1)


def together(pieces, places, padded, unit, member):
    rows = pieces[0].shape[0]
    whole = jax.ShapeDtypeStruct((rows, unit * sum(len(p) for p in places)), f32)
    return pl.pallas_call(
        lambda *refs: together_body(places, padded, unit, *refs),
        out_shape=[whole, whole],
        in_specs=[pl.BlockSpec(memory_space=pltpu.SMEM)] + [INV] * 4,
        out_specs=[INV, INV],
        scratch_shapes=[pltpu.VMEM((4,) + pieces[0].shape, f32)],
        compiler_params=pltpu.CompilerParams(vmem_limit_bytes=40 * MIB),
        cost_estimate=pl.CostEstimate(flops=0, bytes_accessed=0, transcendentals=0),
    )(jnp.reshape(member, (1,)).astype(jnp.int32), *pieces)


def wide_body(d_ref, w_ref, out_ref):
    out_ref[...] = dot_cols(d_ref[...], w_ref[...]).astype(bf16)


def times_transposed(d, w, tile=256):
    return pl.pallas_call(
        wide_body,
        out_shape=jax.ShapeDtypeStruct((d.shape[0], w.shape[0]), bf16),
        grid=(d.shape[0] // tile,),
        in_specs=[
            pl.BlockSpec((tile, d.shape[1]), lambda i: (i, 0)),
            pl.BlockSpec(w.shape, lambda i: (0, 0)),
        ],
        out_specs=pl.BlockSpec((tile, w.shape[0]), lambda i: (i, 0)),
        compiler_params=pltpu.CompilerParams(vmem_limit_bytes=48 * MIB),
        cost_estimate=pl.CostEstimate(flops=0, bytes_accessed=0, transcendentals=0),
    )(d, w)


def part_maker(left, right, bits, within=(0,), half=None):
    n = lax.axis_size("tok")
    size = left[0].shape[1] * 2 // n
    cols = right[0].shape[1] // (1 if half is None else 2)
    ids = np.asarray([(at + more) // 2 for at in grown(bits[:-1][::-1]) for more in within], np.int32)

    def make(index, *deps):
        index = jnp.asarray(ids) + index * (bits[-1] // 2)
        if size % 128 == 0:
            out = row_blocks(left, right, index, size, half, deps)
        else:
            out = sum(dot_rows(a, b) for a, b in zip(left, right)).astype(bf16).reshape(n // 2, size, -1)
            out = out[index][..., (half or 0) * cols : (half or 0) * cols + cols]
        return out.reshape(-1, size * len(within), cols)

    return make


def feature_tables(heads):
    pairs = [(a, b) for a in range(QK + 1) for b in range(a, QK + 1)]
    one = np.zeros((heads, heads * QK, FEATS), np.float32)
    two = np.zeros((heads, heads * QK, FEATS), np.float32)
    rows = np.zeros((8, FEATS), np.float32)
    for f, (a, b) in enumerate(pairs):
        for h in range(heads):
            if a < QK:
                one[h, h * QK + a, f] = 1
            if b < QK:
                two[h, h * QK + b, f] = 1
        rows[0, f] = a == QK
        rows[1, f] = b == QK
        if a == QK:
            rows[2, f] = 1.0
        elif b == QK:
            rows[2, f] = QK**-0.5
        else:
            rows[2, f] = (0.5 if a == b else 1.0) / QK
    return jnp.asarray(one, bf16), jnp.asarray(two, bf16), jnp.asarray(rows)


def dot(a, b):
    return lax.dot_general(a, b, (((1,), (0,)), ((), ())), preferred_element_type=f32)


def dot_rows(a, b):
    return lax.dot_general(a, b, (((0,), (0,)), ((), ())), preferred_element_type=f32)


def dot_cols(a, b):
    return lax.dot_general(a, b, (((1,), (1,)), ((), ())), preferred_element_type=f32)


def halves(x):
    high = x.astype(bf16)
    return high, (x - high.astype(f32)).astype(bf16)


def features(x, one, two, rows):
    return dot(x, one) + rows[0:1], dot(x, two) + rows[1:2]


def total_row(state):
    return jnp.concatenate([state[FEATS : FEATS + 1], state[FEATS + 1 : FEATS + 2, : FEATS - 128]], axis=1)


def store_state(ref, state, row):
    ref[0, 0, :FEATS, :] = state
    ref[0, 0, FEATS:, :] = jnp.zeros((ROWS - FEATS, state.shape[1]), f32)
    ref[0, 0, FEATS : FEATS + 1, :] = row[:, :128]
    ref[0, 0, FEATS + 1 : FEATS + 2, : FEATS - 128] = row[:, 128:]


def kept_rows(scal, tile, tokens):
    index = lax.broadcasted_iota(jnp.int32, (tokens, 1), 0) + tile * tokens
    return index >= scal[tile]


def state_body(scal, k_ref, v_ref, one, two, rows, out_ref):
    tile = pl.program_id(0)
    a, b = features(k_ref[...], one[0], two[0], rows)
    phi = jnp.where(kept_rows(scal, tile, a.shape[0]), a * b, 0.0)
    high, low = halves(phi)
    v = v_ref[...]
    store_state(out_ref, dot_rows(high, v) + dot_rows(low, v), jnp.sum(phi, axis=0, keepdims=True))


def weights(q_ref, k_ref, lo_ref, tile, head):
    tokens, lanes = q_ref.shape
    lane = lax.broadcasted_iota(jnp.int32, (tokens, lanes), 1) // QK == head
    q = jnp.where(lane, q_ref[...], jnp.zeros((), bf16))
    score = dot_cols(q, k_ref[...]) * QK**-0.5
    row = lax.broadcasted_iota(jnp.int32, score.shape, 0)
    col = lax.broadcasted_iota(jnp.int32, score.shape, 1)
    lo = lo_ref[...] - tile * tokens
    mask = (col <= row) & (col >= lo)
    weight = jnp.where(mask, 1.0 + score + 0.5 * score * score, 0.0)
    return lane, score, mask, weight, lo < 0


def forward_body(q_ref, k_ref, v_ref, lo_ref, carry_ref, one, two, rows, y_ref, mixed_ref):
    tile, head = pl.program_id(0), pl.program_id(1)
    _, _, _, weight, alive = weights(q_ref, k_ref, lo_ref, tile, head)
    a, b = features(q_ref[...], one[0], two[0], rows)
    phi = jnp.where(alive, a * b * rows[2:3], 0.0)
    high, low = halves(phi)
    carry = carry_ref[0, 0]
    s_high, s_low = halves(carry[:FEATS])
    numer = dot(weight.astype(bf16), v_ref[...])
    numer = numer + (dot(high, s_high) + dot(high, s_low) + dot(low, s_high))
    denom = jnp.sum(weight, axis=1, keepdims=True) + jnp.sum(phi * total_row(carry), axis=1, keepdims=True)
    y = numer / denom
    y_ref[...] = y
    mixed_ref[...] = y.astype(bf16)


def spread(t, a, b, one, two):
    first_high, first_low = halves(t * b)
    second_high, second_low = halves(t * a)
    return (
        dot_cols(first_high, one) + dot_cols(first_low, one) + dot_cols(second_high, two) + dot_cols(second_low, two)
    )


def backward_body(
    q_ref, k_ref, v_ref, lo_ref, carry_ref, one, two, rows, y_ref, d_ref, dq_ref, dk_ref, dv_ref, ds_ref, dq_acc, dk_acc
):
    tile, head = pl.program_id(0), pl.program_id(1)
    lane, score, mask, weight, alive = weights(q_ref, k_ref, lo_ref, tile, head)
    a, b = features(q_ref[...], one[0], two[0], rows)
    phi = jnp.where(alive, a * b * rows[2:3], 0.0)
    high, low = halves(phi)
    carry = carry_ref[0, 0]
    s_high, s_low = halves(carry[:FEATS])
    row = total_row(carry)
    denom = jnp.sum(weight, axis=1, keepdims=True) + jnp.sum(phi * row, axis=1, keepdims=True)
    d = d_ref[...].astype(f32)
    g = d / denom
    c = -jnp.sum(d * y_ref[...], axis=1, keepdims=True) / denom
    g_high, g_low = halves(g)
    v = v_ref[...]
    dk = dot_cols(g_high, v) + dot_cols(g_low, v) + c
    ds = jnp.where(mask, dk * (1.0 + score) * QK**-0.5, 0.0).astype(bf16)
    dv_ref[...] = dot_rows(weight.astype(bf16), g_high)
    dphi = dot_cols(g_high, s_high) + dot_cols(g_high, s_low) + dot_cols(g_low, s_high) + c * row
    t = jnp.where(alive, dphi * rows[2:3], 0.0)
    dq = jnp.where(lane, dot(ds, k_ref[...]), 0.0) + spread(t, a, b, one[0], two[0])
    dkeys = jnp.where(lane, dot_rows(ds, q_ref[...]), 0.0)

    @pl.when(head == 0)
    def _():
        dq_acc[...] = dq
        dk_acc[...] = dkeys

    @pl.when(head > 0)
    def _():
        dq_acc[...] += dq
        dk_acc[...] += dkeys

    @pl.when(head == pl.num_programs(1) - 1)
    def _():
        dq_ref[...] = dq_acc[...].astype(bf16)
        dk_ref[...] = dk_acc[...]

    state = dot_rows(high, g_high) + dot_rows(high, g_low) + dot_rows(low, g_high)
    store_state(ds_ref, state, jnp.sum(phi * c, axis=0, keepdims=True))


def carried_body(scal, k_ref, v_ref, one, two, rows, grad_ref, dk_in, dv_in, dk_ref, dv_ref, acc):
    tile, head = pl.program_id(0), pl.program_id(1)
    a, b = features(k_ref[...], one[0], two[0], rows)
    keep = kept_rows(scal, tile, a.shape[0])
    high, low = halves(jnp.where(keep, a * b, 0.0))
    grad = grad_ref[0, 0]
    g_high, g_low = halves(grad[:FEATS])
    v = v_ref[...]
    dv = dv_in[...] + dot(high, g_high) + dot(high, g_low) + dot(low, g_high)
    dv_ref[...] = dv.astype(bf16)
    t = jnp.where(keep, dot_cols(v, g_high) + dot_cols(v, g_low) + total_row(grad), 0.0)
    dk = spread(t, a, b, one[0], two[0])

    @pl.when(head == 0)
    def _():
        acc[...] = dk_in[...] + dk

    @pl.when(head > 0)
    def _():
        acc[...] += dk

    @pl.when(head == pl.num_programs(1) - 1)
    def _():
        dk_ref[...] = acc[...].astype(bf16)


class Attention:
    def __init__(self, qkv, lo, heads, tokens):
        self.qkv, self.heads, self.tokens = qkv, heads, tokens
        self.lo = lo[:, None]
        self.scal = jnp.stack([lo[tokens - 1], lo[2 * tokens - 1]])
        self.tables = feature_tables(heads)
        lanes = heads * QK
        self.value = (qkv.shape[1] - 2 * lanes) // heads
        skip = 2 * lanes // self.value
        self.q = pl.BlockSpec((tokens, lanes), lambda t, h: (t, 0))
        self.k = pl.BlockSpec((tokens, lanes), lambda t, h: (t, 1))
        self.v = pl.BlockSpec((tokens, self.value), lambda t, h: (t, h + skip))
        self.o = pl.BlockSpec((tokens, self.value), lambda t, h: (t, h))
        self.l = pl.BlockSpec((tokens, 1), lambda t, h: (t, 0))
        self.s = pl.BlockSpec((1, 1, ROWS, self.value), lambda t, h: (h, t, 0, 0))
        self.e = pl.BlockSpec((1, lanes, FEATS), lambda t, h: (h, 0, 0))
        self.r = pl.BlockSpec((8, FEATS), lambda t, h: (0, 0))
        self.m = pl.BlockSpec(memory_space=pltpu.SMEM)
        self.table_specs = [self.e, self.e, self.r]
        self.acc = pltpu.VMEM((tokens, lanes), f32)
        self.state_shape = jax.ShapeDtypeStruct((heads, 2, ROWS, self.value), f32)

    def wide(self, kind):
        return jax.ShapeDtypeStruct((2 * self.tokens, self.heads * self.value), kind)

    def narrow(self, kind):
        return jax.ShapeDtypeStruct((2 * self.tokens, self.heads * QK), kind)

    def call(self, body, ins, outs, shapes, scratch, limit, args):
        return pl.pallas_call(
            body,
            grid=(2, self.heads),
            in_specs=ins,
            out_specs=outs,
            out_shape=shapes,
            scratch_shapes=scratch,
            compiler_params=pltpu.CompilerParams(vmem_limit_bytes=limit * MIB),
            cost_estimate=pl.CostEstimate(flops=0, bytes_accessed=0, transcendentals=0),
        )(*args)

    def states(self):
        (out,) = self.call(
            state_body,
            [self.m, self.k, self.v] + self.table_specs,
            [self.s],
            [self.state_shape],
            [],
            24,
            (self.scal, self.qkv, self.qkv, *self.tables),
        )
        return out

    def forward(self, carry):
        return self.call(
            forward_body,
            [self.q, self.k, self.v, self.l, self.s] + self.table_specs,
            [self.o, self.o],
            [self.wide(f32), self.wide(bf16)],
            [],
            48,
            (self.qkv, self.qkv, self.qkv, self.lo, carry, *self.tables),
        )

    def backward(self, carry, y, d_heads):
        return self.call(
            backward_body,
            [self.q, self.k, self.v, self.l, self.s] + self.table_specs + [self.o, self.o],
            [self.q, self.q, self.o, self.s],
            [self.narrow(bf16), self.narrow(f32), self.wide(f32), self.state_shape],
            [self.acc, self.acc],
            48,
            (self.qkv, self.qkv, self.qkv, self.lo, carry, *self.tables, y, d_heads),
        )

    def carried(self, grad, dk, dv):
        return self.call(
            carried_body,
            [self.m, self.k, self.v] + self.table_specs + [self.s, self.q, self.o],
            [self.q, self.o],
            [self.narrow(bf16), self.wide(bf16)],
            [self.acc],
            48,
            (self.scal, self.qkv, self.qkv, *self.tables, grad, dk, dv),
        )


def others(state, earlier, kind):
    n = lax.axis_size("tok")
    me = lax.axis_index("tok")
    sign = 1 if earlier else -1
    if n != 32:
        parts = lax.all_gather(state.astype(kind), "tok").astype(f32)
        index = jnp.arange(n)
        before = (sign * (me // 2 - index // 2) > 0) & (index % 2 == me % 2)
        out = jnp.sum(jnp.where(before.reshape((n,) + (1,) * state.ndim), parts, 0.0), axis=0)
        return out
    block = (state.shape[0] // 4,) + state.shape[1:]
    slots = pltpu.VMEM((3,) + block, kind)
    return pl.pallas_call(
        lambda *refs: scan_body(sign, *refs),
        out_shape=jax.ShapeDtypeStruct(state.shape, f32),
        in_specs=[INV],
        out_specs=INV,
        scratch_shapes=[slots, slots, pltpu.VMEM(block, kind), slots, slots, slots, pltpu.SemaphoreType.DMA((3, 2, 3))],
        compiler_params=pltpu.CompilerParams(
            collective_id=3 if earlier else 4, has_side_effects=True, vmem_limit_bytes=16 * MIB
        ),
        cost_estimate=pl.CostEstimate(flops=0, bytes_accessed=0, transcendentals=0),
    )(state)


def row_starts(positions, lengths, offsets):
    inside = (positions[:, None] >= offsets[None, :]) & (positions[:, None] < offsets[None, :] + lengths[None, :])
    return jnp.sum(jnp.where(inside, offsets[None, :], 0), axis=1)


def side_by_side(core, mine, theirs, axis=0):
    size = mine.shape[axis]
    shape = list(mine.shape)
    shape[axis] *= 2
    out = jnp.zeros(shape, mine.dtype)
    out = lax.dynamic_update_slice_in_dim(out, mine, core * size, axis)
    return lax.dynamic_update_slice_in_dim(out, theirs, (1 - core) * size, axis)


def shards(
    block_input,
    lengths,
    offsets,
    norm1_gain,
    w_query,
    w_key,
    w_value,
    w_out,
    norm2_gain,
    w_gate,
    w_up,
    w_down,
    out_grad,
):
    n = lax.axis_size("tok")
    me = lax.axis_index("tok")
    core, member = me % 2, side(PAIR) * 2 + me % 2
    cbits = bits_from(n, 2)
    qbits = [bit for bit in cbits if bit != PAIR]
    swapped = qbits[:-2] + [qbits[-1], qbits[-2]]
    chips, quads = n // 2, n // 4
    above, below = n // (2 * PAIR), PAIR // 2
    groups = [
        [i * 2 * PAIR + p * PAIR + j * 2 + c for i in range(above) for j in range(below)] for p in (0, 1) for c in (0, 1)
    ]
    to_member = {1: 1, 2: PAIR, 3: PAIR + 1}
    tokens, width = block_input.shape
    rows = w_query.shape[0]
    heads = w_query.shape[1] // QK // 2
    half = width // 2
    lanes = heads * QK
    def column_half(w, which):
        return lax.dynamic_slice_in_dim(w, which * (w.shape[1] // 2), w.shape[1] // 2, 1)

    def row_half(w, which):
        return lax.dynamic_slice_in_dim(w, which * (w.shape[0] // 2), w.shape[0] // 2, 0)

    unit = w_down.shape[0]
    padded = -(-unit // 16) * 16
    cols = quads * padded

    gate, up = apart(w_gate, groups, padded), apart(w_up, groups, padded)
    down = jnp.pad(w_down, ((0, padded - unit), (0, 0)))
    near_grad = side_by_side(core, out_grad, flip(out_grad, 1))

    def by_core(which):
        return jnp.concatenate([column_half(w, which) for w in (w_query, w_key, w_value)], axis=1)

    gains = jnp.stack([norm1_gain, norm2_gain]).astype(f32)
    if n == 32:
        gains = jnp.pad(gains, ((0, 6), (0, 128 - rows)))[None]
        gains = after(gains, near_grad)
        gains, gate, up, qkv_all, down = spread_first(gains, gate, up, by_core(core), by_core(1 - core), down)
        gains = gains[:, :2, :rows].transpose(1, 0, 2).reshape(2, 1, width)
        z4 = qkv_all
        qkv_all, out_half, gate = spread_second(z4, column_half(w_out, core), column_half(w_out, 1 - core), gate)
        qkv_all = qkv_all.reshape(width, -1)
    else:

        def to_group(x):
            pieces = [(member, pick(x, member))]
            for k in range(1, 4):
                pieces.append((member ^ k, flip(pick(x, member ^ k), to_member[k])))
            return assemble_all(pieces)

        gate, up = to_group(gate), to_group(up)
        qkv_all = side_by_side(core, by_core(core), flip(by_core(1 - core), 1))
        gains = grow(gains, 1)
        for bit in cbits:
            gains, qkv_all = grow(gains, bit), grow(qkv_all, bit)
        gains = in_order(gains, [1] + cbits).transpose(1, 0, 2).reshape(2, 1, width)
        qkv_all = in_order(qkv_all, cbits).reshape(width, -1)
        out_half = side_by_side(core, column_half(w_out, core), flip(column_half(w_out, 1 - core), 1))
        for bit in cbits[:-2]:
            out_half = grow(out_half, bit)
        out_half = in_order(out_half, cbits[:-2])
        gate = grow(gate, qbits[0])
        for bit in qbits[1:]:
            down = grow(down, bit)
        down = in_order(down, qbits[1:])
    gain_one, gain_two = gains[0], gains[1]

    inputs32 = block_input.astype(f32)
    ratio_one = lax.rsqrt(jnp.mean(inputs32 * inputs32, axis=1, keepdims=True) + eps)
    normed_one = inputs32 * ratio_one
    hidden_one = (normed_one * gain_one).astype(bf16)
    hidden_chip = side_by_side(core, hidden_one, move(hidden_one, 1, (), (qkv_all,)))
    qkv = dot(hidden_chip, qkv_all).astype(bf16)

    first = (me // 2) * 2 * tokens
    positions = first + jnp.arange(2 * tokens, dtype=jnp.int32)
    lo = row_starts(positions, lengths, offsets) - first
    attention = Attention(qkv, lo, heads, tokens)
    states = attention.states()
    fresh0 = (lo[tokens - 1] >= 0).astype(f32)
    fresh1 = (lo[2 * tokens - 1] >= tokens).astype(f32)

    start, stop = (qkv_all,), (states,)
    for bit in qbits[1:-2]:
        gate = grow(gate, bit)
    gate_x = move(gate, 2, start, stop)
    up = grow(up, qbits[0], start, stop)
    for bit in qbits[1:-2]:
        up = grow(up, bit)
    out_y = move(out_half, 4, start, stop)
    leaving = states[:, 1] + (1.0 - fresh1) * states[:, 0]
    leaving, gate_x, up, out_y = lax.optimization_barrier((leaving, gate_x, up, out_y))
    entering = others(leaving, True, f32)
    start, stop = (leaving,), (entering,)
    down = down.reshape(cols // 2, width)
    down_a, down_b = down[:, : width * 3 // 4], down[:, width * 3 // 4 :]
    out_both = jnp.stack([out_half, out_y])
    gate_up = jnp.concatenate([gate, up], axis=-1)
    flows = [(out_both, 2), (gate_up, 4), (up, 2), (down_a, qbits[0]), (out_grad, PAIR)]
    flows = [move(w, bit, start, stop) for w, bit in flows]
    entering, out_x, gate_up, up_x, down_a, far_grad = lax.optimization_barrier((entering, *flows))
    gate_y, up_y = gate_up[..., :cols], gate_up[..., cols:]
    carry = jnp.stack([entering, states[:, 0] + (1.0 - fresh0) * entering], axis=1)
    place = (me // 2) % 4
    out_pieces = [(place, out_half), (place ^ 1, out_x[0]), (place ^ 2, out_y), (place ^ 3, out_x[1])]
    out_half = jnp.zeros((chips // 4, 4, 2 * rows, half), bf16)
    for index, piece in out_pieces:
        out_half = lax.dynamic_update_index_in_dim(out_half, piece, index, 1)
    out_half = out_half.reshape(width, half)
    carry = after(carry, out_half)
    y_heads, mixed_heads = attention.forward(carry)
    start, stop = (carry,), (mixed_heads,)
    flows = [move(w, bit, start, stop) for w, bit in [(gate_x, 4), (up_y, 2), (down_b, qbits[0])]]
    out_there = move(out_half, 1, start, stop)
    mixed_heads, out_there, *flows = lax.optimization_barrier((mixed_heads, out_there, *flows))
    gate_xy, up_xy, down_b = flows
    down = [down, down_a, down_b]
    out_all = side_by_side(core, out_half, out_there, 1)
    mixed_chip = side_by_side(core, mixed_heads, flip(mixed_heads, 1), 1)
    middle = inputs32 + dot(row_half(mixed_chip, core), out_all)
    ratio_two = lax.rsqrt(jnp.mean(middle * middle, axis=1, keepdims=True) + eps)
    normed_two = middle * ratio_two
    hidden_two = (normed_two * gain_two).astype(bf16)

    far_hidden = flip(hidden_two, PAIR)
    near_hidden = side_by_side(core, hidden_two, flip(hidden_two, 1))
    gate = [w.reshape(-1, 2 * rows, cols) for w in (gate, gate_x, gate_y, gate_xy)]
    up = [w.reshape(-1, 2 * rows, cols) for w in (up, up_x, up_y, up_xy)]
    order = [(at + more) // 2 for at in grown(qbits[:-2]) for more in (0, PAIR)]
    sides = jnp.stack([place, place ^ 1, place ^ 2, place ^ 3, side(qbits[0]), core]).astype(jnp.int32)
    near = ffn(near_hidden, near_grad, gate, up, down, order, sides)
    far_hidden, far_there = after(far_hidden, *near), move(far_grad, 1, (near_hidden,), (near[0],))
    far_grad = side_by_side(core, far_grad, far_there)
    far_hidden = side_by_side(core, far_hidden, flip(far_hidden, 1))
    far = ffn(far_hidden, far_grad, gate, up, down, order, sides)
    start, stop = (near[0], far_hidden), (far[0],)
    near_parts = [move(near[i], 1, start, stop) for i in (5, 4)]
    far, near_parts = lax.optimization_barrier((far, near_parts))

    right = [near[2], far[2]]
    sum_gate = Scatter(part_maker([near_hidden, far_hidden], right, qbits, (0, PAIR), 0), qbits)
    sum_gate.send()
    start, stop = (far[0],), (sum_gate.sent,)
    far_parts = [move(far[i], 1, start, stop) for i in (5, 4)]
    sent, far_parts = lax.optimization_barrier((sum_gate.sent, far_parts))
    d_far = (far[3].astype(f32) + far_parts[0].astype(f32)).astype(bf16)
    y_far = (far[0].astype(f32) + far_parts[1].astype(f32)).astype(bf16)
    sum_up = Scatter(part_maker([near_hidden, far_hidden], right, swapped, (0, PAIR), 1), swapped)
    sum_up.send(sent, d_far, y_far)
    sum_gate.keep(sum_up.sent)
    sum_up.keep(sum_gate.kept)
    term = row_blocks([near[1], far[1]], [near_grad, far_grad], jnp.arange(cols // 128), 128, None, (sum_up.kept,))
    d_far = move(d_far, PAIR, (), (term,))
    d_far = sum_gate.hold(d_far, term)
    near_parts = after(near_parts, d_far)
    d_near = near[3].astype(f32) + near_parts[0].astype(f32)
    y_near = near[0].astype(f32) + near_parts[1].astype(f32)
    d_hidden_two = d_near + d_far.astype(f32)
    term_norm_two = jnp.sum(d_hidden_two * normed_two, axis=0)
    scaled_two = d_hidden_two * gain_two
    d_middle = out_grad.astype(f32) + ratio_two * (
        scaled_two - normed_two * jnp.mean(scaled_two * normed_two, axis=1, keepdims=True)
    )
    d_mixed = d_middle.astype(bf16)
    d_mixed_chip = side_by_side(core, d_mixed, flip(d_mixed, 1))
    d_heads = dot_cols(d_mixed_chip, row_half(out_all, core)).astype(bf16)

    d_heads = sum_up.hold(d_heads, d_mixed)
    d_heads = after(d_heads, sum_gate.step(), sum_up.step())
    dq, dk, dv, d_states = attention.backward(carry, y_heads, d_heads)
    flows = (sum_gate.here, sum_up.here, move(y_far, PAIR, (d_heads,)))
    flows = [after(flow, d_states) for flow in flows]
    d_states, sum_gate.here, sum_up.here, y_far = lax.optimization_barrier((d_states, *flows))
    sum_both = join([sum_gate, sum_up])
    sent = [sum_both.step()]

    def down_x(index, *_):
        return pick(term.reshape(quads // 2, 2, padded, width)[..., :half], index, 1)

    def down_y(index, *_):
        return pick(term.reshape(quads // 4, 2, 2, padded, width)[..., half:], index, 1).reshape(-1, padded, half)

    sum_down = [Scatter(down_x, qbits), Scatter(down_y, swapped)]
    for part in sum_down:
        part.send(d_states)
        part.keep()
    sent += [part.sent for part in sum_down]
    d_mixed_half = column_half(d_mixed_chip, core)
    out_sums = []
    for h, bits in ((0, cbits), (1, cbits[:-2] + [cbits[-1], cbits[-2]])):
        out_sums.append(Scatter(part_maker([after(mixed_chip, *sent)], [d_mixed_half], bits, (0,), h), bits))
        out_sums[-1].send()
    leaving = d_states[:, 0] + (1.0 - fresh0) * d_states[:, 1]
    leaving = others(after(leaving, *(part.sent for part in out_sums)), False, bf16)
    for part in out_sums:
        leaving = after(leaving, part.keep(leaving))
    for part in [sum_both] + sum_down + out_sums:
        leaving = part.hold(leaving, leaving)
    leaving = after(leaving, *(part.step() for part in sum_down + out_sums))
    d_states = jnp.stack([d_states[:, 1] + (1.0 - fresh1) * leaving, leaving], axis=1)
    dk, dv = attention.carried(d_states, dk, dv)
    for part in out_sums + sum_down:
        dk = part.hold(dk, dk)
    sum_down = join(sum_down)
    dk = after(dk, sum_down.step())
    d_qkv = jnp.concatenate([dq, dk, dv], axis=1)

    cut = d_qkv.shape[1] // 2
    sums = []
    for h, bits in ((0, cbits), (1, cbits[:-2] + [cbits[-1], cbits[-2]])):
        sums.append(Scatter(part_maker([hidden_chip], [d_qkv], bits, (0,), h), bits))
        sums[-1].send(*(p.sent for p in sums[:-1]))
    start = tuple(part.sent for part in sums)
    for part in sums:
        part.keep(*start)
        start = (part.kept,)
    rest_out = join([part.gated(start) for part in out_sums])
    start = start + (rest_out.step(),)
    d_hidden_one = times_transposed(after(d_qkv, *start), qkv_all)
    for part in [sum_down, rest_out] + sums:
        d_hidden_one = part.hold(d_hidden_one, d_hidden_one)
    sent = [part.step() for part in sums]
    d_hidden_one = after(d_hidden_one, *sent)
    theirs = flip(row_half(d_hidden_one, 1 - core), 1)
    gate_sum = after(sum_both.finish(), *sent).astype(bf16).reshape(4, rows, 2 * cols)
    parts = [flip(after(pick(gate_sum, member ^ k), theirs), to_member[k]) for k in range(1, 4)]
    d_hidden_one = row_half(d_hidden_one, core).astype(f32) + theirs.astype(f32)
    term_norm_one = jnp.sum(d_hidden_one * normed_one, axis=0)
    scaled_one = d_hidden_one * gain_one
    mean_one = jnp.mean(scaled_one * normed_one, axis=1, keepdims=True)
    norms = jnp.stack([term_norm_one, term_norm_two])
    for part in sums:
        norms = part.hold(norms, theirs)
    norms, parts = lax.optimization_barrier((norms, parts))
    rest = join(sums)
    sent = [rest.step()] + [rest_out.step() for _ in rest_out.bits[1:]]
    norms = after(norms, *sent)
    norms = norms + flip(norms, 1)
    norms = norms + flip(norms, cbits[-1])
    norms = norms + flip(norms, cbits[-2])
    norms = norms + flip(norms, cbits[-3])
    norms = rest_out.hold(rest.hold(norms, norms), norms)
    while len(rest.bits) > 1:
        sent = [rest.step()]
    norms = after(norms, *sent)
    grad_gate, grad_up = together([pick(gate_sum, member), *parts], groups, padded, unit, member)
    for bit in cbits[:-3]:
        norms = norms + flip(norms, bit)
    norms = pick(norms.reshape(2, n, rows), me, 1)
    input_grad = d_middle + ratio_one * (after(scaled_one, *sent) - normed_one * mean_one)
    output = (after(middle, *sent) + y_near + y_far.astype(f32)).astype(bf16)
    grad_down = sum_down.finish()[:unit]
    rest.kept = jnp.concatenate([rest.kept, rest_out.kept], axis=2)
    rest.here = jnp.concatenate([rest.here, rest_out.here], axis=2)
    total = rest.step()
    mine, theirs = row_half(total, core), flip(row_half(total, 1 - core), 1)
    spans = [(0, lanes), (lanes, 2 * lanes), (2 * lanes, 2 * lanes + half), (2 * cut, 2 * cut + half)]
    grad_query, grad_key, grad_value, grad_out = (
        side_by_side(core, mine[:, a:b], theirs[:, a:b], 1) for a, b in spans
    )

    return (
        output,
        input_grad,
        norms[0],
        grad_query,
        grad_key,
        grad_value,
        grad_out,
        norms[1],
        grad_gate,
        grad_up,
        grad_down,
    )


def solution(mesh):
    return jax.shard_map(
        shards,
        mesh=mesh,
        in_specs=(
            P("tok", None),
            P(),
            P(),
            P("tok"),
            P("tok", None),
            P("tok", None),
            P("tok", None),
            P("tok", None),
            P("tok"),
            P("tok", None),
            P("tok", None),
            P("tok", None),
            P("tok", None),
        ),
        out_specs=(
            P("tok", None),
            P("tok", None),
            P("tok"),
            P("tok", None),
            P("tok", None),
            P("tok", None),
            P("tok", None),
            P("tok"),
            P("tok", None),
            P("tok", None),
            P("tok", None),
        ),
        check_vma=False,
    )
```
